256 devices in a mesh: dp: 16 (over z_hi, x), tensor: 16 (over y, z_lo, core).
Axes of the slice: x: 4, y: 4, z: 8 (z_hi: 4, z_lo: 2; z = z_hi * 2 + z_lo), core: 2. Of those that a mesh axis runs over, the one named last changes fastest.
Arguments:
- inputs: bfloat16 [8192, 5120], P(('dp', 'tensor')), may hold values from -6 to 6
- upstream: bfloat16 [8192, 5120], P(('dp', 'tensor')), may hold values from -6 to 6
- w_query: bfloat16 [5120, 4096], P(None, 'tensor'), may hold values from -0.078125 to 0.078125
- w_key: bfloat16 [5120, 512], P(None, 'tensor'), may hold values from -0.078125 to 0.078125
- w_value: bfloat16 [5120, 512], P(None, 'tensor'), may hold values from -0.078125 to 0.078125
- w_output: bfloat16 [4096, 5120], P('tensor'), may hold values from -0.09375 to 0.09375
- norm_gain: float32 [5120], replicated, may hold values from 0.25 to 1.75
- query_gain: float32 [128], replicated, may hold values from 0.25 to 1.75
- key_gain: float32 [128], replicated, may hold values from 0.25 to 1.75
- lengths: int32 [16, 8], P('dp'), may hold values from 1 to 256, 512 in all within a row
- rewards: float32 [128], P('dp'), may hold values from -4 to 4
- groups: int32 [128], P('dp'), may hold values from 0 to 15
Outputs:
- input_grad: bfloat16 [8192, 5120], P(('dp', 'tensor'))
- query_grads: float32 [5120, 4096], P('dp', 'tensor')
- key_grads: float32 [5120, 512], P('dp', 'tensor')
- value_grads: float32 [5120, 512], P('dp', 'tensor')
- output_grads: float32 [5120, 4096], P('dp', 'tensor')
- norm_delta: float32 [5120], replicated
- query_delta: float32 [128], replicated
- key_delta: float32 [128], replicated
The draws below stay inside these ranges and needn't reach their ends.
Inputs may be any that keep to these rules, and one draw needn't show every extreme that they name: Row i lists the lengths of the 8 rollout segments packed in order into data shard i; each row sums to 512.
All inputs are finite; a program needn't handle non-finite values.
Results may differ from the reference program's by a relative error of at most 0.03.
Values may be sent and summed in bfloat16 or wider, within the bound.
No kernel may reach another device: no remote copies, remote signals or barrier semaphores. Data moves between devices by JAX's collectives and lax.ppermute only.
A program may use at most 128 MiB of HBM per device.

```python
import math
import jax
import jax.numpy as jnp
import numpy as np
from jax import lax

D = 5120
HEADS = 32
KVH = 4
HD = 128
TOK_DEV = 512
SEGS = 8
GROUPS = 16
MOSTLEN = 256
SHARDS = 16
SEGMENTS = 128
TOKENS = 8192
N_DP = 16
N_TENSOR = 16


def plant(array, own_key, least, high):
    shape = array.shape
    place = [jax.random.randint(jax.random.fold_in(own_key, axis), (), 0, shape[axis]) for axis in range(len(shape))]
    array = array.at[tuple(place)].set(least)
    longest = shape.index(max(shape))
    place[longest] = (place[longest] + 1) % shape[longest]
    return array.at[tuple(place)].set(high)


def shard_levels(stream_key, shape, split, smallest, top_value):
    factor_of = 1.0
    for axis_at, blocks in split:
        draws = jax.random.uniform(jax.random.fold_in(jax.random.fold_in(stream_key, 6), axis_at), (blocks,), jnp.float32, smallest / len(split), top_value / len(split))
        factor_of = factor_of * jnp.repeat(jnp.exp(draws), shape[axis_at] // blocks).reshape((-1,) + (1,) * (len(shape) - 1 - axis_at))
    return factor_of


def length_profile(amount, total, reach, lean):
    loads = [(1 << 20) // math.isqrt(standing ** lean) + 1 for standing in range(2, amount + 1)]
    surplus, given = total - reach - (amount - 1), [1] * (amount - 1)
    while surplus > 0:
        free = [i for i in range(amount - 1) if given[i] < reach]
        whole, left = sum([loads[i] for i in free]), surplus
        for i in free:
            more = min(reach - given[i], max(1, left * loads[i] // whole), surplus)
            given[i] = given[i] + more
            surplus = surplus - more
    return np.array([reach] + given)


def uneven(own_key, amount, total, bound, skew):
    if amount == 2:
        one = jax.random.randint(own_key, (), max(1, total - bound), min(bound, total - 1) + 1)
        return jnp.stack([one, total - one])
    tallies = jnp.asarray(length_profile(amount, total, bound, skew), jnp.int32)
    pairs = (amount - 1) // 2
    giver, sink = tallies[1:1 + 2 * pairs:2], tallies[2:2 + 2 * pairs:2]
    room = jnp.minimum(giver - 1, bound - sink)
    moved = jax.random.randint(jax.random.fold_in(own_key, 1), (pairs,), 0, 1 << 20) % (room + 1)
    tallies = tallies.at[1:1 + 2 * pairs:2].set(giver - moved).at[2:2 + 2 * pairs:2].set(sink + moved)
    return tallies[jax.random.permutation(jax.random.fold_in(own_key, 2), amount)]


def noise(own_key, shape, deviation, reach, pieces=(), kind=jnp.bfloat16):
    drawn = jax.random.normal(own_key, shape, jnp.float32) * deviation
    if len(pieces) > 0:
        drawn = shard_levels(own_key, shape, pieces, -0.22, 0.18) * drawn
    return jnp.clip(drawn, min=-reach, max=reach).astype(kind)


def setup_inputs(seed: int = 0) -> dict:
    key_of = jax.random.split(jax.random.key(seed), 13)
    inputs = noise(key_of[0], (TOKENS, D), 1.0, 6.0, ((0, 256),))
    upstream = noise(key_of[1], (TOKENS, D), 1.0, 6.0, ((0, 256),))
    w_query = noise(key_of[2], (D, HEADS * HD), D ** -0.5, 0.078125, ((1, 16),))
    w_key = noise(key_of[3], (D, KVH * HD), D ** -0.5, 0.078125, ((1, 16),))
    w_value = noise(key_of[4], (D, KVH * HD), D ** -0.5, 0.078125, ((1, 16),))
    w_output = noise(key_of[5], (HEADS * HD, D), (HEADS * HD) ** -0.5, 0.09375, ((0, 16),))
    norm_gain = jnp.clip(1.0 + 0.15 * jax.random.normal(key_of[6], (D,), jnp.float32), 0.25, 1.75)
    query_gain = jnp.clip(1.0 + 0.15 * jax.random.normal(key_of[7], (HD,), jnp.float32), 0.25, 1.75)
    key_gain = jnp.clip(1.0 + 0.15 * jax.random.normal(key_of[8], (HD,), jnp.float32), 0.25, 1.75)
    lengths = jax.vmap(lambda own: uneven(own, SEGS, TOK_DEV, MOSTLEN, 2))(jax.random.split(key_of[9], SHARDS)).reshape((SHARDS, SEGS)).astype(jnp.int32)
    rewards = noise(key_of[10], (SEGMENTS,), 1.0, 4.0, ((0, 16),), jnp.float32)
    groups = plant(jax.random.randint(key_of[11], (SEGMENTS,), 0, GROUPS), jax.random.fold_in(key_of[11], 1), 0, GROUPS - 1).astype(jnp.int32)
    return dict(inputs=inputs, upstream=upstream, w_query=w_query, w_key=w_key, w_value=w_value, w_output=w_output, norm_gain=norm_gain, query_gain=query_gain, key_gain=key_gain, lengths=lengths, rewards=rewards, groups=groups)


eps = 1e-06
rope_base = 1000000.0

def segment_rows(lens, total):
    ends = jnp.cumsum(lens).astype(jnp.int32)
    starts = (ends - lens).astype(jnp.int32)
    rows = jnp.arange(total, dtype=jnp.int32)
    inside = (rows[:, None] >= starts[None, :]) & (rows[:, None] < ends[None, :])
    labels = jnp.arange(lens.shape[0], dtype=jnp.int32)
    segment = lax.optimization_barrier(jnp.sum(jnp.where(inside, labels[None, :], 0), axis=1)).astype(jnp.int32)
    position = (rows - lax.optimization_barrier(jnp.sum(jnp.where(inside, starts[None, :], 0), axis=1))).astype(jnp.int32)
    return (rows, segment, position, inside)

def rope_tables(position, head_dim):
    half = head_dim // 2
    inverse = rope_base ** (-(jnp.arange(half, dtype=jnp.float32) * 2.0 / head_dim))
    angle = position.astype(jnp.float32)[:, None] * inverse[None, :]
    cosine = jnp.concatenate([jnp.cos(angle), jnp.cos(angle)], axis=1)
    sine = jnp.concatenate([jnp.sin(angle), jnp.sin(angle)], axis=1)
    return (cosine, sine)

def rotate(value, cosine, sine):
    half = value.shape[-1] // 2
    return value * cosine + jnp.concatenate([-value[..., half:], value[..., :half]], axis=-1) * sine

def rotate_back(grad, cosine, sine):
    half = grad.shape[-1] // 2
    moved = grad * sine
    return grad * cosine + jnp.concatenate([moved[..., half:], -moved[..., :half]], axis=-1)

def head_norm(value, gain):
    scale = lax.rsqrt(lax.optimization_barrier(jnp.mean(value * value, axis=-1, keepdims=True)) + eps)
    unit = value * scale
    return (unit * gain, unit, scale)

def head_norm_back(grad, gain, unit, scale):
    weighted = grad * gain
    inner = weighted - unit * lax.optimization_barrier(jnp.mean(weighted * unit, axis=-1, keepdims=True))
    return (scale * inner, lax.optimization_barrier(jnp.sum(grad * unit, axis=(0, 1))))

def attend_forward(query, keys, values, q_gain, k_gain, cosine, sine, mask):
    q_normed, q_unit, q_scale = head_norm(query, q_gain)
    k_normed, k_unit, k_scale = head_norm(keys, k_gain)
    q_rot = rotate(q_normed, cosine, sine).astype(jnp.bfloat16)
    k_rot = rotate(k_normed, cosine, sine).astype(jnp.bfloat16)
    factor = query.shape[-1] ** (-0.5)
    scores = jnp.einsum('hqd,hkd->hqk', q_rot.astype(jnp.float32), k_rot.astype(jnp.float32)) * factor
    scores = jnp.where(mask[None, :, :], scores, -1e+30)
    top = lax.optimization_barrier(jnp.max(scores, axis=-1, keepdims=True))
    weights = jnp.exp(scores - top)
    probs = weights / lax.optimization_barrier(jnp.sum(weights, axis=-1, keepdims=True))
    probs_b = probs.astype(jnp.bfloat16)
    output = jnp.einsum('hqk,hkd->hqd', probs_b.astype(jnp.float32), values.astype(jnp.float32)).astype(jnp.bfloat16)
    saved = (q_unit, q_scale, k_unit, k_scale)
    return (output, probs, probs_b, q_rot, k_rot, saved)

def attend_backward(grad_out, output, probs, probs_b, q_rot, k_rot, values, q_gain, k_gain, saved, cosine, sine):
    q_unit, q_scale, k_unit, k_scale = saved
    factor = q_rot.shape[-1] ** (-0.5)
    grad_f = grad_out.astype(jnp.float32)
    grad_probs = jnp.einsum('hqd,hkd->hqk', grad_f, values.astype(jnp.float32))
    delta = lax.optimization_barrier(jnp.sum(grad_f * output.astype(jnp.float32), axis=-1, keepdims=True))
    grad_scores = (probs * (grad_probs - delta) * factor).astype(jnp.bfloat16).astype(jnp.float32)
    grad_qr = jnp.einsum('hqk,hkd->hqd', grad_scores, k_rot.astype(jnp.float32))
    grad_kr = jnp.einsum('hqk,hqd->hkd', grad_scores, q_rot.astype(jnp.float32))
    grad_v = jnp.einsum('hqk,hqd->hkd', probs_b.astype(jnp.float32), grad_f)
    grad_q, q_gain_grad = head_norm_back(rotate_back(grad_qr, cosine, sine), q_gain, q_unit, q_scale)
    grad_k, k_gain_grad = head_norm_back(rotate_back(grad_kr, cosine, sine), k_gain, k_unit, k_scale)
    return (grad_q, grad_k, grad_v, q_gain_grad, k_gain_grad)

def group_sums(rewards, groups):
    onehot = (groups[:, None] == jnp.arange(GROUPS, dtype=jnp.int32)[None, :]).astype(jnp.float32)
    counts = lax.optimization_barrier(jnp.sum(onehot, axis=0))
    sums = lax.optimization_barrier(jnp.sum(onehot * rewards[:, None], axis=0))
    squares = lax.optimization_barrier(jnp.sum(onehot * (rewards * rewards)[:, None], axis=0))
    return (counts, sums, squares)

def advantage_from(rewards, groups, counts, sums, squares):
    onehot = (groups[:, None] == jnp.arange(GROUPS, dtype=jnp.int32)[None, :]).astype(jnp.float32)
    safe = jnp.maximum(counts, 1.0)
    mean = sums / safe
    variance = squares / safe - mean * mean
    row_mean = lax.optimization_barrier(jnp.sum(onehot * mean[None, :], axis=1))
    row_var = lax.optimization_barrier(jnp.sum(onehot * variance[None, :], axis=1))
    return (rewards - row_mean) / jnp.sqrt(row_var + 1.0)

def shard_terms(x_rows, dy_rows, lens, seg_adv, wq, wk, wv, wo, ln_gain, q_gain, k_gain):
    total = x_rows.shape[0]
    rows, segment, position, inside = segment_rows(lens, total)
    row_adv = lax.optimization_barrier(jnp.sum(jnp.where(inside, seg_adv[None, :], 0.0), axis=1))
    cosine, sine = rope_tables(position, HD)
    xf = x_rows.astype(jnp.float32)
    scale = lax.rsqrt(lax.optimization_barrier(jnp.mean(xf * xf, axis=-1, keepdims=True)) + eps)
    unit = xf * scale
    h = (unit * ln_gain).astype(jnp.bfloat16)
    q = jnp.dot(h, wq, preferred_element_type=jnp.float32).astype(jnp.bfloat16)
    k = jnp.dot(h, wk, preferred_element_type=jnp.float32).astype(jnp.bfloat16)
    v = jnp.dot(h, wv, preferred_element_type=jnp.float32).astype(jnp.bfloat16)
    kv_index = (jnp.arange(HEADS, dtype=jnp.int32) % KVH).astype(jnp.int32)
    query = q.reshape(total, HEADS, HD).transpose(1, 0, 2).astype(jnp.float32)
    keys = k.reshape(total, KVH, HD).transpose(1, 0, 2)[kv_index].astype(jnp.float32)
    values = v.reshape(total, KVH, HD).transpose(1, 0, 2)[kv_index]
    mask = (segment[:, None] == segment[None, :]) & (rows[:, None] >= rows[None, :])
    output, probs, probs_b, q_rot, k_rot, saved = attend_forward(query, keys, values, q_gain, k_gain, cosine, sine, mask)
    attn = output.transpose(1, 0, 2).reshape(total, HEADS * HD)
    grad_rows = (dy_rows.astype(jnp.float32) * row_adv[:, None]).astype(jnp.bfloat16)
    dwo_term = jnp.dot(grad_rows.T, attn, preferred_element_type=jnp.float32).astype(jnp.bfloat16)
    grad_out = jnp.dot(grad_rows, wo.T, preferred_element_type=jnp.float32).astype(jnp.bfloat16)
    grad_out = grad_out.reshape(total, HEADS, HD).transpose(1, 0, 2)
    grad_q, grad_k, grad_v, q_gain_grad, k_gain_grad = attend_backward(grad_out, output, probs, probs_b, q_rot, k_rot, values, q_gain, k_gain, saved, cosine, sine)
    per_dev = HEADS // N_TENSOR
    onehot = (kv_index.reshape(N_TENSOR, per_dev)[:, :, None] == jnp.arange(KVH, dtype=jnp.int32)[None, None, :]).astype(jnp.float32)
    k_parts = jnp.einsum('njth,njk->nkth', grad_k.reshape(N_TENSOR, per_dev, total, HD), onehot).astype(jnp.bfloat16)
    v_parts = jnp.einsum('njth,njk->nkth', grad_v.reshape(N_TENSOR, per_dev, total, HD), onehot).astype(jnp.bfloat16)
    k_parts = lax.optimization_barrier(k_parts)
    v_parts = lax.optimization_barrier(v_parts)
    dk = lax.optimization_barrier(jnp.sum(k_parts.astype(jnp.float32), axis=0)).transpose(1, 0, 2).reshape(total, KVH * HD).astype(jnp.bfloat16)
    dv = lax.optimization_barrier(jnp.sum(v_parts.astype(jnp.float32), axis=0)).transpose(1, 0, 2).reshape(total, KVH * HD).astype(jnp.bfloat16)
    dq = grad_q.transpose(1, 0, 2).reshape(total, HEADS * HD).astype(jnp.bfloat16)
    q_cols = HEADS * HD // N_TENSOR
    kv_cols = KVH * HD // N_TENSOR
    dh_parts = jnp.einsum('tnc,dnc->ntd', dq.reshape(total, N_TENSOR, q_cols).astype(jnp.float32), wq.reshape(D, N_TENSOR, q_cols).astype(jnp.float32))
    dh_parts = dh_parts + jnp.einsum('tnc,dnc->ntd', dk.reshape(total, N_TENSOR, kv_cols).astype(jnp.float32), wk.reshape(D, N_TENSOR, kv_cols).astype(jnp.float32))
    dh_parts = dh_parts + jnp.einsum('tnc,dnc->ntd', dv.reshape(total, N_TENSOR, kv_cols).astype(jnp.float32), wv.reshape(D, N_TENSOR, kv_cols).astype(jnp.float32))
    dh_parts = lax.optimization_barrier(dh_parts.astype(jnp.bfloat16))
    dh = lax.optimization_barrier(jnp.sum(dh_parts.astype(jnp.float32), axis=0))
    weighted = dh * ln_gain
    dx_rows = scale * (weighted - unit * lax.optimization_barrier(jnp.mean(weighted * unit, axis=-1, keepdims=True))) + grad_rows.astype(jnp.float32)
    gain_term = lax.optimization_barrier(jnp.sum(dh * unit, axis=0))
    dwq_term = jnp.dot(h.T, dq, preferred_element_type=jnp.float32).astype(jnp.bfloat16)
    dwk_term = jnp.dot(h.T, dk, preferred_element_type=jnp.float32).astype(jnp.bfloat16)
    dwv_term = jnp.dot(h.T, dv, preferred_element_type=jnp.float32).astype(jnp.bfloat16)
    terms = (dwq_term, dwk_term, dwv_term, dwo_term, gain_term, q_gain_grad, k_gain_grad)
    return (dx_rows.astype(jnp.bfloat16), terms)

def reference(inputs, upstream, w_query, w_key, w_value, w_output, norm_gain, query_gain, key_gain, lengths, rewards, groups):
    counts, sums, squares = group_sums(rewards, groups)
    advantage = advantage_from(rewards, groups, counts, sums, squares)
    x_shards = inputs.reshape(N_DP, TOK_DEV, D)
    dy_shards = upstream.reshape(N_DP, TOK_DEV, D)
    adv_shards = advantage.reshape(N_DP, SEGS)

    def step(carry, item):
        x_rows, dy_rows, lens, seg_adv = item
        dx_rows, terms = shard_terms(x_rows, dy_rows, lens, seg_adv, w_query, w_key, w_value, w_output, norm_gain, query_gain, key_gain)
        carry = tuple((c + t.astype(jnp.float32) for c, t in zip(carry, terms)))
        return (carry, dx_rows)
    init = (jnp.zeros((D, HEADS * HD), jnp.float32), jnp.zeros((D, KVH * HD), jnp.float32), jnp.zeros((D, KVH * HD), jnp.float32), jnp.zeros((D, HEADS * HD), jnp.float32), jnp.zeros((D,), jnp.float32), jnp.zeros((HD,), jnp.float32), jnp.zeros((HD,), jnp.float32))
    sums_out, dx_all = lax.scan(step, init, (x_shards, dy_shards, lengths, adv_shards))
    g_query, g_key, g_value, g_output, g_norm, g_qgain, g_kgain = sums_out
    return (dx_all.reshape(TOKENS, D), g_query, g_key, g_value, g_output, g_norm, g_qgain, g_kgain)
```

```python
import jax
import jax.numpy as jnp
from jax import lax
from jax.sharding import PartitionSpec as P

KVH = 4
GROUPS = 16
HD = 128
EPS = 1e-06
ROPE_BASE = 1000000.0


F32 = jnp.float32
BF16 = jnp.bfloat16


def t_pairs(move, keep=None):
    pairs = []
    for y in range(4):
        for z in range(2):
            for c in range(2):
                if keep is None or keep(y, z, c):
                    a, b, d = move(y, z, c)
                    pairs.append((y * 4 + z * 2 + c, (a % 4) * 4 + b * 2 + d))
    return pairs


def send_y(value, step, keep=None):
    return lax.ppermute(value, "tensor", t_pairs(lambda y, z, c: (y + step, z, c), keep))


def swap_y(value, bits):
    return lax.ppermute(value, "tensor", t_pairs(lambda y, z, c: (y ^ bits, z, c)))


def swap_z(value):
    return lax.ppermute(value, "tensor", t_pairs(lambda y, z, c: (y, 1 - z, c)))


def swap_core(value):
    return lax.ppermute(value, "tensor", t_pairs(lambda y, z, c: (y, z, 1 - c)))


def send_x(value, step):
    return lax.ppermute(
        value, "dp", [(h * 4 + x, h * 4 + (x + step) % 4) for h in range(4) for x in range(4)]
    )


def send_h(value, step):
    return lax.ppermute(
        value, "dp", [(h * 4 + x, ((h + step) % 4) * 4 + x) for h in range(4) for x in range(4)]
    )


def swap_x(value, bits):
    return lax.ppermute(
        value, "dp", [(h * 4 + x, h * 4 + (x ^ bits)) for h in range(4) for x in range(4)]
    )


def swap_h(value, bits):
    return lax.ppermute(
        value, "dp", [(h * 4 + x, (h ^ bits) * 4 + x) for h in range(4) for x in range(4)]
    )


def total4(value, swap):
    one, two, three = swap(value, 1), swap(value, 2), swap(value, 3)
    return (value + one) + (two + three)


def gather_chips(own):
    from_m = send_y(own, 1)
    from_p = send_y(own, -1)
    from_z = swap_z(own)
    from_2 = send_y(own, 2)
    zm = send_y(from_z, 1)
    zp = send_y(from_z, -1)
    z2 = swap_z(from_2)
    return jnp.concatenate([own, from_z, from_p, zp, from_2, z2, from_m, zm], axis=0)


def gather_rows(own):
    mine = gather_chips(own)
    mine = lax.optimization_barrier(mine)
    other = swap_core(mine)
    return jnp.concatenate([mine, other], axis=0)


def roll_y(value, shift):
    cols = value.shape[-1]
    return jnp.roll(value.reshape(2, 4, 64, cols), shift, axis=1).reshape(512, cols)


def flip_z(value):
    cols = value.shape[-1]
    return jnp.flip(value.reshape(8, 2, 32, cols), axis=1).reshape(512, cols)


def flip_c(value):
    cols = value.shape[-1]
    return jnp.flip(value.reshape(2, 256, cols), axis=0).reshape(512, cols)


def rotate(value, cosine, sine):
    half = value.shape[-1] // 2
    return value * cosine + jnp.concatenate([-value[..., half:], value[..., :half]], axis=-1) * sine


def rotate_back(grad, cosine, sine):
    half = grad.shape[-1] // 2
    moved = grad * sine
    return grad * cosine + jnp.concatenate([moved[..., half:], -moved[..., :half]], axis=-1)


def head_norm(value, gain):
    scale = lax.rsqrt(jnp.mean(value * value, axis=-1, keepdims=True) + EPS)
    unit = value * scale
    return (unit * gain, unit, scale)


def head_norm_back(grad, gain, unit, scale):
    weighted = grad * gain
    inner = weighted - unit * jnp.mean(weighted * unit, axis=-1, keepdims=True)
    return (scale * inner, jnp.sum(grad * unit, axis=(0, 1)))


def reduce_dp(blocks, h_at):
    far = blocks[2]
    a = send_x(far[:2], 1)
    b = send_x(far[2:], -1)
    right = jnp.concatenate([blocks[1][:2] + a, blocks[1][2:]], axis=0)
    left = jnp.concatenate([blocks[3][:2], blocks[3][2:] + b], axis=0)
    r = send_x(right, 1)
    s = send_x(left, -1)
    here = (blocks[0].astype(F32) + r.astype(F32) + s.astype(F32)).astype(BF16)
    part = [lax.dynamic_index_in_dim(here, (h_at + k) % 4, 0, keepdims=False) for k in range(4)]
    one, three, two = send_h(part[1], 1), send_h(part[3], -1), send_h(part[2], 2)
    return (part[0].astype(F32) + two.astype(F32)) + (one.astype(F32) + three.astype(F32))


def weight_grad(left, right, x_at):
    full = jnp.dot(left.T, right, preferred_element_type=F32).astype(BF16)
    full = full.reshape(4, 4, 320, right.shape[1])
    return [lax.dynamic_index_in_dim(full, (x_at + s) % 4, 1, keepdims=False) for s in range(4)]


def on_device(
    inputs,
    upstream,
    w_query,
    w_key,
    w_value,
    w_output,
    norm_gain,
    query_gain,
    key_gain,
    lengths,
    rewards,
    groups,
):
    t_at = lax.axis_index("tensor")
    d_at = lax.axis_index("dp")
    y_at, z_at, c_at = t_at // 4, (t_at // 2) % 2, t_at % 2
    h_at, x_at = d_at // 4, d_at % 4

    x_own = inputs.astype(F32)
    scale_own = lax.rsqrt(jnp.mean(x_own * x_own, axis=-1, keepdims=True) + EPS)
    unit_own = x_own * scale_own
    normed_own = (unit_own * norm_gain).astype(BF16)
    normed = gather_rows(normed_own)

    onehot = (groups[:, None] == jnp.arange(GROUPS, dtype=jnp.int32)[None, :]).astype(F32)
    stats = jnp.concatenate(
        [
            jnp.sum(onehot, axis=0),
            jnp.sum(onehot * rewards[:, None], axis=0),
            jnp.sum(onehot * (rewards * rewards)[:, None], axis=0),
        ]
    )
    stats = total4(total4(stats, swap_x), swap_h)
    counts, sums, squares = stats[:GROUPS], stats[GROUPS : 2 * GROUPS], stats[2 * GROUPS :]
    safe = jnp.maximum(counts, 1.0)
    mean = sums / safe
    variance = squares / safe - mean * mean
    seg_mean = jnp.sum(onehot * mean[None, :], axis=1)
    seg_var = jnp.sum(onehot * variance[None, :], axis=1)
    seg_adv = (rewards - seg_mean) / jnp.sqrt(seg_var + 1.0)

    lens = lengths[0]
    ends = jnp.cumsum(lens)
    starts = ends - lens
    j = jnp.arange(512, dtype=jnp.int32)
    t_of = (
        ((y_at + (j // 64) % 4) % 4) * 4
        + jnp.bitwise_xor(z_at, (j // 32) % 2) * 2
        + jnp.bitwise_xor(c_at, j // 256)
    )
    rows = t_of * 32 + j % 32
    inside = (rows[:, None] >= starts[None, :]) & (rows[:, None] < ends[None, :])
    segment = jnp.sum(jnp.where(inside, jnp.arange(8, dtype=jnp.int32)[None, :], 0), axis=1)
    position = rows - jnp.sum(jnp.where(inside, starts[None, :], 0), axis=1)
    own_adv = jnp.sum(jnp.where(inside[:32], seg_adv[None, :], 0.0), axis=1)
    grad_own = (upstream.astype(F32) * own_adv[:, None]).astype(BF16)
    grad_rows = gather_rows(grad_own)

    half = HD // 2
    inverse = ROPE_BASE ** (-(jnp.arange(half, dtype=F32) * 2.0 / HD))
    angle = position.astype(F32)[:, None] * inverse[None, :]
    cosine = jnp.concatenate([jnp.cos(angle), jnp.cos(angle)], axis=1)
    sine = jnp.concatenate([jnp.sin(angle), jnp.sin(angle)], axis=1)
    mask = (segment[:, None] == segment[None, :]) & (rows[:, None] >= rows[None, :])

    wkv = jnp.stack([w_key.T, w_value.T])
    wkv_pair = swap_core(wkv)
    wkv = jnp.stack(
        [jnp.where(c_at == 0, wkv, wkv_pair), jnp.where(c_at == 0, wkv_pair, wkv)], axis=1
    )
    wkv_pair = swap_z(wkv)
    wkv = jnp.stack(
        [jnp.where(z_at == 0, wkv, wkv_pair), jnp.where(z_at == 0, wkv_pair, wkv)], axis=1
    ).reshape(256, -1)

    kv = lax.dot_general(
        normed, wkv, (((1,), (1,)), ((), ())), preferred_element_type=F32
    ).astype(BF16)
    of_core = lambda step: (lambda y, z, c: (y % 4) // 2 == c)
    kv_at = [
        kv,
        roll_y(send_y(kv, -1, of_core(-1)), 1),
        roll_y(send_y(kv, 2, of_core(2)), 2),
        roll_y(send_y(kv, 1, of_core(1)), 3),
    ]
    query_proj = jnp.dot(normed, w_query, preferred_element_type=F32).astype(BF16)
    kv_at = jnp.stack(kv_at)
    step_a = (2 * c_at - y_at) % 4
    step_b = (2 * c_at + 1 - y_at) % 4
    kv_two = jnp.stack(
        [
            lax.dynamic_index_in_dim(kv_at, step_a, 0, keepdims=False),
            lax.dynamic_index_in_dim(kv_at, step_b, 0, keepdims=False),
        ]
    )
    keys = kv_two[:, :, :HD].astype(F32)
    values = kv_two[:, :, HD:]
    query = query_proj.reshape(512, 2, HD).transpose(1, 0, 2).astype(F32)

    factor = HD ** (-0.5)
    q_normed, q_unit, q_scale = head_norm(query, query_gain)
    k_normed, k_unit, k_scale = head_norm(keys, key_gain)
    q_rot = rotate(q_normed, cosine, sine).astype(BF16)
    k_rot = rotate(k_normed, cosine, sine).astype(BF16)
    scores = jnp.einsum("hqd,hkd->hqk", q_rot, k_rot, preferred_element_type=F32) * factor
    scores = jnp.where(mask[None, :, :], scores, -1e30)
    top = jnp.max(scores, axis=-1, keepdims=True)
    weights = jnp.exp(scores - top)
    probs = weights / jnp.sum(weights, axis=-1, keepdims=True)
    probs_b = probs.astype(BF16)
    output = jnp.einsum("hqk,hkd->hqd", probs_b, values, preferred_element_type=F32).astype(BF16)
    attended = output.transpose(1, 0, 2).reshape(512, 2 * HD)
    out_blocks = weight_grad(grad_rows, attended, x_at)
    output_grads = reduce_dp(out_blocks, h_at)

    grad_out = lax.dot_general(
        grad_rows, w_output, (((1,), (1,)), ((), ())), preferred_element_type=F32
    ).astype(BF16)
    grad_out = grad_out.reshape(512, 2, HD).transpose(1, 0, 2)
    grad_probs = jnp.einsum("hqd,hkd->hqk", grad_out, values, preferred_element_type=F32)
    delta = jnp.sum(grad_out.astype(F32) * output.astype(F32), axis=-1, keepdims=True)
    grad_scores = (probs * (grad_probs - delta) * factor).astype(BF16)
    grad_qr = jnp.einsum("hqk,hkd->hqd", grad_scores, k_rot, preferred_element_type=F32)
    grad_kr = jnp.einsum("hqk,hqd->hkd", grad_scores, q_rot, preferred_element_type=F32)
    grad_v = jnp.einsum("hqk,hqd->hkd", probs_b, grad_out, preferred_element_type=F32)
    grad_q, q_gain_grad = head_norm_back(
        rotate_back(grad_qr, cosine, sine), query_gain, q_unit, q_scale
    )
    grad_k, k_gain_grad = head_norm_back(
        rotate_back(grad_kr, cosine, sine), key_gain, k_unit, k_scale
    )
    query_proj_grad = grad_q.transpose(1, 0, 2).reshape(512, 2 * HD).astype(BF16)

    back = lambda rows_of: lax.dot_general(
        rows_of, w_query, (((1,), (1,)), ((), ())), preferred_element_type=F32
    ).astype(BF16)
    part_other = back(query_proj_grad[256:])
    part_mine = back(query_proj_grad[:256])
    both = (part_mine.astype(F32) + swap_core(part_other).astype(F32)).reshape(4, 2, 32, -1)
    first_z = swap_z(both[2, 1].astype(BF16))
    first_p = send_y(both[1, 1].astype(BF16), 1)
    first_m = send_y(both[3, 1].astype(BF16), -1)

    dkv = jnp.concatenate([grad_k, grad_v], axis=2).astype(BF16)
    zero = jnp.zeros_like(dkv[0])
    slot = [jnp.where(step_a == s, dkv[0], jnp.where(step_b == s, dkv[1], zero)) for s in range(4)]
    to_core = lambda step: (lambda y, z, c: ((y + step) % 4) // 2 == c)
    got = [slot[0]] + [
        roll_y(send_y(slot[s], s, to_core(s)), -s) for s in (1, 2, 3)
    ]
    dkv_sum = sum(g.astype(F32) for g in got)
    dkv_sum = (dkv_sum + flip_z(swap_z(dkv_sum.astype(BF16))).astype(F32)).astype(BF16)
    dkv_sum = dkv_sum + flip_c(swap_core(dkv_sum))

    rows_here = dkv_sum[:256].reshape(4, 2, 32, 2 * HD)[:, 0].reshape(128, 2 * HD)
    kv_term = jnp.dot(rows_here, wkv, preferred_element_type=F32).reshape(4, 32, -1)
    second_2 = send_y((both[2, 0] + first_z.astype(F32) + kv_term[2]).astype(BF16), 2)
    second_p = send_y((both[1, 0] + kv_term[1]).astype(BF16), 1)
    second_m = send_y((both[3, 0] + kv_term[3]).astype(BF16), -1)
    second_z = swap_z((both[0, 1] + first_p.astype(F32) + first_m.astype(F32)).astype(BF16))
    normed_grad = (
        both[0, 0]
        + kv_term[0]
        + second_z.astype(F32)
        + second_2.astype(F32)
        + second_p.astype(F32)
        + second_m.astype(F32)
    )

    weighted = normed_grad * norm_gain
    input_grad = scale_own * (
        weighted - unit_own * jnp.mean(weighted * unit_own, axis=-1, keepdims=True)
    ) + grad_own.astype(F32)

    gains = jnp.concatenate([jnp.sum(normed_grad * unit_own, axis=0), q_gain_grad, k_gain_grad])
    gains = gains + swap_core(gains)
    gains = gains + swap_z(gains)
    gains = total4(total4(total4(gains, swap_y), swap_x), swap_h)

    own_cols = lax.dynamic_index_in_dim(
        dkv_sum.reshape(512, 2, 4, 32), z_at * 2 + c_at, 2, keepdims=False
    ).reshape(512, 64)
    combined = jnp.concatenate([query_proj_grad, own_cols], axis=1)
    grads = reduce_dp(weight_grad(normed, combined, x_at), h_at)

    return (
        input_grad.astype(BF16),
        grads[:, :256],
        grads[:, 256:288],
        grads[:, 288:320],
        output_grads,
        gains[:5120],
        gains[5120:5248],
        gains[5248:],
    )


def solution(mesh):
    in_specs = (
        P(("dp", "tensor"), None),
        P(("dp", "tensor"), None),
        P(None, "tensor"),
        P(None, "tensor"),
        P(None, "tensor"),
        P("tensor", None),
        P(),
        P(),
        P(),
        P("dp", None),
        P("dp"),
        P("dp"),
    )
    out_specs = (
        P(("dp", "tensor"), None),
        P("dp", "tensor"),
        P("dp", "tensor"),
        P("dp", "tensor"),
        P("dp", "tensor"),
        P(),
        P(),
        P(),
    )
    return jax.shard_map(
        on_device, mesh=mesh, in_specs=in_specs, out_specs=out_specs, check_vma=False
    )
```

```python
import functools

import jax
import jax.numpy as jnp
from jax import lax
from jax.experimental import pallas as pl
from jax.experimental.pallas import tpu as pltpu
from jax.sharding import PartitionSpec as P

KVH = 4
GROUPS = 16
HD = 128
EPS = 1e-06
ROPE_BASE = 1000000.0


F32 = jnp.float32
BF16 = jnp.bfloat16


def t_pairs(move, keep=None):
    pairs = []
    for y in range(4):
        for z in range(2):
            for c in range(2):
                if keep is None or keep(y, z, c):
                    a, b, d = move(y, z, c)
                    pairs.append((y * 4 + z * 2 + c, (a % 4) * 4 + b * 2 + d))
    return pairs


def send_y(value, step, keep=None):
    return lax.ppermute(value, "tensor", t_pairs(lambda y, z, c: (y + step, z, c), keep))


def swap_y(value, bits):
    return lax.ppermute(value, "tensor", t_pairs(lambda y, z, c: (y ^ bits, z, c)))


def swap_z(value):
    return lax.ppermute(value, "tensor", t_pairs(lambda y, z, c: (y, 1 - z, c)))


def swap_core(value):
    return lax.ppermute(value, "tensor", t_pairs(lambda y, z, c: (y, z, 1 - c)))


def send_x(value, step):
    return lax.ppermute(
        value, "dp", [(h * 4 + x, h * 4 + (x + step) % 4) for h in range(4) for x in range(4)]
    )


def send_h(value, step):
    return lax.ppermute(
        value, "dp", [(h * 4 + x, ((h + step) % 4) * 4 + x) for h in range(4) for x in range(4)]
    )


def swap_x(value, bits):
    return lax.ppermute(
        value, "dp", [(h * 4 + x, h * 4 + (x ^ bits)) for h in range(4) for x in range(4)]
    )


def swap_h(value, bits):
    return lax.ppermute(
        value, "dp", [(h * 4 + x, (h ^ bits) * 4 + x) for h in range(4) for x in range(4)]
    )


def total4(value, swap):
    one, two, three = swap(value, 1), swap(value, 2), swap(value, 3)
    return (value + one) + (two + three)


def tie(*values):
    return lax.optimization_barrier(values)


VMEM = pl.BlockSpec(memory_space=pltpu.VMEM)
SMEM = pl.BlockSpec(memory_space=pltpu.SMEM)
ANY = pl.BlockSpec(memory_space=pl.ANY)
NT = (((1,), (1,)), ((), ()))
TN = (((0,), (0,)), ((), ()))
D = 5120


def dot(a, b, dims=(((1,), (0,)), ((), ()))):
    return lax.dot_general(a, b, dims, preferred_element_type=F32)


def call(kernel, out, args, specs=None, scratch=(), limit=48):
    many = isinstance(out, list)
    shapes = [jax.ShapeDtypeStruct(s, t) for s, t in (out if many else [out])]
    result = pl.pallas_call(
        kernel,
        out_shape=shapes,
        in_specs=list(specs) if specs else [VMEM] * len(args),
        out_specs=[VMEM] * len(shapes),
        scratch_shapes=list(scratch),
        compiler_params=pltpu.CompilerParams(vmem_limit_bytes=limit * 2**20),
    )(*args)
    return result if many else result[0]


def load_rows(blocks, whole, sems):
    copies = [
        pltpu.make_async_copy(block, whole.at[pl.ds(n * 32, 32)], sems.at[n])
        for n, block in enumerate(blocks)
    ]
    for copy in copies:
        copy.start()
    return copies


ROWS_SCRATCH = (pltpu.VMEM((512, D), BF16), pltpu.SemaphoreType.DMA((16,)))


def project_kernel(*refs):
    blocks, (w_q, w_kv, q_out, kv_out, whole, sems) = refs[:16], refs[16:]
    copies = load_rows(blocks, whole, sems)
    for part in range(2):
        for copy in copies[part * 8 : part * 8 + 8]:
            copy.wait()
        at = pl.ds(part * 256, 256)
        kv_out[at] = dot(whole[at], w_kv[...], NT).astype(BF16)
        q_out[at] = dot(whole[at], w_q[...]).astype(BF16)


def project(blocks, w_q, w_kv):
    return call(
        project_kernel,
        [((512, 256), BF16), ((512, 128), BF16)],
        [*blocks, w_q, w_kv],
        [ANY] * 16 + [VMEM] * 2,
        ROWS_SCRATCH,
    )


def flip_z(value):
    return jnp.concatenate([value[128:256], value[:128], value[384:], value[256:384]], axis=0)


def flip_c(value):
    return jnp.concatenate([value[256:], value[:256]], axis=0)


def turn_y(value, step):
    if step % 4 == 0:
        return value
    parts = []
    for group in range(4):
        for dy in range(4):
            at = group * 128 + ((dy + step) % 4) * 32
            parts.append(value[at : at + 32])
    return jnp.concatenate(parts, axis=0)


def merge_kernel(place, own, pair, out):
    mine = own[...]
    theirs = flip_z(pair[...])
    first = place[1] == 0
    lo = jnp.where(first, mine, theirs)
    hi = jnp.where(first, theirs, mine)
    out[...] = jnp.concatenate([lo[:, :64], hi[:, :64], lo[:, 64:], hi[:, 64:]], axis=1)


def pick_heads(place, slots, heads):
    for n in range(2):
        step = (2 * place[2] + n - place[0] + 4) % 4
        for s in range(4):

            @pl.when(step == s)
            def _():
                heads[n] = turn_y(slots[s][...], -s)


def spin(value, cosine, sine):
    return value * cosine + pltpu.roll(value, 64, 1) * sine


def spin_back(grad, cosine, sine):
    return grad * cosine - pltpu.roll(grad, 64, 1) * sine


def norm(value):
    value = value.astype(F32)
    scale = lax.rsqrt(jnp.mean(value * value, axis=-1, keepdims=True) + EPS)
    return value * scale, scale


def forward_kernel(place, q, s0, s1, s2, s3, cosine, sine, seg, q_gain, k_gain, out, probs, heads):
    pick_heads(place, (s0, s1, s2, s3), heads)
    co, si = cosine[...], sine[...]
    seg_q, row_q = seg[:, 0:1], seg[:, 1:2]
    turned = seg[...].T
    keep = (seg_q == turned[0:1]) & (row_q >= turned[1:2])
    for n in range(2):
        q_unit, _ = norm(q[:, n * HD : n * HD + HD])
        k_unit, _ = norm(heads[n, :, :HD])
        q_rot = spin(q_unit * q_gain[...], co, si).astype(BF16)
        k_rot = spin(k_unit * k_gain[...], co, si).astype(BF16)
        scores = jnp.where(keep, dot(q_rot, k_rot, NT) * HD**-0.5, -1e30)
        weights = jnp.exp(scores - jnp.max(scores, axis=-1, keepdims=True))
        soft = weights / jnp.sum(weights, axis=-1, keepdims=True)
        probs[n] = soft
        out[:, n * HD : n * HD + HD] = dot(soft.astype(BF16), heads[n, :, HD:]).astype(BF16)


def backward_kernel(*refs):
    blocks = refs[:16]
    place, w_out, q, s0, s1, s2, s3, cosine, sine, q_gain, k_gain, probs, attended = refs[16:29]
    dq, d0, d1, d2, d3, gains, heads, whole, sems, grad_out = refs[29:]
    copies = load_rows(blocks, whole, sems)
    pick_heads(place, (s0, s1, s2, s3), heads)
    for part in range(2):
        for copy in copies[part * 8 : part * 8 + 8]:
            copy.wait()
        at = pl.ds(part * 256, 256)
        grad_out[at] = dot(whole[at], w_out[...], NT).astype(BF16)
    co, si = cosine[...], sine[...]
    q_sum = jnp.zeros((1, HD), F32)
    k_sum = jnp.zeros((1, HD), F32)
    d0[...] = jnp.zeros_like(d0)
    for n in range(2):
        cols = slice(n * HD, n * HD + HD)
        q_unit, q_scale = norm(q[:, cols])
        k_unit, k_scale = norm(heads[n, :, :HD])
        q_rot = spin(q_unit * q_gain[...], co, si).astype(BF16)
        k_rot = spin(k_unit * k_gain[...], co, si).astype(BF16)
        grad = grad_out[:, cols]
        delta = jnp.sum(
            grad.astype(F32) * attended[:, cols].astype(F32), axis=-1, keepdims=True
        )
        soft = probs[n]
        score = (soft * (dot(grad, heads[n, :, HD:], NT) - delta) * HD**-0.5).astype(BF16)
        e_q = spin_back(dot(score, k_rot), co, si)
        e_k = spin_back(dot(score, q_rot, TN), co, si)
        grad_v = dot(soft.astype(BF16), grad, TN).astype(BF16)
        q_sum += jnp.sum(e_q * q_unit, axis=0, keepdims=True)
        k_sum += jnp.sum(e_k * k_unit, axis=0, keepdims=True)
        e_q = e_q * q_gain[...]
        e_k = e_k * k_gain[...]
        grad_q = q_scale * (e_q - q_unit * jnp.mean(e_q * q_unit, axis=-1, keepdims=True))
        grad_k = k_scale * (e_k - k_unit * jnp.mean(e_k * k_unit, axis=-1, keepdims=True))
        dq[:, cols] = grad_q.astype(BF16)
        both = jnp.concatenate([grad_k.astype(BF16), grad_v], axis=1)
        step = (2 * place[2] + n - place[0] + 4) % 4
        for s, slot in enumerate((d0, d1, d2, d3)):

            @pl.when(step == s)
            def _():
                slot[...] = both

    gains[...] = jnp.concatenate([q_sum, k_sum], axis=0)


def plane_kernel(a, b, c, d, out):
    total = a[...].astype(F32)
    for step, ref in ((1, b), (2, c), (3, d)):
        total += turn_y(ref[...], step).astype(F32)
    out[...] = total.astype(BF16)


def pair_kernel(a, b, out):
    out[...] = (a[...].astype(F32) + flip_z(b[...]).astype(F32)).astype(BF16)


def columns_kernel(place, a, b, dq, right, rows_own, rows_pair):
    full = (a[...].astype(F32) + flip_c(b[...]).astype(F32)).astype(BF16)
    halves = [jnp.concatenate([full[:128, z * 64 : z * 64 + 64], full[:128, HD + z * 64 : HD + z * 64 + 64]], axis=1) for z in range(2)]
    first = place[1] == 0
    rows_own[...] = jnp.where(first, halves[0], halves[1])
    rows_pair[...] = jnp.where(first, halves[1], halves[0])
    right[:, :256] = dq[...]
    spot = place[1] * 2 + place[2]
    for n in range(4):

        @pl.when(spot == n)
        def _():
            right[:, 256:] = jnp.concatenate(
                [full[:, n * 32 : n * 32 + 32], full[:, HD + n * 32 : HD + n * 32 + 32]], axis=1
            )


def weight_kernel(*refs):
    blocks = refs[:16]
    place, right, o0, o1, o2a, o2b, o3, whole, sems = refs[16:]
    copies = load_rows(blocks, whole, sems)
    for copy in copies:
        copy.wait()
    for j in range(8):
        part = dot(whole[:, j * 640 : j * 640 + 640], right[...], TN).astype(BF16)
        for n in range(2):
            x, h = (2 * j + n) % 4, (2 * j + n) // 4
            s = (x - place[4] + 4) % 4
            k = (h - place[3] + 4) % 4
            tile = part[n * 320 : n * 320 + 320]
            for at, out in ((0, o0), (1, o1), (3, o3)):

                @pl.when(s == at)
                def _():
                    out[k] = tile

            @pl.when((s == 2) & (k < 2))
            def _():
                o2a[jnp.minimum(k, 1)] = tile

            @pl.when((s == 2) & (k >= 2))
            def _():
                o2b[jnp.maximum(k - 2, 0)] = tile


def weight_grad(blocks, place, right):
    cols = right.shape[1]
    four, two = ((4, 320, cols), BF16), ((2, 320, cols), BF16)
    return call(
        weight_kernel,
        [four, four, two, two, four],
        [*blocks, place, right],
        [ANY] * 16 + [SMEM, VMEM],
        ROWS_SCRATCH,
    )


def around_kernel(o1, o3, a, b, right, left):
    right[0:2] = (o1[0:2].astype(F32) + a[...].astype(F32)).astype(BF16)
    right[2:4] = o1[2:4]
    left[0:2] = o3[0:2]
    left[2:4] = (o3[2:4].astype(F32) + b[...].astype(F32)).astype(BF16)


def meet_kernel(o0, r, s, p0, p1, p2, p3):
    for k, out in enumerate((p0, p1, p2, p3)):
        out[...] = (o0[k].astype(F32) + r[k].astype(F32) + s[k].astype(F32)).astype(BF16)


def reduce_first(parts):
    o0, o1, o2a, o2b, o3 = parts
    return o0, o1, o3, send_x(o2a, 1), send_x(o2b, -1)


def reduce_second(state):
    o0, o1, o3, a, b = state
    right, left = call(around_kernel, [(o1.shape, BF16)] * 2, [o1, o3, a, b])
    return o0, send_x(right, 1), send_x(left, -1)


def reduce_third(state):
    o0, r, s = state
    p0, p1, p2, p3 = call(meet_kernel, [(o0.shape[1:], BF16)] * 4, [o0, r, s])
    return p0, send_h(p1, 1), send_h(p2, 2), send_h(p3, -1)


def reduce_last(state):
    zero, one, two, three = [part.astype(F32) for part in state]
    return (zero + two) + (one + three)


def block_at(dz, dy):
    return pl.ds((dz * 4 + dy) * 32, 32)


def first_kernel(mine, pair, z2, p, m):
    for out, dy in ((z2, 2), (p, 1), (m, 3)):
        at = block_at(1, dy)
        out[...] = (mine[at].astype(F32) + pair[at].astype(F32)).astype(BF16)


def second_kernel(mine, pair, fz, fp, fm, ro, rp, wo, wp, s2, sp, sm, sz, own):
    term = dot(ro[...], wo[...]) + dot(rp[...], wp[...])

    def both(dz, dy):
        at = block_at(dz, dy)
        return mine[at].astype(F32) + pair[at].astype(F32)

    s2[...] = (both(0, 2) + fz[...].astype(F32) + term[64:96]).astype(BF16)
    sp[...] = (both(0, 1) + term[32:64]).astype(BF16)
    sm[...] = (both(0, 3) + term[96:128]).astype(BF16)
    sz[...] = (both(1, 0) + fp[...].astype(F32) + fm[...].astype(F32)).astype(BF16)
    own[...] = both(0, 0) + term[0:32]


def last_kernel(own, s2, sp, sm, sz, x, gain, grad, out, sums):
    total = own[...] + s2[...].astype(F32) + sp[...].astype(F32)
    total += sm[...].astype(F32) + sz[...].astype(F32)
    value = x[...].astype(F32)
    scale = lax.rsqrt(jnp.mean(value * value, axis=-1, keepdims=True) + EPS)
    unit = value * scale
    weighted = total * gain[...]
    inner = weighted - unit * jnp.mean(weighted * unit, axis=-1, keepdims=True)
    out[...] = (scale * inner + grad[...].astype(F32)).astype(BF16)
    sums[...] = jnp.sum(total * unit, axis=0, keepdims=True)


def normed_kernel(x, gain, out):
    value = x[...].astype(F32)
    scale = lax.rsqrt(jnp.mean(value * value, axis=-1, keepdims=True) + EPS)
    out[...] = (value * scale * gain[...]).astype(BF16)


def on_device(
    inputs,
    upstream,
    w_query,
    w_key,
    w_value,
    w_output,
    norm_gain,
    query_gain,
    key_gain,
    lengths,
    rewards,
    groups,
):
    t_at = lax.axis_index("tensor")
    d_at = lax.axis_index("dp")
    y_at, z_at, c_at = t_at // 4, (t_at // 2) % 2, t_at % 2
    place = jnp.stack([y_at, z_at, c_at, d_at // 4, d_at % 4]).astype(jnp.int32)
    gain_row = norm_gain.reshape(1, D)

    normed_own = call(normed_kernel, ((32, D), BF16), [inputs, gain_row])
    x_m, x_p, x_z, x_2 = (
        send_y(normed_own, 1),
        send_y(normed_own, -1),
        swap_z(normed_own),
        send_y(normed_own, 2),
    )

    onehot = (groups[:, None] == jnp.arange(GROUPS, dtype=jnp.int32)[None, :]).astype(F32)
    stats = jnp.concatenate(
        [
            jnp.sum(onehot, axis=0),
            jnp.sum(onehot * rewards[:, None], axis=0),
            jnp.sum(onehot * (rewards * rewards)[:, None], axis=0),
        ]
    )
    stats = total4(total4(stats, swap_x), swap_h)
    counts, sums, squares = stats[:GROUPS], stats[GROUPS : 2 * GROUPS], stats[2 * GROUPS :]
    safe = jnp.maximum(counts, 1.0)
    mean = sums / safe
    variance = squares / safe - mean * mean
    seg_mean = jnp.sum(onehot * mean[None, :], axis=1)
    seg_var = jnp.sum(onehot * variance[None, :], axis=1)
    seg_adv = (rewards - seg_mean) / jnp.sqrt(seg_var + 1.0)

    lens = lengths[0]
    ends = jnp.cumsum(lens)
    starts = ends - lens
    j = jnp.arange(512, dtype=jnp.int32)
    t_of = (
        ((y_at + (j // 32) % 4) % 4) * 4
        + jnp.bitwise_xor(z_at, (j // 128) % 2) * 2
        + jnp.bitwise_xor(c_at, j // 256)
    )
    rows = t_of * 32 + j % 32
    inside = (rows[:, None] >= starts[None, :]) & (rows[:, None] < ends[None, :])
    segment = jnp.sum(jnp.where(inside, jnp.arange(8, dtype=jnp.int32)[None, :], 0), axis=1)
    position = rows - jnp.sum(jnp.where(inside, starts[None, :], 0), axis=1)
    own_adv = jnp.sum(jnp.where(inside[:32], seg_adv[None, :], 0.0), axis=1)
    grad_own = (upstream.astype(F32) * own_adv[:, None]).astype(BF16)
    half = HD // 2
    inverse = ROPE_BASE ** (-(jnp.arange(half, dtype=F32) * 2.0 / HD))
    angle = position.astype(F32)[:, None] * inverse[None, :]
    cosine = jnp.concatenate([jnp.cos(angle), jnp.cos(angle)], axis=1)
    sine = jnp.concatenate([-jnp.sin(angle), jnp.sin(angle)], axis=1)
    marks = jnp.concatenate(
        [segment[:, None], rows[:, None], jnp.zeros((512, 126), jnp.int32)], axis=1
    ).astype(F32)

    w_kv = jnp.stack([w_key.T, w_value.T])
    w_kv_pair = swap_core(w_kv)
    first = c_at == 0
    w_kv = jnp.stack(
        [jnp.where(first, w_kv, w_kv_pair), jnp.where(first, w_kv_pair, w_kv)], axis=1
    ).reshape(128, D)

    x_m, x_p, x_z, x_2, grad_own, cosine, sine, marks, w_kv = tie(
        x_m, x_p, x_z, x_2, grad_own, cosine, sine, marks, w_kv
    )
    x_zm, x_zp, x_z2 = send_y(x_z, 1), send_y(x_z, -1), swap_z(x_2)
    near = [normed_own, x_p, x_2, x_m, x_z]
    near_pair = [swap_core(block) for block in near]
    *near_pair, grad_own = tie(*near_pair, grad_own)
    g_m, g_p, g_z, g_2 = (
        send_y(grad_own, 1),
        send_y(grad_own, -1),
        swap_z(grad_own),
        send_y(grad_own, 2),
    )
    far = [x_zp, x_z2, x_zm]
    far_pair = [swap_core(block) for block in far]
    x_blocks = [*near, *far, *near_pair, *far_pair]

    query_proj, kv = project(x_blocks, w_query, w_kv)
    kv = call(
        merge_kernel, ((512, 256), BF16), [place, kv, swap_z(kv)], [SMEM, VMEM, VMEM]
    )
    of_core = lambda y, z, c: y // 2 == c
    slots = [kv, send_y(kv, -1, of_core), send_y(kv, 2, of_core), send_y(kv, 1, of_core)]

    g_zm, g_zp, g_z2 = send_y(g_z, 1), send_y(g_z, -1), swap_z(g_2)
    g_near = [grad_own, g_p, g_2, g_m, g_z]
    g_near_pair = [swap_core(block) for block in g_near]
    g_far = [g_zp, g_z2, g_zm]
    g_far_pair = [swap_core(block) for block in g_far]
    g_blocks = [*g_near, *g_far, *g_near_pair, *g_far_pair]

    q_row, k_row = query_gain.reshape(1, HD), key_gain.reshape(1, HD)
    attended, probs = call(
        forward_kernel,
        [((512, 256), BF16), ((2, 512, 512), F32)],
        [place, query_proj, *slots, cosine, sine, marks, q_row, k_row],
        [SMEM] + [VMEM] * 10,
        (pltpu.VMEM((2, 512, 256), BF16),),
    )
    out_state = reduce_first(weight_grad(g_blocks, place, attended))

    dq, d0, d1, d2, d3, head_gains = call(
        backward_kernel,
        [((512, 256), BF16)] * 5 + [((2, HD), F32)],
        [*g_blocks, place, w_output, query_proj, *slots, cosine, sine, q_row, k_row, probs, attended],
        [ANY] * 16 + [SMEM] + [VMEM] * 12,
        (pltpu.VMEM((2, 512, 256), BF16), *ROWS_SCRATCH, pltpu.VMEM((512, 256), BF16)),
    )
    out_state = reduce_second(out_state)
    w_kv_pair = swap_z(w_kv)

    to_core = lambda step: (lambda y, z, c: ((y + step) % 4) // 2 == c)
    dkv = call(
        plane_kernel,
        ((512, 256), BF16),
        [d0, send_y(d1, 1, to_core(1)), send_y(d2, 2, to_core(2)), send_y(d3, 3, to_core(3))],
    )

    back = lambda rows_of: dot(rows_of, w_query, NT).astype(BF16)
    pair = swap_core(back(dq[256:]))
    mine = back(dq[:256])
    first_z, first_p, first_m = call(first_kernel, [((32, D), BF16)] * 3, [mine, pair])
    first_z, first_p, first_m = swap_z(first_z), send_y(first_p, 1), send_y(first_m, -1)

    dkv = call(pair_kernel, ((512, 256), BF16), [dkv, swap_z(dkv)])
    combined, rows_own, rows_pair = call(
        columns_kernel,
        [((512, 320), BF16), ((128, 128), BF16), ((128, 128), BF16)],
        [place, dkv, swap_core(dkv), dq],
        [SMEM] + [VMEM] * 3,
    )
    s_2, s_p, s_m, s_z, own = call(
        second_kernel,
        [((32, D), BF16)] * 4 + [((32, D), F32)],
        [mine, pair, first_z, first_p, first_m, rows_own, rows_pair, w_kv, w_kv_pair],
    )
    s_2, s_p, s_m, s_z = send_y(s_2, 2), send_y(s_p, 1), send_y(s_m, -1), swap_z(s_z)

    state = reduce_first(weight_grad(x_blocks, place, combined))
    out_state = reduce_third(out_state)
    state = reduce_second(state)

    input_grad, norm_sums = call(
        last_kernel,
        [((32, D), BF16), ((1, D), F32)],
        [own, s_2, s_p, s_m, s_z, inputs, gain_row, grad_own],
    )
    gains = jnp.concatenate([norm_sums[0], head_gains[0], head_gains[1]])
    gains = gains + swap_core(gains)
    gains = gains + swap_z(gains)
    gains = total4(total4(total4(gains, swap_y), swap_x), swap_h)

    state = reduce_third(state)
    output_grads = reduce_last(out_state)
    grads = reduce_last(state)
    return (
        input_grad,
        grads[:, :256],
        grads[:, 256:288],
        grads[:, 288:320],
        output_grads,
        gains[:D],
        gains[D : D + HD],
        gains[D + HD :],
    )


def solution(mesh):
    in_specs = (
        P(("dp", "tensor"), None),
        P(("dp", "tensor"), None),
        P(None, "tensor"),
        P(None, "tensor"),
        P(None, "tensor"),
        P("tensor", None),
        P(),
        P(),
        P(),
        P("dp", None),
        P("dp"),
        P("dp"),
    )
    out_specs = (
        P(("dp", "tensor"), None),
        P("dp", "tensor"),
        P("dp", "tensor"),
        P("dp", "tensor"),
        P("dp", "tensor"),
        P(),
        P(),
        P(),
    )
    return jax.shard_map(
        on_device, mesh=mesh, in_specs=in_specs, out_specs=out_specs, check_vma=False
    )
```

```python
import functools

import jax
import jax.numpy as jnp
from jax import lax
from jax.experimental import pallas as pl
from jax.experimental.pallas import tpu as pltpu
from jax.sharding import PartitionSpec as P

KVH = 4
GROUPS = 16
HD = 128
EPS = 1e-06
ROPE_BASE = 1000000.0


F32 = jnp.float32
BF16 = jnp.bfloat16


def t_pairs(move, keep=None):
    pairs = []
    for y in range(4):
        for z in range(2):
            for c in range(2):
                if keep is None or keep(y, z, c):
                    a, b, d = move(y, z, c)
                    pairs.append((y * 4 + z * 2 + c, (a % 4) * 4 + b * 2 + d))
    return pairs


def send_y(value, step, keep=None):
    return lax.ppermute(value, "tensor", t_pairs(lambda y, z, c: (y + step, z, c), keep))


def swap_y(value, bits):
    return lax.ppermute(value, "tensor", t_pairs(lambda y, z, c: (y ^ bits, z, c)))


def swap_z(value):
    return lax.ppermute(value, "tensor", t_pairs(lambda y, z, c: (y, 1 - z, c)))


def swap_core(value):
    return lax.ppermute(value, "tensor", t_pairs(lambda y, z, c: (y, z, 1 - c)))


def send_x(value, step):
    return lax.ppermute(
        value, "dp", [(h * 4 + x, h * 4 + (x + step) % 4) for h in range(4) for x in range(4)]
    )


def send_h(value, step):
    return lax.ppermute(
        value, "dp", [(h * 4 + x, ((h + step) % 4) * 4 + x) for h in range(4) for x in range(4)]
    )


def swap_x(value, bits):
    return lax.ppermute(
        value, "dp", [(h * 4 + x, h * 4 + (x ^ bits)) for h in range(4) for x in range(4)]
    )


def swap_h(value, bits):
    return lax.ppermute(
        value, "dp", [(h * 4 + x, (h ^ bits) * 4 + x) for h in range(4) for x in range(4)]
    )


def total4(value, swap):
    one, two, three = swap(value, 1), swap(value, 2), swap(value, 3)
    return (value + one) + (two + three)


def tie(*values):
    return lax.optimization_barrier(values)


VMEM = pl.BlockSpec(memory_space=pltpu.VMEM)
SMEM = pl.BlockSpec(memory_space=pltpu.SMEM)
ANY = pl.BlockSpec(memory_space=pl.ANY)
NT = (((1,), (1,)), ((), ()))
TN = (((0,), (0,)), ((), ()))
D = 5120


def dot(a, b, dims=(((1,), (0,)), ((), ()))):
    return lax.dot_general(a, b, dims, preferred_element_type=F32)


def call(kernel, out, args, specs=None, scratch=(), limit=48):
    many = isinstance(out, list)
    shapes = [jax.ShapeDtypeStruct(s, t) for s, t in (out if many else [out])]
    result = pl.pallas_call(
        kernel,
        out_shape=shapes,
        in_specs=list(specs) if specs else [VMEM] * len(args),
        out_specs=[VMEM] * len(shapes),
        scratch_shapes=list(scratch),
        compiler_params=pltpu.CompilerParams(vmem_limit_bytes=limit * 2**20),
        cost_estimate=pl.CostEstimate(flops=1, bytes_accessed=1, transcendentals=0),
    )(*args)
    return result if many else result[0]


def load_rows(place, blocks, whole, sems):
    mid, mid_pair, side, side_pair, far, far_pair, last, last_pair, own = blocks
    core = place[2]

    def pick(zero, one):
        return zero + (one - zero) * core

    plan = [
        (own, 0, 0),
        (mid, pick(96, 32), 0),
        (mid_pair, pick(32, 96), 1),
        (side, pick(128, 64), 0),
        (side_pair, pick(64, 128), 1),
        (far, pick(224, 192), 0),
        (far_pair, pick(192, 224), 1),
    ]
    copies = []
    for n, (block, base, turned) in enumerate(plan):
        for half in range(2):
            at = pl.multiple_of(base + 256 * (half ^ turned), 32)
            copies.append(
                pltpu.make_async_copy(
                    block.at[pl.ds(half * 32, 32)], whole.at[pl.ds(at, 32)], sems.at[2 * n + half]
                )
            )
    for half in range(2):
        for n, (block, turned) in enumerate(((last, 0), (last_pair, 1))):
            copy = pltpu.make_async_copy(
                block.at[pl.ds(half * 32, 32)],
                whole.at[pl.ds(160 + 256 * (half ^ turned), 32)],
                sems.at[14 + half],
            )

            @pl.when(core == n)
            def _():
                copy.start()

    for copy in copies:
        copy.start()
    for copy in copies:
        copy.wait()
    for half in range(2):
        pltpu.make_async_copy(
            last.at[pl.ds(half * 32, 32)], whole.at[pl.ds(160, 32)], sems.at[14 + half]
        ).wait()


ROWS_SCRATCH = (pltpu.VMEM((512, D), BF16), pltpu.SemaphoreType.DMA((16,)))
PLACED = [SMEM] + [ANY] * 9


def by_core(zero, one):
    pairs = []
    for y in range(4):
        for z in range(2):
            for c, move in enumerate((zero, one)):
                if move is not None:
                    a, b = move(y, z)
                    pairs.append((y * 4 + z * 2 + c, (a % 4) * 4 + b * 2 + c))
    return pairs


UP = lambda y, z: (y + 1, z)
DOWN = lambda y, z: (y - 1, z)
ACROSS = lambda y, z: (y + 2, z)
OTHER = lambda y, z: (y, 1 - z)


def gather_one(own):
    mid = lax.ppermute(own, "tensor", by_core(UP, DOWN))
    side = lax.ppermute(own, "tensor", by_core(OTHER, ACROSS))
    return mid, side


def gather_two(side):
    far = lax.ppermute(side, "tensor", by_core(UP, OTHER))
    last = lax.ppermute(side, "tensor", by_core(DOWN, None))
    return far, last


def swap_last(value):
    return lax.ppermute(value, "tensor", [(t, t + 1) for t in range(0, 16, 2)])


def project_kernel(place, *refs):
    blocks, (w_q, w_kv, q_out, kv_out, whole, sems) = refs[:9], refs[9:]
    load_rows(place, blocks, whole, sems)
    kv_out[...] = dot(whole[...], w_kv[...], NT).astype(BF16)
    q_out[...] = dot(whole[...], w_q[...]).astype(BF16)


def project(place, blocks, w_q, w_kv):
    return call(
        project_kernel,
        [((512, 256), BF16), ((512, 128), BF16)],
        [place, *blocks, w_q, w_kv],
        PLACED + [VMEM] * 2,
        ROWS_SCRATCH,
    )


def flip_z(value):
    return jnp.concatenate([value[128:256], value[:128], value[384:], value[256:384]], axis=0)


def flip_c(value):
    return jnp.concatenate([value[256:], value[:256]], axis=0)


def turn_y(value, step):
    if step % 4 == 0:
        return value
    parts = []
    for group in range(4):
        for dy in range(4):
            at = group * 128 + ((dy + step) % 4) * 32
            parts.append(value[at : at + 32])
    return jnp.concatenate(parts, axis=0)


def merge_kernel(place, own, pair, out):
    mine = own[...]
    theirs = flip_z(pair[...])
    first = place[1] == 0
    lo = jnp.where(first, mine, theirs)
    hi = jnp.where(first, theirs, mine)
    out[...] = jnp.concatenate([lo[:, :64], hi[:, :64], lo[:, 64:], hi[:, 64:]], axis=1)


def pick_heads(place, slots, heads):
    for n in range(2):
        step = (2 * place[2] + n - place[0] + 4) % 4
        for s in range(4):

            @pl.when(step == s)
            def _():
                heads[n] = turn_y(slots[s][...], -s)


def spin(value, cosine, sine):
    return value * cosine + pltpu.roll(value, 64, 1) * sine


def spin_back(grad, cosine, sine):
    return grad * cosine - pltpu.roll(grad, 64, 1) * sine


def norm(value):
    value = value.astype(F32)
    scale = lax.rsqrt(jnp.mean(value * value, axis=-1, keepdims=True) + EPS)
    return value * scale, scale


def forward_kernel(place, q, s0, s1, s2, s3, cosine, sine, seg, q_gain, k_gain, out, probs, heads):
    pick_heads(place, (s0, s1, s2, s3), heads)
    co, si = cosine[...], sine[...]
    seg_q, row_q = seg[:, 0:1], seg[:, 1:2]
    turned = seg[...].T
    keep = (seg_q == turned[0:1]) & (row_q >= turned[1:2])
    for n in range(2):
        q_unit, _ = norm(q[:, n * HD : n * HD + HD])
        k_unit, _ = norm(heads[n, :, :HD])
        q_rot = spin(q_unit * q_gain[...], co, si).astype(BF16)
        k_rot = spin(k_unit * k_gain[...], co, si).astype(BF16)
        scores = jnp.where(keep, dot(q_rot, k_rot, NT) * HD**-0.5, -1e30)
        weights = jnp.exp(scores - jnp.max(scores, axis=-1, keepdims=True))
        soft = weights / jnp.sum(weights, axis=-1, keepdims=True)
        probs[n] = soft
        out[:, n * HD : n * HD + HD] = dot(soft.astype(BF16), heads[n, :, HD:]).astype(BF16)


def backward_kernel(place, *refs):
    blocks = refs[:9]
    w_out, q, s0, s1, s2, s3, cosine, sine, q_gain, k_gain, probs, attended = refs[9:21]
    dq, d0, d1, d2, d3, gains, heads, whole, sems = refs[21:]
    pick_heads(place, (s0, s1, s2, s3), heads)
    load_rows(place, blocks, whole, sems)
    grad_out = dot(whole[...], w_out[...], NT).astype(BF16)
    co, si = cosine[...], sine[...]
    q_sum = jnp.zeros((1, HD), F32)
    k_sum = jnp.zeros((1, HD), F32)
    d0[...] = jnp.zeros_like(d0)
    for n in range(2):
        cols = slice(n * HD, n * HD + HD)
        q_unit, q_scale = norm(q[:, cols])
        k_unit, k_scale = norm(heads[n, :, :HD])
        q_rot = spin(q_unit * q_gain[...], co, si).astype(BF16)
        k_rot = spin(k_unit * k_gain[...], co, si).astype(BF16)
        grad = grad_out[:, cols]
        delta = jnp.sum(
            grad.astype(F32) * attended[:, cols].astype(F32), axis=-1, keepdims=True
        )
        soft = probs[n]
        score = (soft * (dot(grad, heads[n, :, HD:], NT) - delta) * HD**-0.5).astype(BF16)
        e_q = spin_back(dot(score, k_rot), co, si)
        e_k = spin_back(dot(q_rot.T, score).T, co, si)
        grad_v = dot(grad.T, soft.astype(BF16)).T.astype(BF16)
        q_sum += jnp.sum(e_q * q_unit, axis=0, keepdims=True)
        k_sum += jnp.sum(e_k * k_unit, axis=0, keepdims=True)
        e_q = e_q * q_gain[...]
        e_k = e_k * k_gain[...]
        grad_q = q_scale * (e_q - q_unit * jnp.mean(e_q * q_unit, axis=-1, keepdims=True))
        grad_k = k_scale * (e_k - k_unit * jnp.mean(e_k * k_unit, axis=-1, keepdims=True))
        dq[:, cols] = grad_q.astype(BF16)
        both = jnp.concatenate([grad_k.astype(BF16), grad_v], axis=1)
        step = (2 * place[2] + n - place[0] + 4) % 4
        for s, slot in enumerate((d0, d1, d2, d3)):

            @pl.when(step == s)
            def _():
                slot[...] = both

    gains[...] = jnp.concatenate([q_sum, k_sum], axis=0)


def plane_kernel(a, b, c, d, out):
    total = a[...].astype(F32)
    for step, ref in ((1, b), (2, c), (3, d)):
        total += turn_y(ref[...], step).astype(F32)
    out[...] = total.astype(BF16)


def pair_kernel(a, b, out):
    out[...] = (a[...].astype(F32) + flip_z(b[...]).astype(F32)).astype(BF16)


def columns_kernel(place, a, b, dq, right, rows_own, rows_pair):
    full = (a[...].astype(F32) + flip_c(b[...]).astype(F32)).astype(BF16)
    halves = [jnp.concatenate([full[:128, z * 64 : z * 64 + 64], full[:128, HD + z * 64 : HD + z * 64 + 64]], axis=1) for z in range(2)]
    first = place[1] == 0
    rows_own[...] = jnp.where(first, halves[0], halves[1])
    rows_pair[...] = jnp.where(first, halves[1], halves[0])
    right[:, :256] = dq[...]
    spot = place[1] * 2 + place[2]
    for n in range(4):

        @pl.when(spot == n)
        def _():
            right[:, 256:] = jnp.concatenate(
                [full[:, n * 32 : n * 32 + 32], full[:, HD + n * 32 : HD + n * 32 + 32]], axis=1
            )


def weight_kernel(place, *refs):
    blocks, (right, o0, o1, o2a, o2b, o3, whole, sems) = refs[:9], refs[9:]
    turned = right[...].T
    one = lax.broadcasted_iota(jnp.int32, (256, 256), 0)
    eye = jnp.where(one == lax.broadcasted_iota(jnp.int32, (256, 256), 1), 1.0, 0.0).astype(BF16)
    load_rows(place, blocks, whole, sems)
    for h in range(4):
        side = dot(turned, whole[:, h * 1280 : h * 1280 + 1280]).astype(BF16)
        part = [dot(eye, side[:, i * 256 : i * 256 + 256], NT).astype(BF16) for i in range(5)]
        part = jnp.concatenate(part, axis=0)
        k = (h - place[3] + 4) % 4
        for x in range(4):
            s = (x - place[4] + 4) % 4
            tile = part[x * 320 : x * 320 + 320]
            if right.shape[1] == 256:
                tile = jnp.concatenate([tile[:, :HD], tile[:, HD:]], axis=0)
            else:
                tile = jnp.concatenate(
                    [
                        tile[:, :HD],
                        tile[:, HD : 2 * HD],
                        jnp.concatenate([tile[:160, 2 * HD :], tile[160:, 2 * HD :]], axis=1),
                    ],
                    axis=0,
                )
            for at, out in ((0, o0), (1, o1), (3, o3)):

                @pl.when(s == at)
                def _():
                    out[k] = tile

            @pl.when((s == 2) & (k < 2))
            def _():
                o2a[jnp.minimum(k, 1)] = tile

            @pl.when((s == 2) & (k >= 2))
            def _():
                o2b[jnp.maximum(k - 2, 0)] = tile


def weight_grad(blocks, place, right):
    rows = right.shape[1] * 320 // HD
    four, two = ((4, rows, HD), BF16), ((2, rows, HD), BF16)
    return call(
        weight_kernel,
        [four, four, two, two, four],
        [place, *blocks, right],
        PLACED + [VMEM],
        ROWS_SCRATCH,
    )


def around_kernel(o1, o3, a, b, right, left):
    right[0:2] = (o1[0:2].astype(F32) + a[...].astype(F32)).astype(BF16)
    right[2:4] = o1[2:4]
    left[0:2] = o3[0:2]
    left[2:4] = (o3[2:4].astype(F32) + b[...].astype(F32)).astype(BF16)


def meet_kernel(o0, r, s, p0, p1, p2, p3):
    for k, out in enumerate((p0, p1, p2, p3)):
        out[...] = (o0[k].astype(F32) + r[k].astype(F32) + s[k].astype(F32)).astype(BF16)


def reduce_first(parts):
    o0, o1, o2a, o2b, o3 = parts
    return o0, o1, o3, send_x(o2a, 1), send_x(o2b, -1)


def reduce_around(state):
    o0, o1, o3, a, b = state
    right, left = call(around_kernel, [(o1.shape, BF16)] * 2, [o1, o3, a, b])
    return o0, right, left


def reduce_second(state):
    o0, right, left = state
    return o0, send_x(right, 1), send_x(left, -1)


def reduce_meet(state):
    o0, r, s = state
    return call(meet_kernel, [(o0.shape[1:], BF16)] * 4, [o0, r, s])


def reduce_third(state):
    p0, p1, p2, p3 = state
    return p0, send_h(p1, 1), send_h(p2, 2), send_h(p3, -1)


def reduce_last(state):
    zero, one, two, three = [part.astype(F32) for part in state]
    return (zero + two) + (one + three)


def block_at(dz, dy):
    return pl.ds((dz * 4 + dy) * 32, 32)


def first_kernel(mine, pair, z2, p, m):
    for out, dy in ((z2, 2), (p, 1), (m, 3)):
        at = block_at(1, dy)
        out[...] = (mine[at].astype(F32) + pair[at].astype(F32)).astype(BF16)


def second_kernel(mine, pair, fz, fp, fm, ro, rp, wo, wp, s2, sp, sm, sz, own):
    term = dot(ro[...], wo[...]) + dot(rp[...], wp[...])

    def both(dz, dy):
        at = block_at(dz, dy)
        return mine[at].astype(F32) + pair[at].astype(F32)

    s2[...] = (both(0, 2) + fz[...].astype(F32) + term[64:96]).astype(BF16)
    sp[...] = (both(0, 1) + term[32:64]).astype(BF16)
    sm[...] = (both(0, 3) + term[96:128]).astype(BF16)
    sz[...] = (both(1, 0) + fp[...].astype(F32) + fm[...].astype(F32)).astype(BF16)
    own[...] = both(0, 0) + term[0:32]


def last_kernel(own, s2, sp, sm, sz, x, gain, grad, out, sums):
    total = own[...] + s2[...].astype(F32) + sp[...].astype(F32)
    total += sm[...].astype(F32) + sz[...].astype(F32)
    value = x[...].astype(F32)
    scale = lax.rsqrt(jnp.mean(value * value, axis=-1, keepdims=True) + EPS)
    unit = value * scale
    weighted = total * gain[...]
    inner = weighted - unit * jnp.mean(weighted * unit, axis=-1, keepdims=True)
    out[...] = (scale * inner + grad[0:32].astype(F32)).astype(BF16)
    sums[...] = jnp.sum(total * unit, axis=0, keepdims=True)


def normed_kernel(x, pair, gain, out):
    for n, ref in enumerate((x, pair)):
        unit, _ = norm(ref[...])
        out[n * 32 : n * 32 + 32] = (unit * gain[...]).astype(BF16)


def scaled_kernel(x, pair, advantage, out):
    for n, ref in enumerate((x, pair)):
        factor = advantage[n * 32 : n * 32 + 32, 0:1]
        out[n * 32 : n * 32 + 32] = (ref[...].astype(F32) * factor).astype(BF16)


def on_device(
    inputs,
    upstream,
    w_query,
    w_key,
    w_value,
    w_output,
    norm_gain,
    query_gain,
    key_gain,
    lengths,
    rewards,
    groups,
):
    t_at = lax.axis_index("tensor")
    d_at = lax.axis_index("dp")
    y_at, z_at, c_at = t_at // 4, (t_at // 2) % 2, t_at % 2
    place = jnp.stack([y_at, z_at, c_at, d_at // 4, d_at % 4]).astype(jnp.int32)
    gain_row = norm_gain.reshape(1, D)

    onehot = (groups[:, None] == jnp.arange(GROUPS, dtype=jnp.int32)[None, :]).astype(F32)
    stats = jnp.concatenate(
        [
            jnp.sum(onehot, axis=0),
            jnp.sum(onehot * rewards[:, None], axis=0),
            jnp.sum(onehot * (rewards * rewards)[:, None], axis=0),
        ]
    )
    w_kv_own = w_kv = jnp.stack([w_key.T, w_value.T])
    inputs_pair, w_kv_pair, stats = tie(swap_core(inputs), swap_core(w_kv), total4(stats, swap_x))
    x_own = call(normed_kernel, ((64, D), BF16), [inputs, inputs_pair, gain_row])

    x_own, stats, upstream_here = tie(x_own, stats, upstream)
    x_mid, x_side = gather_one(x_own)
    upstream_pair = swap_core(upstream_here)
    stats = total4(stats, swap_h)
    counts, sums, squares = stats[:GROUPS], stats[GROUPS : 2 * GROUPS], stats[2 * GROUPS :]
    safe = jnp.maximum(counts, 1.0)
    mean = sums / safe
    variance = squares / safe - mean * mean
    seg_mean = jnp.sum(onehot * mean[None, :], axis=1)
    seg_var = jnp.sum(onehot * variance[None, :], axis=1)
    seg_adv = (rewards - seg_mean) / jnp.sqrt(seg_var + 1.0)

    lens = lengths[0]
    ends = jnp.cumsum(lens)
    starts = ends - lens
    j = jnp.arange(512, dtype=jnp.int32)
    t_of = (
        ((y_at + (j // 32) % 4) % 4) * 4
        + jnp.bitwise_xor(z_at, (j // 128) % 2) * 2
        + jnp.bitwise_xor(c_at, j // 256)
    )
    rows = t_of * 32 + j % 32
    inside = (rows[:, None] >= starts[None, :]) & (rows[:, None] < ends[None, :])
    segment = jnp.sum(jnp.where(inside, jnp.arange(8, dtype=jnp.int32)[None, :], 0), axis=1)
    position = rows - jnp.sum(jnp.where(inside, starts[None, :], 0), axis=1)
    near = jnp.concatenate([inside[:32], inside[256:288]], axis=0)
    own_adv = jnp.sum(jnp.where(near, seg_adv[None, :], 0.0), axis=1)
    own_adv = jnp.broadcast_to(own_adv[:, None], (64, HD))
    g_own = call(scaled_kernel, ((64, D), BF16), [upstream, upstream_pair, own_adv])
    half = HD // 2
    inverse = ROPE_BASE ** (-(jnp.arange(half, dtype=F32) * 2.0 / HD))
    angle = position.astype(F32)[:, None] * inverse[None, :]
    cosine = jnp.concatenate([jnp.cos(angle), jnp.cos(angle)], axis=1)
    sine = jnp.concatenate([-jnp.sin(angle), jnp.sin(angle)], axis=1)
    marks = jnp.concatenate(
        [segment[:, None], rows[:, None], jnp.zeros((512, 126), jnp.int32)], axis=1
    ).astype(F32)

    first = c_at == 0
    w_kv = jnp.stack(
        [jnp.where(first, w_kv, w_kv_pair), jnp.where(first, w_kv_pair, w_kv)], axis=1
    ).reshape(128, D)

    x_mid, x_side, g_own, cosine, sine, marks, w_kv = tie(
        x_mid, x_side, g_own, cosine, sine, marks, w_kv
    )
    x_far, x_last = gather_two(x_side)
    g_side = lax.ppermute(g_own, "tensor", by_core(OTHER, ACROSS))
    x_mid_pair, x_side_pair = swap_core(x_mid), swap_core(x_side)
    x_far, x_last, g_side, x_mid_pair, x_side_pair, g_own = tie(
        x_far, x_last, g_side, x_mid_pair, x_side_pair, g_own
    )
    g_mid = lax.ppermute(g_own, "tensor", by_core(UP, DOWN))
    x_blocks = [
        x_mid, x_mid_pair, x_side, x_side_pair, x_far, swap_core(x_far), x_last, swap_last(x_last), x_own
    ]
    query_proj, kv = project(place, x_blocks, w_query, w_kv)
    kv_pair, g_side_pair = swap_z(kv), swap_core(g_side)
    kv = call(merge_kernel, ((512, 256), BF16), [place, kv, kv_pair], [SMEM, VMEM, VMEM])
    kv, g_mid, g_side, g_side_pair = tie(kv, g_mid, g_side, g_side_pair)

    of_core = lambda y, z, c: y // 2 == c
    slots = [kv, send_y(kv, -1, of_core), send_y(kv, 2, of_core), send_y(kv, 1, of_core)]
    g_far, g_last = gather_two(g_side)
    *slots, g_far, g_last, g_mid, w_kv_own = tie(*slots, g_far, g_last, g_mid, w_kv_own)
    w_kv_far = swap_z(w_kv_own)
    g_blocks = [
        g_mid, swap_core(g_mid), g_side, g_side_pair, g_far, swap_core(g_far), g_last, swap_last(g_last), g_own
    ]
    q_row, k_row = query_gain.reshape(1, HD), key_gain.reshape(1, HD)
    attended, probs = call(
        forward_kernel,
        [((512, 256), BF16), ((2, 512, 512), F32)],
        [place, query_proj, *slots, cosine, sine, marks, q_row, k_row],
        [SMEM] + [VMEM] * 10,
        (pltpu.VMEM((2, 512, 256), BF16),),
    )
    parts = weight_grad(g_blocks, place, attended)

    *parts, probs, w_kv_far = tie(*parts, probs, w_kv_far)
    w_kv_pair = swap_core(w_kv_far)
    out_state = reduce_first(parts)
    dq, d0, d1, d2, d3, head_gains = call(
        backward_kernel,
        [((512, 256), BF16)] * 5 + [((2, HD), F32)],
        [place, *g_blocks, w_output, query_proj, *slots, cosine, sine, q_row, k_row, probs, attended],
        PLACED + [VMEM] * 12,
        (pltpu.VMEM((2, 512, 256), BF16), *ROWS_SCRATCH),
    )
    w_kv_pair = jnp.stack(
        [jnp.where(first, w_kv_far, w_kv_pair), jnp.where(first, w_kv_pair, w_kv_far)], axis=1
    ).reshape(128, D)
    out_state = reduce_around(out_state)
    *out_state, dq, d0, d1, d2, d3, w_kv_pair = tie(*out_state, dq, d0, d1, d2, d3, w_kv_pair)

    to_core = lambda step: (lambda y, z, c: ((y + step) % 4) // 2 == c)
    d1, d2, d3 = send_y(d1, 1, to_core(1)), send_y(d2, 2, to_core(2)), send_y(d3, 3, to_core(3))
    out_state = reduce_second(out_state)

    back = lambda rows_of: dot(rows_of, w_query, NT).astype(BF16)
    other, mine = back(dq[256:]), back(dq[:256])
    other, mine, d1, d2, d3 = tie(other, mine, d1, d2, d3)
    pair = swap_core(other)
    dkv = call(plane_kernel, ((512, 256), BF16), [d0, d1, d2, d3])
    dkv_pair = swap_z(dkv)
    pair, dkv, dkv_pair = tie(pair, dkv, dkv_pair)
    first_z, first_p, first_m = call(first_kernel, [((32, D), BF16)] * 3, [mine, pair])
    dkv = call(pair_kernel, ((512, 256), BF16), [dkv, dkv_pair])
    dkv_pair, first_z, first_p, first_m = (
        swap_core(dkv),
        swap_z(first_z),
        send_y(first_p, 1),
        send_y(first_m, -1),
    )
    dkv_pair, first_z, first_p, first_m, *out_state = tie(
        dkv_pair, first_z, first_p, first_m, *out_state
    )
    out_state = reduce_meet(out_state)
    combined, rows_own, rows_pair = call(
        columns_kernel,
        [((512, 320), BF16), ((128, 128), BF16), ((128, 128), BF16)],
        [place, dkv, dkv_pair, dq],
        [SMEM] + [VMEM] * 3,
    )
    s_2, s_p, s_m, s_z, own = call(
        second_kernel,
        [((32, D), BF16)] * 4 + [((32, D), F32)],
        [mine, pair, first_z, first_p, first_m, rows_own, rows_pair, w_kv, w_kv_pair],
    )
    s_2, s_p, s_m, s_z, own, combined = tie(s_2, s_p, s_m, s_z, own, combined)
    s_2, s_p, s_m, s_z = send_y(s_2, 2), send_y(s_p, 1), send_y(s_m, -1), swap_z(s_z)
    parts = weight_grad(x_blocks, place, combined)
    *parts, s_2, s_p, s_m, s_z = tie(*parts, s_2, s_p, s_m, s_z)

    state = reduce_first(parts)
    out_state = reduce_third(out_state)
    input_grad, norm_sums = call(
        last_kernel,
        [((32, D), BF16), ((1, D), F32)],
        [own, s_2, s_p, s_m, s_z, inputs, gain_row, g_own],
    )
    *state, norm_sums, o0, o1, o2, o3 = tie(*state, norm_sums, *out_state)
    out_state = o0, o1, o2, o3
    state = reduce_second(reduce_around(state))
    gains = jnp.concatenate([norm_sums[0], head_gains[0], head_gains[1]])
    gains = gains + swap_core(gains)
    gains = gains + swap_z(gains)
    gains = total4(total4(gains, swap_y), swap_x)
    *state, gains = tie(*reduce_meet(state), gains)
    state = reduce_third(state)
    gains = gains + swap_h(gains, 1)
    gains = gains + swap_h(gains, 2)

    out_grads = reduce_last(out_state)
    grads = reduce_last(state)
    last = grads[640:]
    return (
        input_grad,
        jnp.concatenate([grads[:320], grads[320:640]], axis=1),
        jnp.concatenate([last[:, :32], last[:, 64:96]], axis=0),
        jnp.concatenate([last[:, 32:64], last[:, 96:]], axis=0),
        jnp.concatenate([out_grads[:320], out_grads[320:]], axis=1),
        gains[:D],
        gains[D : D + HD],
        gains[D + HD :],
    )


def solution(mesh):
    in_specs = (
        P(("dp", "tensor"), None),
        P(("dp", "tensor"), None),
        P(None, "tensor"),
        P(None, "tensor"),
        P(None, "tensor"),
        P("tensor", None),
        P(),
        P(),
        P(),
        P("dp", None),
        P("dp"),
        P("dp"),
    )
    out_specs = (
        P(("dp", "tensor"), None),
        P("dp", "tensor"),
        P("dp", "tensor"),
        P("dp", "tensor"),
        P("dp", "tensor"),
        P(),
        P(),
        P(),
    )
    return jax.shard_map(
        on_device, mesh=mesh, in_specs=in_specs, out_specs=out_specs, check_vma=False
    )
```

```python
import functools

import jax
import jax.numpy as jnp
from jax import lax
from jax.experimental import pallas as pl
from jax.experimental.pallas import tpu as pltpu
from jax.sharding import PartitionSpec as P

KVH = 4
GROUPS = 16
HD = 128
EPS = 1e-06
ROPE_BASE = 1000000.0


F32 = jnp.float32
BF16 = jnp.bfloat16


def t_pairs(move, keep=None):
    pairs = []
    for y in range(4):
        for z in range(2):
            for c in range(2):
                if keep is None or keep(y, z, c):
                    a, b, d = move(y, z, c)
                    pairs.append((y * 4 + z * 2 + c, (a % 4) * 4 + b * 2 + d))
    return pairs


def send_y(value, step, keep=None):
    return lax.ppermute(value, "tensor", t_pairs(lambda y, z, c: (y + step, z, c), keep))


def swap_y(value, bits):
    return lax.ppermute(value, "tensor", t_pairs(lambda y, z, c: (y ^ bits, z, c)))


def swap_z(value):
    return lax.ppermute(value, "tensor", t_pairs(lambda y, z, c: (y, 1 - z, c)))


def swap_core(value):
    return lax.ppermute(value, "tensor", t_pairs(lambda y, z, c: (y, z, 1 - c)))


def send_x(value, step):
    return lax.ppermute(
        value, "dp", [(h * 4 + x, h * 4 + (x + step) % 4) for h in range(4) for x in range(4)]
    )


def send_h(value, step):
    return lax.ppermute(
        value, "dp", [(h * 4 + x, ((h + step) % 4) * 4 + x) for h in range(4) for x in range(4)]
    )


def swap_x(value, bits):
    return lax.ppermute(
        value, "dp", [(h * 4 + x, h * 4 + (x ^ bits)) for h in range(4) for x in range(4)]
    )


def swap_h(value, bits):
    return lax.ppermute(
        value, "dp", [(h * 4 + x, (h ^ bits) * 4 + x) for h in range(4) for x in range(4)]
    )


def total4(value, swap):
    one, two, three = swap(value, 1), swap(value, 2), swap(value, 3)
    return (value + one) + (two + three)


def tie(*values):
    return lax.optimization_barrier(values)


VMEM = pl.BlockSpec(memory_space=pltpu.VMEM)
SMEM = pl.BlockSpec(memory_space=pltpu.SMEM)
ANY = pl.BlockSpec(memory_space=pl.ANY)
NT = (((1,), (1,)), ((), ()))
TN = (((0,), (0,)), ((), ()))
D = 5120


def dot(a, b, dims=(((1,), (0,)), ((), ()))):
    return lax.dot_general(a, b, dims, preferred_element_type=F32)


def call(kernel, out, args, specs=None, scratch=(), limit=48):
    many = isinstance(out, list)
    shapes = [jax.ShapeDtypeStruct(s, t) for s, t in (out if many else [out])]
    result = pl.pallas_call(
        kernel,
        out_shape=shapes,
        in_specs=list(specs) if specs else [VMEM] * len(args),
        out_specs=[VMEM] * len(shapes),
        scratch_shapes=list(scratch),
        compiler_params=pltpu.CompilerParams(vmem_limit_bytes=limit * 2**20),
        cost_estimate=pl.CostEstimate(flops=1, bytes_accessed=1, transcendentals=0),
    )(*args)
    return result if many else result[0]


def load_rows(place, blocks, whole, sems):
    mid, mid_pair, side, side_pair, far, far_pair, last, last_pair, own = blocks
    core = place[2]

    def pick(zero, one):
        return zero + (one - zero) * core

    plan = [
        (own, 0, 0),
        (mid, pick(96, 32), 0),
        (mid_pair, pick(32, 96), 1),
        (side, pick(128, 64), 0),
        (side_pair, pick(64, 128), 1),
        (far, pick(224, 192), 0),
        (far_pair, pick(192, 224), 1),
    ]
    copies = []
    for n, (block, base, turned) in enumerate(plan):
        for half in range(2):
            at = pl.multiple_of(base + 256 * (half ^ turned), 32)
            copies.append(
                pltpu.make_async_copy(
                    block.at[pl.ds(half * 32, 32)], whole.at[pl.ds(at, 32)], sems.at[2 * n + half]
                )
            )
    for half in range(2):
        for n, (block, turned) in enumerate(((last, 0), (last_pair, 1))):
            copy = pltpu.make_async_copy(
                block.at[pl.ds(half * 32, 32)],
                whole.at[pl.ds(160 + 256 * (half ^ turned), 32)],
                sems.at[14 + half],
            )

            @pl.when(core == n)
            def _():
                copy.start()

    for copy in copies:
        copy.start()
    for copy in copies:
        copy.wait()
    for half in range(2):
        pltpu.make_async_copy(
            last.at[pl.ds(half * 32, 32)], whole.at[pl.ds(160, 32)], sems.at[14 + half]
        ).wait()


def load_plane(place, parts, w_kv, sems):
    copies = []
    for n, part in enumerate(parts):
        z, core = place[1] ^ (n // 2), place[2] ^ (n % 2)
        for kind in range(2):
            at = pl.multiple_of(kind * HD + z * 64 + core * 32, 32)
            copies.append(
                pltpu.make_async_copy(part.at[kind], w_kv.at[pl.ds(at, 32)], sems.at[2 * n + kind])
            )
    for copy in copies:
        copy.start()
    return copies


PLANE_SCRATCH = (pltpu.VMEM((256, D), BF16), pltpu.SemaphoreType.DMA((8,)))
ROWS_SCRATCH = (pltpu.VMEM((512, D), BF16), pltpu.SemaphoreType.DMA((16,)))
PLACED = [SMEM] + [ANY] * 9


def by_core(zero, one):
    pairs = []
    for y in range(4):
        for z in range(2):
            for c, move in enumerate((zero, one)):
                if move is not None:
                    a, b = move(y, z)
                    pairs.append((y * 4 + z * 2 + c, (a % 4) * 4 + b * 2 + c))
    return pairs


UP = lambda y, z: (y + 1, z)
DOWN = lambda y, z: (y - 1, z)
ACROSS = lambda y, z: (y + 2, z)
OTHER = lambda y, z: (y, 1 - z)


def gather_one(own):
    mid = lax.ppermute(own, "tensor", by_core(UP, DOWN))
    side = lax.ppermute(own, "tensor", by_core(OTHER, ACROSS))
    return mid, side


def gather_two(side):
    far = lax.ppermute(side, "tensor", by_core(UP, OTHER))
    last = lax.ppermute(side, "tensor", by_core(DOWN, None))
    return far, last


def kv_pairs(beside, back):
    pairs = []
    for y in range(4):
        for z in range(2):
            e = y // 2
            ways = [(y + 1, e), (y - 1, 1 - e)] if beside else [(y + 2, e)]
            for to, via in ways:
                here, there = y * 4 + z * 2 + via, (to % 4) * 4 + z * 2 + e
                pairs.append((there, here) if back else (here, there))
    return pairs


KV_BESIDE, KV_ACROSS = kv_pairs(True, False), kv_pairs(False, False)
DKV_BESIDE, DKV_ACROSS = kv_pairs(True, True), kv_pairs(False, True)


def swap_last(value):
    return lax.ppermute(value, "tensor", [(t, t + 1) for t in range(0, 16, 2)])


def project_kernel(place, *refs):
    blocks, planes, (w_q, q_out, kv_out, whole, sems, w_kv, w_sems) = refs[:9], refs[9:13], refs[13:]
    copies = load_plane(place, planes, w_kv, w_sems)
    load_rows(place, blocks, whole, sems)
    q_out[...] = dot(whole[...], w_q[...]).astype(BF16)
    for copy in copies:
        copy.wait()
    kv_out[...] = dot(whole[...], w_kv[...], NT).astype(BF16)


def project(place, blocks, planes, w_q):
    return call(
        project_kernel,
        [((512, 256), BF16), ((512, 256), BF16)],
        [place, *blocks, *planes, w_q],
        PLACED + [ANY] * 4 + [VMEM],
        (*ROWS_SCRATCH, *PLANE_SCRATCH),
    )


def flip_z(value):
    return jnp.concatenate([value[128:256], value[:128], value[384:], value[256:384]], axis=0)


def flip_c(value):
    return jnp.concatenate([value[256:], value[:256]], axis=0)


def turn_y(value, step):
    if step % 4 == 0:
        return value
    parts = []
    for group in range(4):
        for dy in range(4):
            at = group * 128 + ((dy + step) % 4) * 32
            parts.append(value[at : at + 32])
    return jnp.concatenate(parts, axis=0)


def pick_heads(place, slots, heads):
    own, side, across = slots
    for n in range(2):
        step = (2 * place[2] + n - place[0] + 4) % 4
        for s, slot in enumerate((own, side, across, side)):

            @pl.when(step == s)
            def _():
                value = flip_c(slot[...]) if s == 1 else slot[...]
                heads[n] = turn_y(value, -s)


def spin(value, cosine, sine):
    return value * cosine + pltpu.roll(value, 64, 1) * sine


def spin_back(grad, cosine, sine):
    return grad * cosine - pltpu.roll(grad, 64, 1) * sine


def norm(value):
    value = value.astype(F32)
    scale = lax.rsqrt(jnp.mean(value * value, axis=-1, keepdims=True) + EPS)
    return value * scale, scale


def forward_kernel(place, q, s0, s1, s2, cosine, sine, seg, q_gain, k_gain, out, probs, heads):
    pick_heads(place, (s0, s1, s2), heads)
    co, si = cosine[...], sine[...]
    seg_q, row_q = seg[:, 0:1], seg[:, 1:2]
    turned = seg[...].T
    keep = (seg_q == turned[0:1]) & (row_q >= turned[1:2])
    for n in range(2):
        q_unit, _ = norm(q[:, n * HD : n * HD + HD])
        k_unit, _ = norm(heads[n, :, :HD])
        q_rot = spin(q_unit * q_gain[...], co, si).astype(BF16)
        k_rot = spin(k_unit * k_gain[...], co, si).astype(BF16)
        scores = jnp.where(keep, dot(q_rot, k_rot, NT) * HD**-0.5, -1e30)
        weights = jnp.exp(scores - jnp.max(scores, axis=-1, keepdims=True))
        soft = weights / jnp.sum(weights, axis=-1, keepdims=True)
        probs[n] = soft
        out[:, n * HD : n * HD + HD] = dot(soft.astype(BF16), heads[n, :, HD:]).astype(BF16)


SUMS = (
    ((1, 1), (3, 1), (0, 1), (3, 0)),
    ((2, 1), (2, 0), (1, 0)),
)


def rows_of(core, turned):
    slices = []
    for dy, dz in SUMS[core]:
        for dc in range(2):
            slices.append(slice((dc ^ turned) * 256 + dz * 128 + dy * 32, (dc ^ turned) * 256 + dz * 128 + dy * 32 + 32))
    slices += [slice(turned * 256, turned * 256 + 32)] * (9 - len(slices))
    return slices


def backward_kernel(place, *refs):
    blocks = refs[:9]
    w_out, q, s0, s1, s2, cosine, sine, q_gain, k_gain, probs, attended = refs[9:20]
    dq, keep, send, d0, d1, d2, gains, heads, whole, sems = refs[20:]
    pick_heads(place, (s0, s1, s2), heads)
    load_rows(place, blocks, whole, sems)
    grad_out = dot(whole[...], w_out[...], NT).astype(BF16)
    co, si = cosine[...], sine[...]
    q_sum = jnp.zeros((1, HD), F32)
    k_sum = jnp.zeros((1, HD), F32)
    d0[...] = jnp.zeros_like(d0)
    for n in range(2):
        cols = slice(n * HD, n * HD + HD)
        q_unit, q_scale = norm(q[:, cols])
        k_unit, k_scale = norm(heads[n, :, :HD])
        q_rot = spin(q_unit * q_gain[...], co, si).astype(BF16)
        k_rot = spin(k_unit * k_gain[...], co, si).astype(BF16)
        grad = grad_out[:, cols]
        delta = jnp.sum(
            grad.astype(F32) * attended[:, cols].astype(F32), axis=-1, keepdims=True
        )
        soft = probs[n]
        score = (soft * (dot(grad, heads[n, :, HD:], NT) - delta) * HD**-0.5).astype(BF16)
        e_q = spin_back(dot(score, k_rot), co, si)
        e_k = spin_back(dot(q_rot.T, score).T, co, si)
        grad_v = dot(grad.T, soft.astype(BF16)).T.astype(BF16)
        q_sum += jnp.sum(e_q * q_unit, axis=0, keepdims=True)
        k_sum += jnp.sum(e_k * k_unit, axis=0, keepdims=True)
        e_q = e_q * q_gain[...]
        e_k = e_k * k_gain[...]
        grad_q = q_scale * (e_q - q_unit * jnp.mean(e_q * q_unit, axis=-1, keepdims=True))
        grad_k = k_scale * (e_k - k_unit * jnp.mean(e_k * k_unit, axis=-1, keepdims=True))
        dq[:, cols] = grad_q.astype(BF16)
        both = jnp.concatenate([grad_k.astype(BF16), grad_v], axis=1)
        step = (2 * place[2] + n - place[0] + 4) % 4
        for s, slot in enumerate((d0, d1, d2, d1)):

            @pl.when(step == s)
            def _():
                slot[...] = both

    gains[...] = jnp.concatenate([q_sum, k_sum], axis=0)
    for core in range(2):

        @pl.when(place[2] == core)
        def _():
            keep[...] = jnp.concatenate([dq[at] for at in rows_of(core, 0)], axis=0)
            send[...] = jnp.concatenate([dq[at] for at in rows_of(1 - core, 1)], axis=0)


def plane_kernel(place, own, side, across, out):
    total = own[...].astype(F32) + turn_y(across[...], 2).astype(F32)
    home = place[0] // 2 == place[2]

    @pl.when(home)
    def _():
        out[...] = (total + turn_y(side[...], 3).astype(F32)).astype(BF16)

    @pl.when(jnp.logical_not(home))
    def _():
        out[...] = (total + turn_y(flip_c(side[...]), 1).astype(F32)).astype(BF16)


def pair_kernel(a, b, out):
    out[...] = (a[...].astype(F32) + flip_z(b[...]).astype(F32)).astype(BF16)


def columns_kernel(place, a, b, dq, right, rows_here):
    full = (a[...].astype(F32) + flip_c(b[...]).astype(F32)).astype(BF16)
    for core in range(2):

        @pl.when(place[2] == core)
        def _():
            some = [full[at] for at in rows_of(core, 0)]
            some = some[4:9] if core == 0 else some[2:7]
            rows_here[...] = jnp.concatenate(some, axis=0)

    right[:, :256] = dq[...]
    spot = place[1] * 2 + place[2]
    for n in range(4):

        @pl.when(spot == n)
        def _():
            right[:, 256:] = jnp.concatenate(
                [full[:, n * 32 : n * 32 + 32], full[:, HD + n * 32 : HD + n * 32 + 32]], axis=1
            )


def weight_kernel(place, *refs):
    blocks, (right, o0, o1, o2a, o2b, o3, whole, sems) = refs[:9], refs[9:]
    turned = right[...].T
    one = lax.broadcasted_iota(jnp.int32, (256, 256), 0)
    eye = jnp.where(one == lax.broadcasted_iota(jnp.int32, (256, 256), 1), 1.0, 0.0).astype(BF16)
    load_rows(place, blocks, whole, sems)
    for h in range(4):
        side = dot(turned, whole[:, h * 1280 : h * 1280 + 1280]).astype(BF16)
        part = [dot(eye, side[:, i * 256 : i * 256 + 256], NT).astype(BF16) for i in range(5)]
        part = jnp.concatenate(part, axis=0)
        k = (h - place[3] + 4) % 4
        for x in range(4):
            s = (x - place[4] + 4) % 4
            tile = part[x * 320 : x * 320 + 320]
            if right.shape[1] == 256:
                tile = jnp.concatenate([tile[:, :HD], tile[:, HD:]], axis=0)
            else:
                tile = jnp.concatenate(
                    [
                        tile[:, :HD],
                        tile[:, HD : 2 * HD],
                        jnp.concatenate([tile[:160, 2 * HD :], tile[160:, 2 * HD :]], axis=1),
                    ],
                    axis=0,
                )
            for at, out in ((0, o0), (1, o1), (3, o3)):

                @pl.when(s == at)
                def _():
                    out[k] = tile

            @pl.when((s == 2) & (k < 2))
            def _():
                o2a[jnp.minimum(k, 1)] = tile

            @pl.when((s == 2) & (k >= 2))
            def _():
                o2b[jnp.maximum(k - 2, 0)] = tile


def weight_grad(blocks, place, right):
    rows = right.shape[1] * 320 // HD
    four, two = ((4, rows, HD), BF16), ((2, rows, HD), BF16)
    return call(
        weight_kernel,
        [four, four, two, two, four],
        [place, *blocks, right],
        PLACED + [VMEM],
        ROWS_SCRATCH,
    )


def around_kernel(o1, o3, a, b, right, left):
    right[0:2] = (o1[0:2].astype(F32) + a[...].astype(F32)).astype(BF16)
    right[2:4] = o1[2:4]
    left[0:2] = o3[0:2]
    left[2:4] = (o3[2:4].astype(F32) + b[...].astype(F32)).astype(BF16)


def meet_kernel(o0, r, s, p0, p1, p2, p3):
    for k, out in enumerate((p0, p1, p2, p3)):
        out[...] = (o0[k].astype(F32) + r[k].astype(F32) + s[k].astype(F32)).astype(BF16)


def reduce_first(parts):
    o0, o1, o2a, o2b, o3 = parts
    return o0, o1, o3, send_x(o2a, 1), send_x(o2b, -1)


def reduce_around(state):
    o0, o1, o3, a, b = state
    right, left = call(around_kernel, [(o1.shape, BF16)] * 2, [o1, o3, a, b])
    return o0, right, left


def reduce_second(state):
    o0, right, left = state
    return o0, send_x(right, 1), send_x(left, -1)


def reduce_meet(state):
    o0, r, s = state
    return call(meet_kernel, [(o0.shape[1:], BF16)] * 4, [o0, r, s])


def reduce_third(state):
    p0, p1, p2, p3 = state
    return p0, send_h(p1, 1), send_h(p2, 2), send_h(p3, -1)


def reduce_last(state):
    zero, one, two, three = [part.astype(F32) for part in state]
    return (zero + two) + (one + three)


def first_kernel(mine, pair, one, two):
    one[...] = (mine[0:64].astype(F32) + pair[0:64].astype(F32)).astype(BF16)
    two[...] = (mine[64:128].astype(F32) + pair[64:128].astype(F32)).astype(BF16)


def second_kernel(place, *refs):
    planes, (mine, pair, one, two, here, three, four, own, w_kv, sems) = refs[:4], refs[4:]
    copies = load_plane(place, planes, w_kv, sems)
    for copy in copies:
        copy.wait()
    term = dot(here[...], w_kv[...])

    def both(at, size=64):
        return mine[at : at + size].astype(F32) + pair[at : at + size].astype(F32)

    @pl.when(place[2] == 0)
    def _():
        three[...] = (both(128) + one[...].astype(F32) + two[...].astype(F32)).astype(BF16)
        four[...] = (both(192) + term[64:128]).astype(BF16)
        own[...] = both(256, 32) + term[128:160]

    @pl.when(place[2] == 1)
    def _():
        three[...] = (both(64) + one[...].astype(F32) + term[0:64]).astype(BF16)
        four[...] = (both(128) + term[64:128]).astype(BF16)
        own[...] = both(192, 32) + term[128:160]


def third_kernel(three, four, out):
    out[...] = (three[32:64].astype(F32) + four[32:64].astype(F32)).astype(BF16)


def last_kernel(own, three, four, pair, x, gain, grad, out, sums):
    total = own[...] + three[0:32].astype(F32) + four[0:32].astype(F32) + pair[...].astype(F32)
    value = x[...].astype(F32)
    scale = lax.rsqrt(jnp.mean(value * value, axis=-1, keepdims=True) + EPS)
    unit = value * scale
    weighted = total * gain[...]
    inner = weighted - unit * jnp.mean(weighted * unit, axis=-1, keepdims=True)
    out[...] = (scale * inner + grad[0:32].astype(F32)).astype(BF16)
    sums[...] = jnp.sum(total * unit, axis=0, keepdims=True)


def normed_kernel(x, pair, gain, out):
    for n, ref in enumerate((x, pair)):
        unit, _ = norm(ref[...])
        out[n * 32 : n * 32 + 32] = (unit * gain[...]).astype(BF16)


def scaled_kernel(x, pair, advantage, out):
    for n, ref in enumerate((x, pair)):
        factor = advantage[n * 32 : n * 32 + 32, 0:1]
        out[n * 32 : n * 32 + 32] = (ref[...].astype(F32) * factor).astype(BF16)


def on_device(
    inputs,
    upstream,
    w_query,
    w_key,
    w_value,
    w_output,
    norm_gain,
    query_gain,
    key_gain,
    lengths,
    rewards,
    groups,
):
    t_at = lax.axis_index("tensor")
    d_at = lax.axis_index("dp")
    y_at, z_at, c_at = t_at // 4, (t_at // 2) % 2, t_at % 2
    place = jnp.stack([y_at, z_at, c_at, d_at // 4, d_at % 4]).astype(jnp.int32)
    gain_row = norm_gain.reshape(1, D)

    inputs_pair, rewards, groups, lengths, w_key, w_value, place, upstream = tie(
        swap_core(inputs), rewards, groups, lengths, w_key, w_value, place, upstream
    )
    x_own = call(normed_kernel, ((64, D), BF16), [inputs, inputs_pair, gain_row])

    x_own, rewards, groups, lengths, w_key, w_value, place, upstream = tie(
        x_own, rewards, groups, lengths, w_key, w_value, place, upstream
    )
    x_mid, x_side = gather_one(x_own)
    onehot = (groups[:, None] == jnp.arange(GROUPS, dtype=jnp.int32)[None, :]).astype(F32)
    stats = jnp.concatenate(
        [
            jnp.sum(onehot, axis=0),
            jnp.sum(onehot * rewards[:, None], axis=0),
            jnp.sum(onehot * (rewards * rewards)[:, None], axis=0),
        ]
    )
    stats = stats + swap_x(stats, 1)
    stats = stats + swap_x(stats, 2)
    lens = lengths[0]
    w_own = jnp.stack([w_key.T, w_value.T])
    w_far = swap_z(w_own)
    x_mid, x_side, stats, upstream, w_own = tie(x_mid, x_side, stats, upstream, w_own)
    x_far, x_last = gather_two(x_side)
    x_mid_pair, x_side_pair = swap_core(x_mid), swap_core(x_side)
    upstream_pair, w_pair = swap_core(upstream), swap_core(w_own)
    stats = stats + swap_h(stats, 1)
    stats = stats + swap_h(stats, 2)
    counts, sums, squares = stats[:GROUPS], stats[GROUPS : 2 * GROUPS], stats[2 * GROUPS :]
    safe = jnp.maximum(counts, 1.0)
    mean = sums / safe
    variance = squares / safe - mean * mean
    seg_mean = jnp.sum(onehot * mean[None, :], axis=1)
    seg_var = jnp.sum(onehot * variance[None, :], axis=1)
    seg_adv = (rewards - seg_mean) / jnp.sqrt(seg_var + 1.0)

    ends = jnp.cumsum(lens)
    starts = ends - lens
    j = jnp.arange(512, dtype=jnp.int32)
    t_of = (
        ((place[0] + (j // 32) % 4) % 4) * 4
        + jnp.bitwise_xor(place[1], (j // 128) % 2) * 2
        + jnp.bitwise_xor(place[2], j // 256)
    )
    rows = t_of * 32 + j % 32
    inside = (rows[:, None] >= starts[None, :]) & (rows[:, None] < ends[None, :])
    segment = jnp.sum(jnp.where(inside, jnp.arange(8, dtype=jnp.int32)[None, :], 0), axis=1)
    position = rows - jnp.sum(jnp.where(inside, starts[None, :], 0), axis=1)
    near = jnp.concatenate([inside[:32], inside[256:288]], axis=0)
    own_adv = jnp.sum(jnp.where(near, seg_adv[None, :], 0.0), axis=1)
    own_adv = jnp.broadcast_to(own_adv[:, None], (64, HD))
    g_own = call(scaled_kernel, ((64, D), BF16), [upstream, upstream_pair, own_adv])
    half = HD // 2
    inverse = ROPE_BASE ** (-(jnp.arange(half, dtype=F32) * 2.0 / HD))
    angle = position.astype(F32)[:, None] * inverse[None, :]
    cosine = jnp.concatenate([jnp.cos(angle), jnp.cos(angle)], axis=1)
    sine = jnp.concatenate([-jnp.sin(angle), jnp.sin(angle)], axis=1)
    marks = jnp.concatenate(
        [segment[:, None], rows[:, None], jnp.zeros((512, 126), jnp.int32)], axis=1
    ).astype(F32)

    x_far, x_last, x_mid_pair, x_side_pair, g_own, w_far, w_pair, cosine, sine, marks = tie(
        x_far, x_last, x_mid_pair, x_side_pair, g_own, w_far, w_pair, cosine, sine, marks
    )
    g_mid, g_side = gather_one(g_own)
    planes = [w_own, w_pair, w_far, swap_core(w_far)]
    x_blocks = [
        x_mid, x_mid_pair, x_side, x_side_pair, x_far, swap_core(x_far), x_last, swap_last(x_last), x_own
    ]
    query_proj, kv = project(place, x_blocks, planes, w_query)
    query_proj, kv, g_mid, g_side = tie(query_proj, kv, g_mid, g_side)

    g_far, g_last = gather_two(g_side)
    slots = [kv, lax.ppermute(kv, "tensor", KV_BESIDE), lax.ppermute(kv, "tensor", KV_ACROSS)]
    *slots, g_mid, g_side = tie(*slots, g_mid, g_side)
    g_mid_pair, g_side_pair = swap_core(g_mid), swap_core(g_side)
    q_row, k_row = query_gain.reshape(1, HD), key_gain.reshape(1, HD)
    attended, probs = call(
        forward_kernel,
        [((512, 256), BF16), ((2, 512, 512), F32)],
        [place, query_proj, *slots, cosine, sine, marks, q_row, k_row],
        [SMEM] + [VMEM] * 9,
        (pltpu.VMEM((2, 512, 256), BF16),),
    )
    g_far, g_last, g_mid_pair, g_side_pair, attended, probs = tie(
        g_far, g_last, g_mid_pair, g_side_pair, attended, probs
    )
    g_blocks = [
        g_mid, g_mid_pair, g_side, g_side_pair, g_far, swap_core(g_far), g_last, swap_last(g_last), g_own
    ]
    dq, keep, send, d0, d1, d2, head_gains = call(
        backward_kernel,
        [((512, 256), BF16), ((288, 256), BF16), ((288, 256), BF16)]
        + [((512, 256), BF16)] * 3
        + [((2, HD), F32)],
        [place, *g_blocks, w_output, query_proj, *slots, cosine, sine, q_row, k_row, probs, attended],
        PLACED + [VMEM] * 11,
        (pltpu.VMEM((2, 512, 256), BF16), *ROWS_SCRATCH),
    )
    dq, keep, send, d0, d1, d2, attended = tie(dq, keep, send, d0, d1, d2, attended)
    d1, d2 = lax.ppermute(d1, "tensor", DKV_BESIDE), lax.ppermute(d2, "tensor", DKV_ACROSS)
    parts = weight_grad(g_blocks, place, attended)
    keep, send, d0, d1, d2, *parts = tie(keep, send, d0, d1, d2, *parts)

    dkv = call(plane_kernel, ((512, 256), BF16), [place, d0, d1, d2], [SMEM] + [VMEM] * 3)
    dkv, keep, send, *parts = tie(dkv, keep, send, *parts)
    dkv_pair = swap_z(dkv)
    out_state = reduce_first(parts)
    back = lambda rows: dot(rows, w_query, NT).astype(BF16)
    pair = swap_core(back(send))
    mine = back(keep)
    pair, mine, dkv, dkv_pair, *out_state = tie(pair, mine, dkv, dkv_pair, *out_state)
    dkv = call(pair_kernel, ((512, 256), BF16), [dkv, dkv_pair])
    one, two = call(first_kernel, [((64, D), BF16)] * 2, [mine, pair])
    dkv, one, two, *out_state = tie(dkv, one, two, *out_state)
    dkv_pair = swap_core(dkv)
    one = lax.ppermute(one, "tensor", by_core(UP, OTHER))
    two = lax.ppermute(two, "tensor", by_core(DOWN, None))
    out_state = reduce_second(reduce_around(out_state))
    dkv_pair, one, two = tie(dkv_pair, one, two)
    combined, rows_here = call(
        columns_kernel,
        [((512, 320), BF16), ((160, 256), BF16)],
        [place, dkv, dkv_pair, dq],
        [SMEM] + [VMEM] * 3,
    )
    three, four, own = call(
        second_kernel,
        [((64, D), BF16), ((64, D), BF16), ((32, D), F32)],
        [place, *planes, mine, pair, one, two, rows_here],
        [SMEM] + [ANY] * 4 + [VMEM] * 5,
        PLANE_SCRATCH,
    )
    three, four, own, combined, *out_state = tie(three, four, own, combined, *out_state)
    three = lax.ppermute(three, "tensor", by_core(OTHER, ACROSS))
    four = lax.ppermute(four, "tensor", by_core(DOWN, UP))
    out_state = reduce_third(reduce_meet(out_state))
    parts = weight_grad(x_blocks, place, combined)
    *parts, three, four, o0, o1, o2, o3 = tie(*parts, three, four, *out_state)
    out_state = o0, o1, o2, o3

    state = reduce_first(parts)
    pair = swap_core(call(third_kernel, ((32, D), BF16), [three, four]))
    input_grad, norm_sums = call(
        last_kernel,
        [((32, D), BF16), ((1, D), F32)],
        [own, three, four, pair, inputs, gain_row, g_own],
    )
    gains = jnp.concatenate([norm_sums[0], head_gains[0], head_gains[1]])
    gains = gains + swap_core(gains)
    gains = gains + swap_z(gains)
    gains = gains + swap_x(gains, 1)
    *state, gains = tie(*state, gains)
    state = reduce_around(state)
    *state, gains = tie(*state, gains)
    state = reduce_second(state)
    for swap in (swap_y, swap_h):
        gains = gains + swap(gains, 1)
        gains = gains + swap(gains, 2)
    *state, gains = tie(*state, gains)
    *state, gains = tie(*reduce_meet(state), gains)
    state = reduce_third(state)
    gains = gains + swap_x(gains, 2)

    out_grads = reduce_last(out_state)
    grads = reduce_last(state)
    last = grads[640:]
    return (
        input_grad,
        jnp.concatenate([grads[:320], grads[320:640]], axis=1),
        jnp.concatenate([last[:, :32], last[:, 64:96]], axis=0),
        jnp.concatenate([last[:, 32:64], last[:, 96:]], axis=0),
        jnp.concatenate([out_grads[:320], out_grads[320:]], axis=1),
        gains[:D],
        gains[D : D + HD],
        gains[D + HD :],
    )


def solution(mesh):
    in_specs = (
        P(("dp", "tensor"), None),
        P(("dp", "tensor"), None),
        P(None, "tensor"),
        P(None, "tensor"),
        P(None, "tensor"),
        P("tensor", None),
        P(),
        P(),
        P(),
        P("dp", None),
        P("dp"),
        P("dp"),
    )
    out_specs = (
        P(("dp", "tensor"), None),
        P("dp", "tensor"),
        P("dp", "tensor"),
        P("dp", "tensor"),
        P("dp", "tensor"),
        P(),
        P(),
        P(),
    )
    return jax.shard_map(
        on_device, mesh=mesh, in_specs=in_specs, out_specs=out_specs, check_vma=False
    )
```

```python
import functools

import jax
import jax.numpy as jnp
from jax import lax
from jax.experimental import pallas as pl
from jax.experimental.pallas import tpu as pltpu
from jax.sharding import PartitionSpec as P

KVH = 4
GROUPS = 16
HD = 128
EPS = 1e-06
ROPE_BASE = 1000000.0


F32 = jnp.float32
BF16 = jnp.bfloat16


def t_pairs(move, keep=None):
    pairs = []
    for y in range(4):
        for z in range(2):
            for c in range(2):
                if keep is None or keep(y, z, c):
                    a, b, d = move(y, z, c)
                    pairs.append((y * 4 + z * 2 + c, (a % 4) * 4 + b * 2 + d))
    return pairs


def send_y(value, step, keep=None):
    return lax.ppermute(value, "tensor", t_pairs(lambda y, z, c: (y + step, z, c), keep))


def swap_y(value, bits):
    return lax.ppermute(value, "tensor", t_pairs(lambda y, z, c: (y ^ bits, z, c)))


def swap_z(value):
    return lax.ppermute(value, "tensor", t_pairs(lambda y, z, c: (y, 1 - z, c)))


def swap_core(value):
    return lax.ppermute(value, "tensor", t_pairs(lambda y, z, c: (y, z, 1 - c)))


def send_x(value, step):
    return lax.ppermute(
        value, "dp", [(h * 4 + x, h * 4 + (x + step) % 4) for h in range(4) for x in range(4)]
    )


def send_h(value, step):
    return lax.ppermute(
        value, "dp", [(h * 4 + x, ((h + step) % 4) * 4 + x) for h in range(4) for x in range(4)]
    )


def swap_x(value, bits):
    return lax.ppermute(
        value, "dp", [(h * 4 + x, h * 4 + (x ^ bits)) for h in range(4) for x in range(4)]
    )


def swap_h(value, bits):
    return lax.ppermute(
        value, "dp", [(h * 4 + x, (h ^ bits) * 4 + x) for h in range(4) for x in range(4)]
    )


def total4(value, swap):
    one, two, three = swap(value, 1), swap(value, 2), swap(value, 3)
    return (value + one) + (two + three)


def tie(*values):
    return lax.optimization_barrier(values)


VMEM = pl.BlockSpec(memory_space=pltpu.VMEM)
SMEM = pl.BlockSpec(memory_space=pltpu.SMEM)
ANY = pl.BlockSpec(memory_space=pl.ANY)
NT = (((1,), (1,)), ((), ()))
TN = (((0,), (0,)), ((), ()))
D = 5120


def dot(a, b, dims=(((1,), (0,)), ((), ()))):
    return lax.dot_general(a, b, dims, preferred_element_type=F32)


def call(kernel, out, args, specs=None, scratch=(), limit=48):
    many = isinstance(out, list)
    shapes = [jax.ShapeDtypeStruct(s, t) for s, t in (out if many else [out])]
    result = pl.pallas_call(
        kernel,
        out_shape=shapes,
        in_specs=list(specs) if specs else [VMEM] * len(args),
        out_specs=[VMEM] * len(shapes),
        scratch_shapes=list(scratch),
        compiler_params=pltpu.CompilerParams(vmem_limit_bytes=limit * 2**20),
        cost_estimate=pl.CostEstimate(flops=1, bytes_accessed=1, transcendentals=0),
    )(*args)
    return result if many else result[0]


def load_rows(place, blocks, whole, sems):
    mid, mid_pair, side, side_pair, far, far_pair, last, last_pair, own = blocks
    core = place[2]

    def pick(zero, one):
        return zero + (one - zero) * core

    plan = [
        (own, 0, 0),
        (mid, pick(96, 32), 0),
        (mid_pair, pick(32, 96), 1),
        (side, pick(128, 64), 0),
        (side_pair, pick(64, 128), 1),
        (far, pick(224, 192), 0),
        (far_pair, pick(192, 224), 1),
    ]
    copies = []
    for n, (block, base, turned) in enumerate(plan):
        for half in range(2):
            at = pl.multiple_of(base + 256 * (half ^ turned), 32)
            copies.append(
                pltpu.make_async_copy(
                    block.at[pl.ds(half * 32, 32)], whole.at[pl.ds(at, 32)], sems.at[2 * n + half]
                )
            )
    for half in range(2):
        for n, (block, turned) in enumerate(((last, 0), (last_pair, 1))):
            copy = pltpu.make_async_copy(
                block.at[pl.ds(half * 32, 32)],
                whole.at[pl.ds(160 + 256 * (half ^ turned), 32)],
                sems.at[14 + half],
            )

            @pl.when(core == n)
            def _():
                copy.start()

    for copy in copies:
        copy.start()
    for copy in copies:
        copy.wait()
    for half in range(2):
        pltpu.make_async_copy(
            last.at[pl.ds(half * 32, 32)], whole.at[pl.ds(160, 32)], sems.at[14 + half]
        ).wait()


def load_plane(place, parts, w_kv, sems):
    copies = []
    for n, part in enumerate(parts):
        z, core = place[1] ^ (n // 2), place[2] ^ (n % 2)
        for kind in range(2):
            at = pl.multiple_of(kind * HD + z * 64 + core * 32, 32)
            copies.append(
                pltpu.make_async_copy(part.at[kind], w_kv.at[pl.ds(at, 32)], sems.at[2 * n + kind])
            )
    for copy in copies:
        copy.start()
    return copies


PLANE_SCRATCH = (pltpu.VMEM((256, D), BF16), pltpu.SemaphoreType.DMA((8,)))
ROWS_SCRATCH = (pltpu.VMEM((512, D), BF16), pltpu.SemaphoreType.DMA((16,)))
PLACED = [SMEM] + [ANY] * 9


def by_core(zero, one):
    pairs = []
    for y in range(4):
        for z in range(2):
            for c, move in enumerate((zero, one)):
                if move is not None:
                    a, b = move(y, z)
                    pairs.append((y * 4 + z * 2 + c, (a % 4) * 4 + b * 2 + c))
    return pairs


UP = lambda y, z: (y + 1, z)
DOWN = lambda y, z: (y - 1, z)
ACROSS = lambda y, z: (y + 2, z)
OTHER = lambda y, z: (y, 1 - z)


def gather_one(own):
    mid = lax.ppermute(own, "tensor", by_core(UP, DOWN))
    side = lax.ppermute(own, "tensor", by_core(OTHER, ACROSS))
    return mid, side


def gather_two(side):
    far = lax.ppermute(side, "tensor", by_core(UP, OTHER))
    last = lax.ppermute(side, "tensor", by_core(DOWN, None))
    return far, last


def kv_pairs(beside, back):
    pairs = []
    for y in range(4):
        for z in range(2):
            e = y // 2
            ways = [(y + 1, e), (y - 1, 1 - e)] if beside else [(y + 2, e)]
            for to, via in ways:
                here, there = y * 4 + z * 2 + via, (to % 4) * 4 + z * 2 + e
                pairs.append((there, here) if back else (here, there))
    return pairs


KV_BESIDE, KV_ACROSS = kv_pairs(True, False), kv_pairs(False, False)
DKV_BESIDE, DKV_ACROSS = kv_pairs(True, True), kv_pairs(False, True)


def swap_last(value):
    return lax.ppermute(value, "tensor", [(t, t + 1) for t in range(0, 16, 2)])


def project_kernel(place, *refs):
    blocks, planes, (w_q, q_out, kv_out, whole, sems, w_kv, w_sems) = refs[:9], refs[9:13], refs[13:]
    copies = load_plane(place, planes, w_kv, w_sems)
    load_rows(place, blocks, whole, sems)
    q_out[...] = dot(whole[...], w_q[...]).astype(BF16)
    for copy in copies:
        copy.wait()
    kv_out[...] = dot(whole[...], w_kv[...], NT).astype(BF16)


def project(place, blocks, planes, w_q):
    return call(
        project_kernel,
        [((512, 256), BF16), ((512, 256), BF16)],
        [place, *blocks, *planes, w_q],
        PLACED + [ANY] * 4 + [VMEM],
        (*ROWS_SCRATCH, *PLANE_SCRATCH),
    )


def flip_z(value):
    return jnp.concatenate([value[128:256], value[:128], value[384:], value[256:384]], axis=0)


def flip_c(value):
    return jnp.concatenate([value[256:], value[:256]], axis=0)


def turn_y(value, step):
    if step % 4 == 0:
        return value
    parts = []
    for group in range(4):
        for dy in range(4):
            at = group * 128 + ((dy + step) % 4) * 32
            parts.append(value[at : at + 32])
    return jnp.concatenate(parts, axis=0)


def pick_heads(place, slots, heads):
    own, side, across = slots
    for n in range(2):
        step = (2 * place[2] + n - place[0] + 4) % 4
        for s, slot in enumerate((own, side, across, side)):

            @pl.when(step == s)
            def _():
                value = flip_c(slot[...]) if s == 1 else slot[...]
                heads[n] = turn_y(value, -s)


def spin(value, cosine, sine):
    return value * cosine + pltpu.roll(value, 64, 1) * sine


def spin_back(grad, cosine, sine):
    return grad * cosine - pltpu.roll(grad, 64, 1) * sine


def norm(value):
    value = value.astype(F32)
    scale = lax.rsqrt(jnp.mean(value * value, axis=-1, keepdims=True) + EPS)
    return value * scale, scale


def forward_kernel(
    place, q, s0, s1, s2, cosine, sine, seg, q_gain, k_gain, out, probs, heads
):
    pick_heads(place, (s0, s1, s2), heads)
    co, si = cosine[...], sine[...]
    seg_q, row_q = seg[:, 0:1], seg[:, 1:2]
    turned = seg[...].T
    keep = (seg_q == turned[0:1]) & (row_q >= turned[1:2])
    for n in range(2):
        q_unit, _ = norm(q[:, n * HD : n * HD + HD])
        k_unit, _ = norm(heads[n, :, :HD])
        q_rot = spin(q_unit * q_gain[...], co, si).astype(BF16)
        k_rot = spin(k_unit * k_gain[...], co, si).astype(BF16)
        scores = jnp.where(keep, dot(q_rot, k_rot, NT) * HD**-0.5, -1e30)
        weights = jnp.exp(scores - jnp.max(scores, axis=-1, keepdims=True))
        soft = weights / jnp.sum(weights, axis=-1, keepdims=True)
        probs[n] = soft
        value = dot(soft.astype(BF16), heads[n, :, HD:]).astype(BF16)
        out[:, n * HD : n * HD + HD] = value


SUMS = (
    ((1, 1), (3, 1), (0, 1), (3, 0)),
    ((2, 1), (2, 0), (1, 0)),
)


def rows_of(core, turned):
    slices = []
    for dy, dz in SUMS[core]:
        for dc in range(2):
            slices.append(slice((dc ^ turned) * 256 + dz * 128 + dy * 32, (dc ^ turned) * 256 + dz * 128 + dy * 32 + 32))
    slices += [slice(turned * 256, turned * 256 + 32)] * (9 - len(slices))
    return slices


def backward_kernel(place, *refs):
    blocks = refs[:9]
    w_out, q, s0, s1, s2, cosine, sine, advantage, q_gain, k_gain, probs, attended = refs[9:21]
    dq, keep, send, d0, d1, d2, gains, heads, whole, sems = refs[21:]
    pick_heads(place, (s0, s1, s2), heads)
    load_rows(place, blocks, whole, sems)
    grad_out = (dot(whole[...], w_out[...], NT) * advantage[:, 0:1]).astype(BF16)
    co, si = cosine[...], sine[...]
    q_sum = jnp.zeros((1, HD), F32)
    k_sum = jnp.zeros((1, HD), F32)
    d0[...] = jnp.zeros_like(d0)
    for n in range(2):
        cols = slice(n * HD, n * HD + HD)
        q_unit, q_scale = norm(q[:, cols])
        k_unit, k_scale = norm(heads[n, :, :HD])
        q_rot = spin(q_unit * q_gain[...], co, si).astype(BF16)
        k_rot = spin(k_unit * k_gain[...], co, si).astype(BF16)
        grad = grad_out[:, cols]
        delta = jnp.sum(
            grad.astype(F32) * attended[:, cols].astype(F32), axis=-1, keepdims=True
        )
        soft = probs[n]
        score = (soft * (dot(grad, heads[n, :, HD:], NT) - delta) * HD**-0.5).astype(BF16)
        e_q = spin_back(dot(score, k_rot), co, si)
        e_k = spin_back(dot(q_rot.T, score).T, co, si)
        grad_v = dot(grad.T, soft.astype(BF16)).T.astype(BF16)
        q_sum += jnp.sum(e_q * q_unit, axis=0, keepdims=True)
        k_sum += jnp.sum(e_k * k_unit, axis=0, keepdims=True)
        e_q = e_q * q_gain[...]
        e_k = e_k * k_gain[...]
        grad_q = q_scale * (e_q - q_unit * jnp.mean(e_q * q_unit, axis=-1, keepdims=True))
        grad_k = k_scale * (e_k - k_unit * jnp.mean(e_k * k_unit, axis=-1, keepdims=True))
        dq[:, cols] = grad_q.astype(BF16)
        both = jnp.concatenate([grad_k.astype(BF16), grad_v], axis=1)
        step = (2 * place[2] + n - place[0] + 4) % 4
        for s, slot in enumerate((d0, d1, d2, d1)):

            @pl.when(step == s)
            def _():
                slot[...] = both

    gains[...] = jnp.concatenate([q_sum, k_sum], axis=0)
    for core in range(2):

        @pl.when(place[2] == core)
        def _():
            keep[...] = jnp.concatenate([dq[at] for at in rows_of(core, 0)], axis=0)
            send[...] = jnp.concatenate([dq[at] for at in rows_of(1 - core, 1)], axis=0)


def plane_kernel(place, own, side, across, out):
    total = own[...].astype(F32) + turn_y(across[...], 2).astype(F32)
    home = place[0] // 2 == place[2]

    @pl.when(home)
    def _():
        out[...] = (total + turn_y(side[...], 3).astype(F32)).astype(BF16)

    @pl.when(jnp.logical_not(home))
    def _():
        out[...] = (total + turn_y(flip_c(side[...]), 1).astype(F32)).astype(BF16)


def pair_kernel(a, b, out):
    out[...] = (a[...].astype(F32) + flip_z(b[...]).astype(F32)).astype(BF16)


def columns_kernel(place, a, b, dq, right, rows_here):
    full = (a[...].astype(F32) + flip_c(b[...]).astype(F32)).astype(BF16)
    for core in range(2):

        @pl.when(place[2] == core)
        def _():
            some = [full[at] for at in rows_of(core, 0)]
            some = some[4:9] if core == 0 else some[2:7]
            rows_here[...] = jnp.concatenate(some, axis=0)

    right[:, :256] = dq[...]
    spot = place[1] * 2 + place[2]
    for n in range(4):

        @pl.when(spot == n)
        def _():
            right[:, 256:] = jnp.concatenate(
                [full[:, n * 32 : n * 32 + 32], full[:, HD + n * 32 : HD + n * 32 + 32]], axis=1
            )


def weight_kernel(place, *refs):
    if len(refs) == 17:
        blocks, (right, o0, o1, o2a, o2b, o3, whole, sems) = refs[:9], refs[9:]
    else:
        blocks, (right, w_q, w_kv, gain, o0, o1, o2a, o2b, o3, sums, whole, sems) = refs[:9], refs[9:]
    turned = right[...].T
    one = lax.broadcasted_iota(jnp.int32, (256, 256), 0)
    eye = jnp.where(one == lax.broadcasted_iota(jnp.int32, (256, 256), 1), 1.0, 0.0).astype(BF16)
    load_rows(place, blocks, whole, sems)
    for h in range(4):
        at = slice(h * 1280, h * 1280 + 1280)
        exact = dot(turned, whole[:, at])
        side = exact.astype(BF16)
        part = [dot(eye, side[:, i * 256 : i * 256 + 256], NT).astype(BF16) for i in range(5)]
        part = jnp.concatenate(part, axis=0)
        if len(refs) != 17:
            product = (part[:, :256].astype(F32) * w_q[at].astype(F32)).astype(BF16)
            total = dot(jnp.ones((8, 256), BF16), product, NT)[0:1]
            total += jnp.sum(exact[256:288] * w_kv[0, :, at].astype(F32), axis=0, keepdims=True)
            total += jnp.sum(exact[288:320] * w_kv[1, :, at].astype(F32), axis=0, keepdims=True)
            sums[:, at] = total / gain[:, at]
        k = (h - place[3] + 4) % 4
        for x in range(4):
            s = (x - place[4] + 4) % 4
            tile = part[x * 320 : x * 320 + 320]
            if right.shape[1] == 256:
                tile = jnp.concatenate([tile[:, :HD], tile[:, HD:]], axis=0)
            else:
                tile = jnp.concatenate(
                    [
                        tile[:, :HD],
                        tile[:, HD : 2 * HD],
                        jnp.concatenate([tile[:160, 2 * HD :], tile[160:, 2 * HD :]], axis=1),
                    ],
                    axis=0,
                )
            for at, out in ((0, o0), (1, o1), (3, o3)):

                @pl.when(s == at)
                def _():
                    out[k] = tile

            @pl.when((s == 2) & (k < 2))
            def _():
                o2a[jnp.minimum(k, 1)] = tile

            @pl.when((s == 2) & (k >= 2))
            def _():
                o2b[jnp.maximum(k - 2, 0)] = tile


def weight_grad(blocks, place, right, *more):
    rows = right.shape[1] * 320 // HD
    four, two = ((4, rows, HD), BF16), ((2, rows, HD), BF16)
    return call(
        weight_kernel,
        [four, four, two, two, four] + ([((1, D), F32)] if more else []),
        [place, *blocks, right, *more],
        PLACED + [VMEM] * (1 + len(more)),
        ROWS_SCRATCH,
    )


def around_kernel(o1, o3, a, b, right, left):
    right[0:2] = (o1[0:2].astype(F32) + a[...].astype(F32)).astype(BF16)
    right[2:4] = o1[2:4]
    left[0:2] = o3[0:2]
    left[2:4] = (o3[2:4].astype(F32) + b[...].astype(F32)).astype(BF16)


def meet_kernel(o0, r, s, p0, p1, p2, p3):
    for k, out in enumerate((p0, p1, p2, p3)):
        out[...] = (o0[k].astype(F32) + r[k].astype(F32) + s[k].astype(F32)).astype(BF16)


def reduce_first(parts):
    o0, o1, o2a, o2b, o3 = parts
    return o0, o1, o3, send_x(o2a, 1), send_x(o2b, -1)


def reduce_around(state):
    o0, o1, o3, a, b = state
    right, left = call(around_kernel, [(o1.shape, BF16)] * 2, [o1, o3, a, b])
    return o0, right, left


def reduce_second(state):
    o0, right, left = state
    return o0, send_x(right, 1), send_x(left, -1)


def halve_kernel(place, o0, r, s, here, near, far):
    def total(k):
        return (o0[k].astype(F32) + r[k].astype(F32) + s[k].astype(F32)).astype(BF16)

    here[...] = total(0)
    far[0:640] = total(2)
    for odd in range(2):

        @pl.when(place[3] % 2 == odd)
        def _():
            near[...] = total(3 if odd else 1)
            far[640:1280] = total(1 if odd else 3)


def reduce_meet(state):
    o0, r, s = state
    return call(meet_kernel, [(o0.shape[1:], BF16)] * 4, [o0, r, s])


def reduce_third(state):
    p0, p1, p2, p3 = state
    return p0, send_h(p1, 1), send_h(p2, 2), send_h(p3, -1)


def reduce_last(state):
    zero, one, two, three = [part.astype(F32) for part in state]
    return (zero + two) + (one + three)


def first_kernel(mine, pair, one, two, m, p, s_m, s_p):
    copies = [
        pltpu.make_async_copy(mine.at[pl.ds(0, 128)], m, s_m),
        pltpu.make_async_copy(pair.at[pl.ds(0, 128)], p, s_p),
    ]
    for copy in copies:
        copy.start()
    for copy in copies:
        copy.wait()
    one[...] = (m[0:64].astype(F32) + p[0:64].astype(F32)).astype(BF16)
    two[...] = (m[64:128].astype(F32) + p[64:128].astype(F32)).astype(BF16)


def second_kernel(place, *refs):
    planes, (mine, pair, one, two, here, three, four, own, w_kv, sems, m, p, s_m, s_p) = refs[:4], refs[4:]
    copies = load_plane(place, planes, w_kv, sems)
    at = pl.ds(pl.multiple_of(128 - 64 * place[2], 32), 160)
    sides = [
        pltpu.make_async_copy(mine.at[at], m, s_m),
        pltpu.make_async_copy(pair.at[at], p, s_p),
    ]
    for copy in sides:
        copy.start()
    for copy in copies + sides:
        copy.wait()
    term = dot(here[...], w_kv[...])

    def both(at, size=64):
        return m[at : at + size].astype(F32) + p[at : at + size].astype(F32)

    own[...] = both(128, 32) + term[128:160]
    four[...] = (both(64) + term[64:128]).astype(BF16)

    @pl.when(place[2] == 0)
    def _():
        three[...] = (both(0) + one[...].astype(F32) + two[...].astype(F32)).astype(BF16)

    @pl.when(place[2] == 1)
    def _():
        three[...] = (both(0) + one[...].astype(F32) + term[0:64]).astype(BF16)


def third_kernel(three, four, out):
    out[...] = (three[32:64].astype(F32) + four[32:64].astype(F32)).astype(BF16)


def last_kernel(own, three, four, pair, x, gain, grad, advantage, out):
    total = own[...] + three[0:32].astype(F32) + four[0:32].astype(F32) + pair[...].astype(F32)
    value = x[...].astype(F32)
    scale = lax.rsqrt(jnp.mean(value * value, axis=-1, keepdims=True) + EPS)
    unit = value * scale
    weighted = total * gain[...]
    inner = weighted - unit * jnp.mean(weighted * unit, axis=-1, keepdims=True)
    scaled = (grad[...].astype(F32) * advantage[0:32, 0:1]).astype(BF16)
    out[...] = (scale * inner + scaled.astype(F32)).astype(BF16)


def normed_kernel(x, pair, gain, out):
    for n, ref in enumerate((x, pair)):
        unit, _ = norm(ref[...])
        out[n * 32 : n * 32 + 32] = (unit * gain[...]).astype(BF16)


def stack_kernel(x, pair, out):
    out[0:32] = x[...]
    out[32:64] = pair[...]


def on_device(
    inputs,
    upstream,
    w_query,
    w_key,
    w_value,
    w_output,
    norm_gain,
    query_gain,
    key_gain,
    lengths,
    rewards,
    groups,
):
    t_at = lax.axis_index("tensor")
    d_at = lax.axis_index("dp")
    y_at, z_at, c_at = t_at // 4, (t_at // 2) % 2, t_at % 2
    place = jnp.stack([y_at, z_at, c_at, d_at // 4, d_at % 4]).astype(jnp.int32)
    gain_row = norm_gain.reshape(1, D)

    inputs_pair, upstream_pair, rewards, groups, lengths, w_key, w_value, place = tie(
        swap_core(inputs), swap_core(upstream), rewards, groups, lengths, w_key, w_value, place
    )
    x_own = call(normed_kernel, ((64, D), BF16), [inputs, inputs_pair, gain_row])

    x_own, w_key, w_value, upstream_pair, lengths, place = tie(
        x_own, w_key, w_value, upstream_pair, lengths, place
    )
    x_mid, x_side = gather_one(x_own)
    w_own = jnp.stack([w_key.T, w_value.T])
    w_pair, w_far = swap_core(w_own), swap_z(w_own)
    g_own = call(stack_kernel, ((64, D), BF16), [upstream, upstream_pair])
    lens = lengths[0]
    ends = jnp.cumsum(lens)
    starts = ends - lens
    j = jnp.arange(512, dtype=jnp.int32)
    t_of = (
        ((place[0] + (j // 32) % 4) % 4) * 4
        + jnp.bitwise_xor(place[1], (j // 128) % 2) * 2
        + jnp.bitwise_xor(place[2], j // 256)
    )
    rows = t_of * 32 + j % 32
    inside = (rows[:, None] >= starts[None, :]) & (rows[:, None] < ends[None, :])
    segment = jnp.sum(jnp.where(inside, jnp.arange(8, dtype=jnp.int32)[None, :], 0), axis=1)
    position = rows - jnp.sum(jnp.where(inside, starts[None, :], 0), axis=1)
    half = HD // 2
    inverse = ROPE_BASE ** (-(jnp.arange(half, dtype=F32) * 2.0 / HD))
    angle = position.astype(F32)[:, None] * inverse[None, :]
    cosine = jnp.concatenate([jnp.cos(angle), jnp.cos(angle)], axis=1)
    sine = jnp.concatenate([-jnp.sin(angle), jnp.sin(angle)], axis=1)
    marks = jnp.stack([segment, rows], axis=1).astype(F32)
    marks = jnp.concatenate([marks, jnp.zeros((512, HD - 2), F32)], axis=1)
    x_mid, x_side, w_pair, w_far, g_own, rewards, groups, cosine, sine, marks, inside = tie(
        x_mid, x_side, w_pair, w_far, g_own, rewards, groups, cosine, sine, marks, inside
    )
    onehot = (groups[:, None] == jnp.arange(GROUPS, dtype=jnp.int32)[None, :]).astype(F32)
    stats = jnp.concatenate(
        [
            jnp.sum(onehot, axis=0),
            jnp.sum(onehot * rewards[:, None], axis=0),
            jnp.sum(onehot * (rewards * rewards)[:, None], axis=0),
        ]
    )
    x_far, x_last = gather_two(x_side)
    stats = total4(stats, swap_x)
    x_mid_pair, x_side_pair = swap_core(x_mid), swap_core(x_side)
    x_far, x_last, x_mid_pair, x_side_pair, stats, g_own = tie(
        x_far, x_last, x_mid_pair, x_side_pair, stats, g_own
    )
    g_mid, g_side = gather_one(g_own)
    planes = [w_own, w_pair, w_far, swap_core(w_far)]
    x_blocks = [
        x_mid, x_mid_pair, x_side, x_side_pair, x_far, swap_core(x_far), x_last, swap_last(x_last), x_own
    ]
    query_proj, kv = project(place, x_blocks, planes, w_query)
    query_proj, kv, g_mid, g_side, stats = tie(query_proj, kv, g_mid, g_side, stats)

    g_far, g_last = gather_two(g_side)
    slots = [kv, lax.ppermute(kv, "tensor", KV_BESIDE), lax.ppermute(kv, "tensor", KV_ACROSS)]
    stats = stats + swap_h(stats, 1)
    stats = stats + swap_h(stats, 2)
    *slots, g_mid, g_side, stats = tie(*slots, g_mid, g_side, stats)
    counts, sums, squares = stats[:GROUPS], stats[GROUPS : 2 * GROUPS], stats[2 * GROUPS :]
    safe = jnp.maximum(counts, 1.0)
    mean = sums / safe
    variance = squares / safe - mean * mean
    seg_mean = jnp.sum(onehot * mean[None, :], axis=1)
    seg_var = jnp.sum(onehot * variance[None, :], axis=1)
    seg_adv = (rewards - seg_mean) / jnp.sqrt(seg_var + 1.0)

    row_adv = jnp.sum(jnp.where(inside, seg_adv[None, :], 0.0), axis=1)
    advantage = jnp.broadcast_to(row_adv[:, None], (512, HD))
    g_mid_pair, g_side_pair = swap_core(g_mid), swap_core(g_side)
    q_row, k_row = query_gain.reshape(1, HD), key_gain.reshape(1, HD)
    attended, probs = call(
        forward_kernel,
        [((512, 256), BF16), ((2, 512, 512), F32)],
        [place, query_proj, *slots, cosine, sine, marks, q_row, k_row],
        [SMEM] + [VMEM] * 9,
        (pltpu.VMEM((2, 512, 256), BF16),),
    )
    scaled = (attended.astype(F32) * row_adv[:, None]).astype(BF16)
    g_far, g_last, g_mid_pair, g_side_pair, attended, scaled, probs, advantage = tie(
        g_far, g_last, g_mid_pair, g_side_pair, attended, scaled, probs, advantage
    )
    g_blocks = [
        g_mid, g_mid_pair, g_side, g_side_pair, g_far, swap_core(g_far), g_last, swap_last(g_last), g_own
    ]
    parts = weight_grad(g_blocks, place, scaled)
    *parts, probs = tie(*parts, probs)
    out_state = reduce_first(parts)
    dq, keep, send, d0, d1, d2, head_gains = call(
        backward_kernel,
        [((512, 256), BF16), ((288, 256), BF16), ((288, 256), BF16)]
        + [((512, 256), BF16)] * 3
        + [((2, HD), F32)],
        [place, *g_blocks, w_output, query_proj, *slots, cosine, sine, advantage, q_row, k_row, probs, attended],
        PLACED + [VMEM] * 12,
        (pltpu.VMEM((2, 512, 256), BF16), *ROWS_SCRATCH),
    )
    dq, keep, send, d0, d1, d2, *out_state = tie(dq, keep, send, d0, d1, d2, *out_state)
    d1, d2 = lax.ppermute(d1, "tensor", DKV_BESIDE), lax.ppermute(d2, "tensor", DKV_ACROSS)
    out_state = reduce_second(reduce_around(out_state))

    back = lambda rows: dot(rows, w_query, NT).astype(BF16)
    other, mine = back(send), back(keep)
    other, mine, d0, d1, d2 = tie(other, mine, d0, d1, d2)
    pair = swap_core(other)
    dkv = call(plane_kernel, ((512, 256), BF16), [place, d0, d1, d2], [SMEM] + [VMEM] * 3)
    dkv_pair = swap_z(dkv)
    one, two = call(
        first_kernel,
        [((64, D), BF16)] * 2,
        [mine, pair],
        [ANY] * 2,
        (pltpu.VMEM((128, D), BF16),) * 2 + (pltpu.SemaphoreType.DMA(()),) * 2,
    )
    dkv, dkv_pair, one, two = tie(dkv, dkv_pair, one, two)
    dkv = call(pair_kernel, ((512, 256), BF16), [dkv, dkv_pair])
    dkv_pair = swap_core(dkv)
    one = lax.ppermute(one, "tensor", by_core(UP, OTHER))
    two = lax.ppermute(two, "tensor", by_core(DOWN, None))
    dkv, dkv_pair = tie(dkv, dkv_pair)
    combined, rows_here = call(
        columns_kernel,
        [((512, 320), BF16), ((160, 256), BF16)],
        [place, dkv, dkv_pair, dq],
        [SMEM] + [VMEM] * 3,
    )
    *parts, norm_sums = weight_grad(x_blocks, place, combined, w_query, w_own, gain_row)
    *parts, one, two, norm_sums, o0, o1, o2 = tie(*parts, one, two, norm_sums, *out_state)
    state = reduce_first(parts)
    gains = jnp.concatenate([norm_sums[0], head_gains[0], head_gains[1]])
    gains = gains + swap_core(gains)
    gains = gains + swap_z(gains)
    out_here, out_near, out_far = call(
        halve_kernel,
        [((640, HD), BF16), ((640, HD), BF16), ((1280, HD), BF16)],
        [place, o0, o1, o2],
        [SMEM] + [VMEM] * 3,
    )
    out_far = swap_h(out_far, 2)
    three, four, own = call(
        second_kernel,
        [((64, D), BF16), ((64, D), BF16), ((32, D), F32)],
        [place, *planes, mine, pair, one, two, rows_here],
        [SMEM] + [ANY] * 6 + [VMEM] * 3,
        (
            *PLANE_SCRATCH,
            pltpu.VMEM((160, D), BF16),
            pltpu.VMEM((160, D), BF16),
            pltpu.SemaphoreType.DMA(()),
            pltpu.SemaphoreType.DMA(()),
        ),
    )
    *state, three, four, out_near, out_far, gains = tie(
        *state, three, four, out_near, out_far, gains
    )

    three = lax.ppermute(three, "tensor", by_core(OTHER, ACROSS))
    four = lax.ppermute(four, "tensor", by_core(DOWN, UP))
    state = reduce_second(reduce_around(state))
    out_near = (out_near.astype(F32) + out_far[640:].astype(F32)).astype(BF16)
    out_near = swap_h(out_near, 1)
    three, four, out_near, gains = tie(three, four, out_near, gains)
    pair = swap_core(call(third_kernel, ((32, D), BF16), [three, four]))
    input_grad = call(
        last_kernel,
        ((32, D), BF16),
        [own, three, four, pair, inputs, gain_row, upstream, advantage],
    )
    gains = total4(total4(gains, swap_y), swap_x)
    *state, gains, input_grad = tie(*state, gains, input_grad)
    *state, gains = tie(*reduce_meet(state), gains)
    state = reduce_third(state)
    gains = gains + swap_h(gains, 1)
    gains = gains + swap_h(gains, 2)
    out_grads = out_here.astype(F32) + out_far[:640].astype(F32) + out_near.astype(F32)
    grads = reduce_last(state)
    last = grads[640:]
    return (
        input_grad,
        jnp.concatenate([grads[:320], grads[320:640]], axis=1),
        jnp.concatenate([last[:, :32], last[:, 64:96]], axis=0),
        jnp.concatenate([last[:, 32:64], last[:, 96:]], axis=0),
        jnp.concatenate([out_grads[:320], out_grads[320:]], axis=1),
        gains[:D],
        gains[D : D + HD],
        gains[D + HD :],
    )


def solution(mesh):
    in_specs = (
        P(("dp", "tensor"), None),
        P(("dp", "tensor"), None),
        P(None, "tensor"),
        P(None, "tensor"),
        P(None, "tensor"),
        P("tensor", None),
        P(),
        P(),
        P(),
        P("dp", None),
        P("dp"),
        P("dp"),
    )
    out_specs = (
        P(("dp", "tensor"), None),
        P("dp", "tensor"),
        P("dp", "tensor"),
        P("dp", "tensor"),
        P("dp", "tensor"),
        P(),
        P(),
        P(),
    )
    return jax.shard_map(
        on_device, mesh=mesh, in_specs=in_specs, out_specs=out_specs, check_vma=False
    )
```

```python
import functools

import jax
import jax.numpy as jnp
from jax import lax
from jax.experimental import pallas as pl
from jax.experimental.pallas import tpu as pltpu
from jax.sharding import PartitionSpec as P

KVH = 4
GROUPS = 16
HD = 128
EPS = 1e-06
ROPE_BASE = 1000000.0


F32 = jnp.float32
BF16 = jnp.bfloat16


def t_pairs(move, keep=None):
    pairs = []
    for y in range(4):
        for z in range(2):
            for c in range(2):
                if keep is None or keep(y, z, c):
                    a, b, d = move(y, z, c)
                    pairs.append((y * 4 + z * 2 + c, (a % 4) * 4 + b * 2 + d))
    return pairs


def send_y(value, step, keep=None):
    return lax.ppermute(value, "tensor", t_pairs(lambda y, z, c: (y + step, z, c), keep))


def swap_y(value, bits):
    return lax.ppermute(value, "tensor", t_pairs(lambda y, z, c: (y ^ bits, z, c)))


def swap_z(value):
    return lax.ppermute(value, "tensor", t_pairs(lambda y, z, c: (y, 1 - z, c)))


def swap_core(value):
    return lax.ppermute(value, "tensor", t_pairs(lambda y, z, c: (y, z, 1 - c)))


def send_x(value, step):
    return lax.ppermute(
        value, "dp", [(h * 4 + x, h * 4 + (x + step) % 4) for h in range(4) for x in range(4)]
    )


def send_h(value, step):
    return lax.ppermute(
        value, "dp", [(h * 4 + x, ((h + step) % 4) * 4 + x) for h in range(4) for x in range(4)]
    )


def swap_x(value, bits):
    return lax.ppermute(
        value, "dp", [(h * 4 + x, h * 4 + (x ^ bits)) for h in range(4) for x in range(4)]
    )


def swap_h(value, bits):
    return lax.ppermute(
        value, "dp", [(h * 4 + x, (h ^ bits) * 4 + x) for h in range(4) for x in range(4)]
    )


def total4(value, swap):
    one, two, three = swap(value, 1), swap(value, 2), swap(value, 3)
    return (value + one) + (two + three)


def tie(*values):
    return lax.optimization_barrier(values)


VMEM = pl.BlockSpec(memory_space=pltpu.VMEM)
SMEM = pl.BlockSpec(memory_space=pltpu.SMEM)
ANY = pl.BlockSpec(memory_space=pl.ANY)
NT = (((1,), (1,)), ((), ()))
TN = (((0,), (0,)), ((), ()))
D = 5120
SUM_ROWS = 256


def dot(a, b, dims=(((1,), (0,)), ((), ()))):
    return lax.dot_general(a, b, dims, preferred_element_type=F32)


def call(kernel, out, args, specs=None, scratch=(), limit=48):
    many = isinstance(out, list)
    shapes = [jax.ShapeDtypeStruct(s, t) for s, t in (out if many else [out])]
    result = pl.pallas_call(
        kernel,
        out_shape=shapes,
        in_specs=list(specs) if specs else [VMEM] * len(args),
        out_specs=[VMEM] * len(shapes),
        scratch_shapes=list(scratch),
        compiler_params=pltpu.CompilerParams(vmem_limit_bytes=limit * 2**20),
        cost_estimate=pl.CostEstimate(flops=1, bytes_accessed=1, transcendentals=0),
    )(*args)
    return result if many else result[0]


def load_rows(place, blocks, whole, sems):
    mid, mid_pair, side, side_pair, far, far_pair, last, last_pair, own = blocks
    core = place[2]

    def pick(zero, one):
        return zero + (one - zero) * core

    plan = [
        (own, 0, 0),
        (mid, pick(96, 32), 0),
        (mid_pair, pick(32, 96), 1),
        (side, pick(128, 64), 0),
        (side_pair, pick(64, 128), 1),
        (far, pick(224, 192), 0),
        (far_pair, pick(192, 224), 1),
    ]
    copies = []
    for n, (block, base, turned) in enumerate(plan):
        for half in range(2):
            at = pl.multiple_of(base + 256 * (half ^ turned), 32)
            copies.append(
                pltpu.make_async_copy(
                    block.at[pl.ds(half * 32, 32)], whole.at[pl.ds(at, 32)], sems.at[2 * n + half]
                )
            )
    for half in range(2):
        for n, (block, turned) in enumerate(((last, 0), (last_pair, 1))):
            copy = pltpu.make_async_copy(
                block.at[pl.ds(half * 32, 32)],
                whole.at[pl.ds(160 + 256 * (half ^ turned), 32)],
                sems.at[14 + half],
            )

            @pl.when(core == n)
            def _():
                copy.start()

    for copy in copies:
        copy.start()
    for copy in copies:
        copy.wait()
    for half in range(2):
        pltpu.make_async_copy(
            last.at[pl.ds(half * 32, 32)], whole.at[pl.ds(160, 32)], sems.at[14 + half]
        ).wait()


def load_plane(place, parts, w_kv, sems):
    copies = []
    for n, part in enumerate(parts):
        z, core = place[1] ^ (n // 2), place[2] ^ (n % 2)
        for kind in range(2):
            at = pl.multiple_of(kind * HD + z * 64 + core * 32, 32)
            copies.append(
                pltpu.make_async_copy(part.at[kind], w_kv.at[pl.ds(at, 32)], sems.at[2 * n + kind])
            )
    for copy in copies:
        copy.start()
    return copies


PLANE_SCRATCH = (pltpu.VMEM((256, D), BF16), pltpu.SemaphoreType.DMA((8,)))
ROWS_SCRATCH = (pltpu.VMEM((512, D), BF16), pltpu.SemaphoreType.DMA((16,)))
PLACED = [SMEM] + [ANY] * 9


def by_core(zero, one):
    pairs = []
    for y in range(4):
        for z in range(2):
            for c, move in enumerate((zero, one)):
                if move is not None:
                    a, b = move(y, z)
                    pairs.append((y * 4 + z * 2 + c, (a % 4) * 4 + b * 2 + c))
    return pairs


UP = lambda y, z: (y + 1, z)
DOWN = lambda y, z: (y - 1, z)
ACROSS = lambda y, z: (y + 2, z)
OTHER = lambda y, z: (y, 1 - z)


def gather_one(own):
    mid = lax.ppermute(own, "tensor", by_core(UP, DOWN))
    side = lax.ppermute(own, "tensor", by_core(OTHER, ACROSS))
    return mid, side


def gather_two(side):
    far = lax.ppermute(side, "tensor", by_core(UP, OTHER))
    last = lax.ppermute(side, "tensor", by_core(DOWN, None))
    return far, last


def kv_pairs(beside, back):
    pairs = []
    for y in range(4):
        for z in range(2):
            e = y // 2
            ways = [(y + 1, e), (y - 1, 1 - e)] if beside else [(y + 2, e)]
            for to, via in ways:
                here, there = y * 4 + z * 2 + via, (to % 4) * 4 + z * 2 + e
                pairs.append((there, here) if back else (here, there))
    return pairs


KV_BESIDE, KV_ACROSS = kv_pairs(True, False), kv_pairs(False, False)
DKV_BESIDE, DKV_ACROSS = kv_pairs(True, True), kv_pairs(False, True)


def swap_last(value):
    return lax.ppermute(value, "tensor", [(t, t + 1) for t in range(0, 16, 2)])


def project_kernel(place, *refs):
    blocks, planes, (w_q, q_out, kv_out, whole, sems, w_kv, w_sems) = refs[:9], refs[9:13], refs[13:]
    copies = load_plane(place, planes, w_kv, w_sems)
    load_rows(place, blocks, whole, sems)
    q_out[...] = dot(whole[...], w_q[...]).astype(BF16)
    for copy in copies:
        copy.wait()
    kv_out[...] = dot(whole[...], w_kv[...], NT).astype(BF16)


def project(place, blocks, planes, w_q):
    return call(
        project_kernel,
        [((512, 256), BF16), ((512, 256), BF16)],
        [place, *blocks, *planes, w_q],
        PLACED + [ANY] * 4 + [VMEM],
        (*ROWS_SCRATCH, *PLANE_SCRATCH),
    )


def flip_z(value):
    return jnp.concatenate([value[128:256], value[:128], value[384:], value[256:384]], axis=0)


def flip_c(value):
    return jnp.concatenate([value[256:], value[:256]], axis=0)


def turn_y(value, step):
    if step % 4 == 0:
        return value
    parts = []
    for group in range(4):
        for dy in range(4):
            at = group * 128 + ((dy + step) % 4) * 32
            parts.append(value[at : at + 32])
    return jnp.concatenate(parts, axis=0)


def pick_heads(place, slots, heads):
    own, side, across = slots
    for n in range(2):
        step = (2 * place[2] + n - place[0] + 4) % 4
        for s, slot in enumerate((own, side, across, side)):

            @pl.when(step == s)
            def _():
                value = flip_c(slot[...]) if s == 1 else slot[...]
                heads[n] = turn_y(value, -s)


def spin(value, cosine, sine):
    return value * cosine + pltpu.roll(value, 64, 1) * sine


def spin_back(grad, cosine, sine):
    return grad * cosine - pltpu.roll(grad, 64, 1) * sine


def norm(value):
    value = value.astype(F32)
    scale = lax.rsqrt(jnp.mean(value * value, axis=-1, keepdims=True) + EPS)
    return value * scale, scale


def forward_kernel(
    place, q, s0, s1, s2, cosine, sine, seg, q_gain, k_gain, out, probs, heads
):
    pick_heads(place, (s0, s1, s2), heads)
    co, si = cosine[...], sine[...]
    seg_q, row_q = seg[:, 0:1], seg[:, 1:2]
    turned = seg[...].T
    keep = (seg_q == turned[0:1]) & (row_q >= turned[1:2])
    for n in range(2):
        q_unit, _ = norm(q[:, n * HD : n * HD + HD])
        k_unit, _ = norm(heads[n, :, :HD])
        q_rot = spin(q_unit * q_gain[...], co, si).astype(BF16)
        k_rot = spin(k_unit * k_gain[...], co, si).astype(BF16)
        scores = jnp.where(keep, dot(q_rot, k_rot, NT) * HD**-0.5, -1e30)
        weights = jnp.exp(scores - jnp.max(scores, axis=-1, keepdims=True))
        soft = weights / jnp.sum(weights, axis=-1, keepdims=True)
        probs[n] = soft
        value = dot(soft.astype(BF16), heads[n, :, HD:]).astype(BF16)
        out[:, n * HD : n * HD + HD] = value


SUMS = (
    ((1, 1), (3, 1), (0, 1), (3, 0)),
    ((2, 1), (2, 0), (1, 0)),
)


def rows_of(core, turned):
    slices = []
    for dy, dz in SUMS[core]:
        for dc in range(2):
            slices.append(slice((dc ^ turned) * 256 + dz * 128 + dy * 32, (dc ^ turned) * 256 + dz * 128 + dy * 32 + 32))
    slices += [slice(turned * 256, turned * 256 + 32)] * (9 - len(slices))
    return slices


def backward_kernel(place, *refs):
    blocks = refs[:9]
    w_out, q, s0, s1, s2, cosine, sine, advantage, q_gain, k_gain, probs, attended = refs[9:21]
    dq, keep, send, d0, d1, d2, gains, heads, whole, sems = refs[21:]
    pick_heads(place, (s0, s1, s2), heads)
    load_rows(place, blocks, whole, sems)
    grad_out = (dot(whole[...], w_out[...], NT) * advantage[:, 0:1]).astype(BF16)
    co, si = cosine[...], sine[...]
    q_sum = jnp.zeros((1, HD), F32)
    k_sum = jnp.zeros((1, HD), F32)
    d0[...] = jnp.zeros_like(d0)
    for n in range(2):
        cols = slice(n * HD, n * HD + HD)
        q_unit, q_scale = norm(q[:, cols])
        k_unit, k_scale = norm(heads[n, :, :HD])
        q_rot = spin(q_unit * q_gain[...], co, si).astype(BF16)
        k_rot = spin(k_unit * k_gain[...], co, si).astype(BF16)
        grad = grad_out[:, cols]
        delta = jnp.sum(
            grad.astype(F32) * attended[:, cols].astype(F32), axis=-1, keepdims=True
        )
        soft = probs[n]
        score = (soft * (dot(grad, heads[n, :, HD:], NT) - delta) * HD**-0.5).astype(BF16)
        e_q = spin_back(dot(score, k_rot), co, si)
        e_k = spin_back(dot(q_rot.T, score).T, co, si)
        grad_v = dot(grad.T, soft.astype(BF16)).T.astype(BF16)
        q_sum += jnp.sum(e_q * q_unit, axis=0, keepdims=True)
        k_sum += jnp.sum(e_k * k_unit, axis=0, keepdims=True)
        e_q = e_q * q_gain[...]
        e_k = e_k * k_gain[...]
        grad_q = q_scale * (e_q - q_unit * jnp.mean(e_q * q_unit, axis=-1, keepdims=True))
        grad_k = k_scale * (e_k - k_unit * jnp.mean(e_k * k_unit, axis=-1, keepdims=True))
        dq[:, cols] = grad_q.astype(BF16)
        both = jnp.concatenate([grad_k.astype(BF16), grad_v], axis=1)
        step = (2 * place[2] + n - place[0] + 4) % 4
        for s, slot in enumerate((d0, d1, d2, d1)):

            @pl.when(step == s)
            def _():
                slot[...] = both

    gains[...] = jnp.concatenate([q_sum, k_sum], axis=0)
    for core in range(2):

        @pl.when(place[2] == core)
        def _():
            keep[...] = jnp.concatenate([dq[at] for at in rows_of(core, 0)], axis=0)
            send[...] = jnp.concatenate([dq[at] for at in rows_of(1 - core, 1)], axis=0)


def plane_kernel(place, own, side, across, out):
    total = own[...].astype(F32) + turn_y(across[...], 2).astype(F32)
    home = place[0] // 2 == place[2]

    @pl.when(home)
    def _():
        out[...] = (total + turn_y(side[...], 3).astype(F32)).astype(BF16)

    @pl.when(jnp.logical_not(home))
    def _():
        out[...] = (total + turn_y(flip_c(side[...]), 1).astype(F32)).astype(BF16)


def pair_kernel(a, b, out):
    out[...] = (a[...].astype(F32) + flip_z(b[...]).astype(F32)).astype(BF16)


def columns_kernel(place, a, b, dq, right, rows_here):
    full = (a[...].astype(F32) + flip_c(b[...]).astype(F32)).astype(BF16)
    for core in range(2):

        @pl.when(place[2] == core)
        def _():
            some = [full[at] for at in rows_of(core, 0)]
            some = some[4:9] if core == 0 else some[2:7]
            rows_here[...] = jnp.concatenate(some, axis=0)

    right[:, :256] = dq[...]
    spot = place[1] * 2 + place[2]
    for n in range(4):

        @pl.when(spot == n)
        def _():
            right[:, 256:] = jnp.concatenate(
                [full[:, n * 32 : n * 32 + 32], full[:, HD + n * 32 : HD + n * 32 + 32]], axis=1
            )


def weight_kernel(place, *refs):
    if len(refs) == 17:
        blocks, (right, o0, o1, o2a, o2b, o3, whole, sems) = refs[:9], refs[9:]
    else:
        blocks, (right, w_q, w_kv, gain, o0, o1, o2a, o2b, o3, sums, whole, sems) = refs[:9], refs[9:]
    turned = right[...].T
    one = lax.broadcasted_iota(jnp.int32, (256, 256), 0)
    eye = jnp.where(one == lax.broadcasted_iota(jnp.int32, (256, 256), 1), 1.0, 0.0).astype(BF16)
    load_rows(place, blocks, whole, sems)
    for h in range(4):
        at = slice(h * 1280, h * 1280 + 1280)
        exact = dot(turned, whole[:, at])
        side = exact.astype(BF16)
        part = [dot(eye, side[:, i * 256 : i * 256 + 256], NT).astype(BF16) for i in range(5)]
        part = jnp.concatenate(part, axis=0)
        if len(refs) != 17:
            product = (part[:, :256].astype(F32) * w_q[at].astype(F32)).astype(BF16)
            total = dot(jnp.ones((8, 256), BF16), product, NT)[0:1]
            total += jnp.sum(exact[256:288] * w_kv[0, :, at].astype(F32), axis=0, keepdims=True)
            total += jnp.sum(exact[288:320] * w_kv[1, :, at].astype(F32), axis=0, keepdims=True)
            sums[:, at] = total / gain[:, at]
        k = (h - place[3] + 4) % 4
        for x in range(4):
            s = (x - place[4] + 4) % 4
            tile = part[x * 320 : x * 320 + 320]
            if right.shape[1] == 256:
                tile = jnp.concatenate([tile[:, :HD], tile[:, HD:]], axis=0)
            else:
                tile = jnp.concatenate(
                    [
                        tile[:, :HD],
                        tile[:, HD : 2 * HD],
                        jnp.concatenate([tile[:160, 2 * HD :], tile[160:, 2 * HD :]], axis=1),
                    ],
                    axis=0,
                )
            for at, out in ((0, o0), (1, o1), (3, o3)):

                @pl.when(s == at)
                def _():
                    out[k] = tile

            @pl.when((s == 2) & (k < 2))
            def _():
                o2a[jnp.minimum(k, 1)] = tile

            @pl.when((s == 2) & (k >= 2))
            def _():
                o2b[jnp.maximum(k - 2, 0)] = tile


def weight_grad(blocks, place, right, *more):
    rows = right.shape[1] * 320 // HD
    four, two = ((4, rows, HD), BF16), ((2, rows, HD), BF16)
    return call(
        weight_kernel,
        [four, four, two, two, four] + ([((1, D), F32)] if more else []),
        [place, *blocks, right, *more],
        PLACED + [VMEM] * (1 + len(more)),
        ROWS_SCRATCH,
    )


def around_kernel(o1, o3, a, b, right, left):
    right[0:2] = (o1[0:2].astype(F32) + a[...].astype(F32)).astype(BF16)
    right[2:4] = o1[2:4]
    left[0:2] = o3[0:2]
    left[2:4] = (o3[2:4].astype(F32) + b[...].astype(F32)).astype(BF16)


def meet_kernel(o0, r, s, gains, p0, p1, p2, p3, own):
    value = gains[...]
    high = value.astype(BF16)
    low = (value - high.astype(F32)).astype(BF16)
    own[...] = high.astype(F32) + low.astype(F32)
    for k, out in enumerate((p0, p1, p2, p3)):
        out[0:800] = (o0[k].astype(F32) + r[k].astype(F32) + s[k].astype(F32)).astype(BF16)
        out[800:848] = high
        out[848:896] = low


def reduce_first(parts):
    o0, o1, o2a, o2b, o3 = parts
    return o0, o1, o3, send_x(o2a, 1), send_x(o2b, -1)


def reduce_around(state):
    o0, o1, o3, a, b = state
    right, left = call(around_kernel, [(o1.shape, BF16)] * 2, [o1, o3, a, b])
    return o0, right, left


def reduce_second(state):
    o0, right, left = state
    return o0, send_x(right, 1), send_x(left, -1)


def halve_kernel(place, o0, r, s, here, near, far):
    def total(k):
        return (o0[k].astype(F32) + r[k].astype(F32) + s[k].astype(F32)).astype(BF16)

    here[...] = total(0)
    far[0:640] = total(2)
    for odd in range(2):

        @pl.when(place[3] % 2 == odd)
        def _():
            near[...] = total(3 if odd else 1)
            far[640:1280] = total(1 if odd else 3)


def reduce_third(state):
    p0, p1, p2, p3 = state
    return p0, send_h(p1, 1), send_h(p2, 2), send_h(p3, -1)


def reduce_last(state):
    zero, one, two, three = [part.astype(F32) for part in state]
    return (zero + two) + (one + three)


def first_kernel(mine, pair, one, two, m, p, s_m, s_p):
    copies = [
        pltpu.make_async_copy(mine.at[pl.ds(0, 128)], m, s_m),
        pltpu.make_async_copy(pair.at[pl.ds(0, 128)], p, s_p),
    ]
    for copy in copies:
        copy.start()
    for copy in copies:
        copy.wait()
    one[...] = (m[0:64].astype(F32) + p[0:64].astype(F32)).astype(BF16)
    two[...] = (m[64:128].astype(F32) + p[64:128].astype(F32)).astype(BF16)


def second_kernel(place, *refs):
    planes, (mine, pair, one, two, here, three, four, own, w_kv, sems, m, p, s_m, s_p) = refs[:4], refs[4:]
    copies = load_plane(place, planes, w_kv, sems)
    at = pl.ds(pl.multiple_of(128 - 64 * place[2], 32), 160)
    sides = [
        pltpu.make_async_copy(mine.at[at], m, s_m),
        pltpu.make_async_copy(pair.at[at], p, s_p),
    ]
    for copy in sides:
        copy.start()
    for copy in copies + sides:
        copy.wait()
    term = dot(here[...], w_kv[...])

    def both(at, size=64):
        return m[at : at + size].astype(F32) + p[at : at + size].astype(F32)

    own[...] = both(128, 32) + term[128:160]
    four[...] = (both(64) + term[64:128]).astype(BF16)

    @pl.when(place[2] == 0)
    def _():
        three[...] = (both(0) + one[...].astype(F32) + two[...].astype(F32)).astype(BF16)

    @pl.when(place[2] == 1)
    def _():
        three[...] = (both(0) + one[...].astype(F32) + term[0:64]).astype(BF16)


def third_kernel(three, four, out):
    out[...] = (three[32:64].astype(F32) + four[32:64].astype(F32)).astype(BF16)


def last_kernel(own, three, four, pair, x, gain, grad, advantage, out):
    total = own[...] + three[0:32].astype(F32) + four[0:32].astype(F32) + pair[...].astype(F32)
    value = x[...].astype(F32)
    scale = lax.rsqrt(jnp.mean(value * value, axis=-1, keepdims=True) + EPS)
    unit = value * scale
    weighted = total * gain[...]
    inner = weighted - unit * jnp.mean(weighted * unit, axis=-1, keepdims=True)
    scaled = (grad[...].astype(F32) * advantage[0:32, 0:1]).astype(BF16)
    out[...] = (scale * inner + scaled.astype(F32)).astype(BF16)


def normed_kernel(x, pair, gain, out):
    for n, ref in enumerate((x, pair)):
        unit, _ = norm(ref[...])
        out[n * 32 : n * 32 + 32] = (unit * gain[...]).astype(BF16)


def stack_kernel(x, pair, out):
    out[0:32] = x[...]
    out[32:64] = pair[...]


def tables_kernel(place, lengths, rewards, groups, inverse, sums, angle, marks):
    lane = lax.broadcasted_iota(jnp.int32, (1, HD), 1)
    count = jnp.zeros((1, HD), F32)
    first, second = count, count
    for n in range(8):
        hit = jnp.where(lane == groups[n], 1.0, 0.0)
        count += hit
        first += hit * rewards[n]
        second += hit * (rewards[n] * rewards[n])
    sums[...] = jnp.zeros_like(sums)
    sums[0:1], sums[1:2], sums[2:3] = count, first, second
    j = lax.broadcasted_iota(jnp.int32, (512, HD), 0)
    spot = (((place[0] + ((j >> 5) & 3)) & 3) << 2) + ((place[1] ^ ((j >> 7) & 1)) << 1)
    rows = ((spot + (place[2] ^ (j >> 8))) << 5) + (j & 31)
    end = lengths[0, 0]
    segment, start = jnp.zeros_like(rows), jnp.zeros_like(rows)
    for n in range(1, 8):
        segment = jnp.where(rows >= end, n, segment)
        start = jnp.where(rows >= end, end, start)
        end = end + lengths[0, n]
    angle[...] = (rows - start).astype(F32) * inverse[...]
    lane = lax.broadcasted_iota(jnp.int32, (512, HD), 1)
    marks[...] = jnp.where(lane == 0, segment, rows).astype(F32)


def advantage_kernel(rewards, groups, gathered, marks, out, held, sems):
    copies = [
        pltpu.make_async_copy(gathered.at[pl.ds(n * SUM_ROWS, 8)], held.at[n], sems.at[n])
        for n in range(16)
    ]
    for copy in copies:
        copy.start()
    for copy in copies:
        copy.wait()
    total = held[0]
    for n in range(1, 16):
        total += held[n]
    safe = jnp.maximum(total[0:1], 1.0)
    mean = total[1:2] / safe
    variance = total[2:3] / safe - mean * mean
    lane = lax.broadcasted_iota(jnp.int32, (1, HD), 1)
    segment = marks[:, 0:1]
    value = jnp.zeros((512, 1), F32)
    for n in range(8):
        hit = lane == groups[n]
        middle = jnp.sum(jnp.where(hit, mean, 0.0), axis=1, keepdims=True)
        spread = jnp.sum(jnp.where(hit, variance, 0.0), axis=1, keepdims=True)
        one = (rewards[n] - middle) / jnp.sqrt(spread + 1.0)
        value = jnp.where(segment == float(n), one, value)
    out[...] = jnp.broadcast_to(value, (512, HD))


def scale_kernel(a, advantage, out):
    out[...] = (a[...].astype(F32) * advantage[:, 0:1]).astype(BF16)


def on_device(
    inputs,
    upstream,
    w_query,
    w_key,
    w_value,
    w_output,
    norm_gain,
    query_gain,
    key_gain,
    lengths,
    rewards,
    groups,
):
    t_at = lax.axis_index("tensor")
    d_at = lax.axis_index("dp")
    y_at, z_at, c_at = t_at // 4, (t_at // 2) % 2, t_at % 2
    place = jnp.stack([y_at, z_at, c_at, d_at // 4, d_at % 4]).astype(jnp.int32)
    gain_row = norm_gain.reshape(1, D)

    inverse = ROPE_BASE ** (-(jnp.arange(HD // 2, dtype=F32) * 2.0 / HD))
    inverse = jnp.concatenate([inverse, inverse]).reshape(1, HD)
    sums, angle, marks = call(
        tables_kernel,
        [((SUM_ROWS, HD), F32), ((512, HD), F32), ((512, HD), F32)],
        [place, lengths, rewards, groups, inverse],
        [SMEM] * 4 + [VMEM],
    )
    gathered = lax.all_gather(sums, "dp", axis=0, tiled=True)
    inputs_pair, upstream_pair, angle, w_key, w_value = tie(
        swap_core(inputs), swap_core(upstream), angle, w_key, w_value
    )
    x_own = call(normed_kernel, ((64, D), BF16), [inputs, inputs_pair, gain_row])

    x_own, w_key, w_value, upstream_pair, angle = tie(x_own, w_key, w_value, upstream_pair, angle)
    x_mid, x_side = gather_one(x_own)
    w_own = jnp.stack([w_key.T, w_value.T])
    w_pair, w_far = swap_core(w_own), swap_z(w_own)
    g_own = call(stack_kernel, ((64, D), BF16), [upstream, upstream_pair])
    cosine, sine = jnp.cos(angle), jnp.sin(angle)
    sine = jnp.where(jnp.arange(HD)[None, :] < HD // 2, -sine, sine)
    x_mid, x_side, w_pair, g_own, cosine, sine = tie(x_mid, x_side, w_pair, g_own, cosine, sine)
    x_far, x_last = gather_two(x_side)
    x_mid_pair, x_side_pair = swap_core(x_mid), swap_core(x_side)
    x_far, x_last, x_mid_pair, x_side_pair, w_far, g_own = tie(
        x_far, x_last, x_mid_pair, x_side_pair, w_far, g_own
    )
    g_mid, g_side = gather_one(g_own)
    planes = [w_own, w_pair, w_far, swap_core(w_far)]
    x_blocks = [
        x_mid, x_mid_pair, x_side, x_side_pair, x_far, swap_core(x_far), x_last, swap_last(x_last), x_own
    ]
    query_proj, kv = project(place, x_blocks, planes, w_query)
    query_proj, kv, g_mid, g_side = tie(query_proj, kv, g_mid, g_side)

    g_far, g_last = gather_two(g_side)
    slots = [kv, lax.ppermute(kv, "tensor", KV_BESIDE), lax.ppermute(kv, "tensor", KV_ACROSS)]
    *slots, g_mid, g_side, gathered = tie(*slots, g_mid, g_side, gathered)
    advantage = call(
        advantage_kernel,
        ((512, HD), F32),
        [rewards, groups, gathered, marks],
        [SMEM, SMEM, ANY, VMEM],
        (pltpu.VMEM((16, 8, HD), F32), pltpu.SemaphoreType.DMA((16,))),
    )
    g_mid_pair, g_side_pair = swap_core(g_mid), swap_core(g_side)
    q_row, k_row = query_gain.reshape(1, HD), key_gain.reshape(1, HD)
    attended, probs = call(
        forward_kernel,
        [((512, 256), BF16), ((2, 512, 512), F32)],
        [place, query_proj, *slots, cosine, sine, marks, q_row, k_row],
        [SMEM] + [VMEM] * 9,
        (pltpu.VMEM((2, 512, 256), BF16),),
    )
    scaled = call(scale_kernel, ((512, 256), BF16), [attended, advantage])
    g_far, g_last, g_mid_pair, g_side_pair, attended, scaled, probs, advantage = tie(
        g_far, g_last, g_mid_pair, g_side_pair, attended, scaled, probs, advantage
    )
    g_blocks = [
        g_mid, g_mid_pair, g_side, g_side_pair, g_far, swap_core(g_far), g_last, swap_last(g_last), g_own
    ]
    parts = weight_grad(g_blocks, place, scaled)
    *parts, probs = tie(*parts, probs)
    out_state = reduce_first(parts)
    dq, keep, send, d0, d1, d2, head_gains = call(
        backward_kernel,
        [((512, 256), BF16), ((288, 256), BF16), ((288, 256), BF16)]
        + [((512, 256), BF16)] * 3
        + [((2, HD), F32)],
        [place, *g_blocks, w_output, query_proj, *slots, cosine, sine, advantage, q_row, k_row, probs, attended],
        PLACED + [VMEM] * 12,
        (pltpu.VMEM((2, 512, 256), BF16), *ROWS_SCRATCH),
    )
    dq, keep, send, d0, d1, d2, *out_state = tie(dq, keep, send, d0, d1, d2, *out_state)
    d1, d2 = lax.ppermute(d1, "tensor", DKV_BESIDE), lax.ppermute(d2, "tensor", DKV_ACROSS)
    out_state = reduce_second(reduce_around(out_state))

    back = lambda rows: dot(rows, w_query, NT).astype(BF16)
    other, mine = back(send), back(keep)
    other, mine, d0, d1, d2 = tie(other, mine, d0, d1, d2)
    pair = swap_core(other)
    dkv = call(plane_kernel, ((512, 256), BF16), [place, d0, d1, d2], [SMEM] + [VMEM] * 3)
    dkv_pair = swap_z(dkv)
    one, two = call(
        first_kernel,
        [((64, D), BF16)] * 2,
        [mine, pair],
        [ANY] * 2,
        (pltpu.VMEM((128, D), BF16),) * 2 + (pltpu.SemaphoreType.DMA(()),) * 2,
    )
    dkv, dkv_pair, one, two, *out_state = tie(dkv, dkv_pair, one, two, *out_state)
    dkv = call(pair_kernel, ((512, 256), BF16), [dkv, dkv_pair])
    dkv_pair = swap_core(dkv)
    one = lax.ppermute(one, "tensor", by_core(UP, OTHER))
    two = lax.ppermute(two, "tensor", by_core(DOWN, None))
    out_here, out_near, out_far = call(
        halve_kernel,
        [((640, HD), BF16), ((640, HD), BF16), ((1280, HD), BF16)],
        [place, *out_state],
        [SMEM] + [VMEM] * 3,
    )
    out_far = swap_h(out_far, 2)
    dkv, dkv_pair = tie(dkv, dkv_pair)
    combined, rows_here = call(
        columns_kernel,
        [((512, 320), BF16), ((160, 256), BF16)],
        [place, dkv, dkv_pair, dq],
        [SMEM] + [VMEM] * 3,
    )
    *parts, norm_sums = weight_grad(x_blocks, place, combined, w_query, w_own, gain_row)
    *parts, one, two, norm_sums, out_near, out_far = tie(
        *parts, one, two, norm_sums, out_near, out_far
    )
    state = reduce_first(parts)
    out_near = (out_near.astype(F32) + out_far[640:].astype(F32)).astype(BF16)
    out_near = swap_h(out_near, 1)
    gains = jnp.concatenate([norm_sums.reshape(40, HD), head_gains, jnp.zeros((6, HD), F32)])
    gains = gains + swap_core(gains)
    gains = gains + swap_z(gains)
    three, four, own = call(
        second_kernel,
        [((64, D), BF16), ((64, D), BF16), ((32, D), F32)],
        [place, *planes, mine, pair, one, two, rows_here],
        [SMEM] + [ANY] * 6 + [VMEM] * 3,
        (
            *PLANE_SCRATCH,
            pltpu.VMEM((160, D), BF16),
            pltpu.VMEM((160, D), BF16),
            pltpu.SemaphoreType.DMA(()),
            pltpu.SemaphoreType.DMA(()),
        ),
    )
    *state, three, four, gains = tie(*state, three, four, gains)

    three = lax.ppermute(three, "tensor", by_core(OTHER, ACROSS))
    four = lax.ppermute(four, "tensor", by_core(DOWN, UP))
    state = reduce_second(reduce_around(state))
    three, four, out_near, gains = tie(three, four, out_near, gains)
    pair = swap_core(call(third_kernel, ((32, D), BF16), [three, four]))
    input_grad = call(
        last_kernel,
        ((32, D), BF16),
        [own, three, four, pair, inputs, gain_row, upstream, advantage],
    )
    gains = total4(total4(gains, swap_y), swap_x)
    *state, gains, input_grad = tie(*state, gains, input_grad)
    *state, gains = call(
        meet_kernel,
        [((896, HD), BF16)] * 4 + [((48, HD), F32)],
        [*state, gains],
    )
    state = reduce_third(state)
    gains = [gains] + [part[800:848].astype(F32) + part[848:].astype(F32) for part in state[1:]]
    gains = ((gains[0] + gains[2]) + (gains[1] + gains[3])).reshape(-1)
    state = [part[:800] for part in state]
    out_grads = out_here.astype(F32) + out_far[:640].astype(F32) + out_near.astype(F32)
    grads = reduce_last(state)
    last = grads[640:]
    return (
        input_grad,
        jnp.concatenate([grads[:320], grads[320:640]], axis=1),
        jnp.concatenate([last[:, :32], last[:, 64:96]], axis=0),
        jnp.concatenate([last[:, 32:64], last[:, 96:]], axis=0),
        jnp.concatenate([out_grads[:320], out_grads[320:]], axis=1),
        gains[:D],
        gains[D : D + HD],
        gains[D + HD : D + 2 * HD],
    )


def solution(mesh):
    in_specs = (
        P(("dp", "tensor"), None),
        P(("dp", "tensor"), None),
        P(None, "tensor"),
        P(None, "tensor"),
        P(None, "tensor"),
        P("tensor", None),
        P(),
        P(),
        P(),
        P("dp", None),
        P("dp"),
        P("dp"),
    )
    out_specs = (
        P(("dp", "tensor"), None),
        P("dp", "tensor"),
        P("dp", "tensor"),
        P("dp", "tensor"),
        P("dp", "tensor"),
        P(),
        P(),
        P(),
    )
    return jax.shard_map(
        on_device, mesh=mesh, in_specs=in_specs, out_specs=out_specs, check_vma=False
    )
```

```python
import functools

import jax
import jax.numpy as jnp
from jax import lax
from jax.experimental import pallas as pl
from jax.experimental.pallas import tpu as pltpu
from jax.sharding import PartitionSpec as P

KVH = 4
GROUPS = 16
HD = 128
EPS = 1e-06
ROPE_BASE = 1000000.0


F32 = jnp.float32
BF16 = jnp.bfloat16


def t_pairs(move, keep=None):
    pairs = []
    for y in range(4):
        for z in range(2):
            for c in range(2):
                if keep is None or keep(y, z, c):
                    a, b, d = move(y, z, c)
                    pairs.append((y * 4 + z * 2 + c, (a % 4) * 4 + b * 2 + d))
    return pairs


def send_y(value, step, keep=None):
    return lax.ppermute(value, "tensor", t_pairs(lambda y, z, c: (y + step, z, c), keep))


def swap_y(value, bits):
    return lax.ppermute(value, "tensor", t_pairs(lambda y, z, c: (y ^ bits, z, c)))


def swap_z(value):
    return lax.ppermute(value, "tensor", t_pairs(lambda y, z, c: (y, 1 - z, c)))


def swap_core(value):
    return lax.ppermute(value, "tensor", t_pairs(lambda y, z, c: (y, z, 1 - c)))


def send_x(value, step):
    return lax.ppermute(
        value, "dp", [(h * 4 + x, h * 4 + (x + step) % 4) for h in range(4) for x in range(4)]
    )


def send_h(value, step):
    return lax.ppermute(
        value, "dp", [(h * 4 + x, ((h + step) % 4) * 4 + x) for h in range(4) for x in range(4)]
    )


def swap_x(value, bits):
    return lax.ppermute(
        value, "dp", [(h * 4 + x, h * 4 + (x ^ bits)) for h in range(4) for x in range(4)]
    )


def swap_h(value, bits):
    return lax.ppermute(
        value, "dp", [(h * 4 + x, (h ^ bits) * 4 + x) for h in range(4) for x in range(4)]
    )


def total4(value, swap):
    one, two, three = swap(value, 1), swap(value, 2), swap(value, 3)
    return (value + one) + (two + three)


def tie(*values):
    return lax.optimization_barrier(values)


VMEM = pl.BlockSpec(memory_space=pltpu.VMEM)
SMEM = pl.BlockSpec(memory_space=pltpu.SMEM)
ANY = pl.BlockSpec(memory_space=pl.ANY)
NT = (((1,), (1,)), ((), ()))
TN = (((0,), (0,)), ((), ()))
D = 5120
SUM_ROWS = 256


def dot(a, b, dims=(((1,), (0,)), ((), ()))):
    return lax.dot_general(a, b, dims, preferred_element_type=F32)


def call(kernel, out, args, specs=None, scratch=(), limit=12):
    many = isinstance(out, list)
    shapes = [jax.ShapeDtypeStruct(s, t) for s, t in (out if many else [out])]
    result = pl.pallas_call(
        kernel,
        out_shape=shapes,
        in_specs=list(specs) if specs else [VMEM] * len(args),
        out_specs=[VMEM] * len(shapes),
        scratch_shapes=list(scratch),
        compiler_params=pltpu.CompilerParams(vmem_limit_bytes=limit * 2**20),
        cost_estimate=pl.CostEstimate(flops=1, bytes_accessed=1, transcendentals=0),
    )(*args)
    return result if many else result[0]


def load_rows(place, blocks, whole, sems):
    mid, mid_pair, side, side_pair, far, far_pair, last, last_pair, own = blocks
    core = place[2]

    def pick(zero, one):
        return zero + (one - zero) * core

    plan = [
        (own, 0, 0),
        (mid, pick(96, 32), 0),
        (mid_pair, pick(32, 96), 1),
        (side, pick(128, 64), 0),
        (side_pair, pick(64, 128), 1),
        (far, pick(224, 192), 0),
        (far_pair, pick(192, 224), 1),
    ]
    copies = []
    for n, (block, base, turned) in enumerate(plan):
        for half in range(2):
            at = pl.multiple_of(base + 256 * (half ^ turned), 32)
            copies.append(
                pltpu.make_async_copy(
                    block.at[pl.ds(half * 32, 32)], whole.at[pl.ds(at, 32)], sems.at[2 * n + half]
                )
            )
    for half in range(2):
        for n, (block, turned) in enumerate(((last, 0), (last_pair, 1))):
            copy = pltpu.make_async_copy(
                block.at[pl.ds(half * 32, 32)],
                whole.at[pl.ds(160 + 256 * (half ^ turned), 32)],
                sems.at[14 + half],
            )

            @pl.when(core == n)
            def _():
                copy.start()

    for copy in copies:
        copy.start()
    for copy in copies:
        copy.wait()
    for half in range(2):
        pltpu.make_async_copy(
            last.at[pl.ds(half * 32, 32)], whole.at[pl.ds(160, 32)], sems.at[14 + half]
        ).wait()


def load_plane(place, parts, w_kv, sems):
    copies = []
    for n, part in enumerate(parts):
        z, core = place[1] ^ (n // 2), place[2] ^ (n % 2)
        for kind in range(2):
            at = pl.multiple_of(kind * HD + z * 64 + core * 32, 32)
            copies.append(
                pltpu.make_async_copy(part.at[kind], w_kv.at[pl.ds(at, 32)], sems.at[2 * n + kind])
            )
    for copy in copies:
        copy.start()
    return copies


PLANE_SCRATCH = (pltpu.VMEM((256, D), BF16), pltpu.SemaphoreType.DMA((8,)))
ROWS_SCRATCH = (pltpu.VMEM((512, D), BF16), pltpu.SemaphoreType.DMA((16,)))
PLACED = [SMEM] + [ANY] * 9


def by_core(zero, one):
    pairs = []
    for y in range(4):
        for z in range(2):
            for c, move in enumerate((zero, one)):
                if move is not None:
                    a, b = move(y, z)
                    pairs.append((y * 4 + z * 2 + c, (a % 4) * 4 + b * 2 + c))
    return pairs


UP = lambda y, z: (y + 1, z)
DOWN = lambda y, z: (y - 1, z)
ACROSS = lambda y, z: (y + 2, z)
OTHER = lambda y, z: (y, 1 - z)


def gather_one(own):
    mid = lax.ppermute(own, "tensor", by_core(UP, DOWN))
    side = lax.ppermute(own, "tensor", by_core(OTHER, ACROSS))
    return mid, side


def gather_two(side):
    far = lax.ppermute(side, "tensor", by_core(UP, OTHER))
    last = lax.ppermute(side, "tensor", by_core(DOWN, None))
    return far, last


def kv_pairs(beside, back):
    pairs = []
    for y in range(4):
        for z in range(2):
            e = y // 2
            ways = [(y + 1, e), (y - 1, 1 - e)] if beside else [(y + 2, e)]
            for to, via in ways:
                here, there = y * 4 + z * 2 + via, (to % 4) * 4 + z * 2 + e
                pairs.append((there, here) if back else (here, there))
    return pairs


KV_BESIDE, KV_ACROSS = kv_pairs(True, False), kv_pairs(False, False)
DKV_BESIDE, DKV_ACROSS = kv_pairs(True, True), kv_pairs(False, True)


def swap_last(value):
    return lax.ppermute(value, "tensor", [(t, t + 1) for t in range(0, 16, 2)])


def project_kernel(place, *refs):
    blocks, planes, (w_q, q_out, kv_out, whole, sems, w_kv, w_sems) = refs[:9], refs[9:13], refs[13:]
    copies = load_plane(place, planes, w_kv, w_sems)
    load_rows(place, blocks, whole, sems)
    q_out[...] = dot(whole[...], w_q[...]).astype(BF16)
    for copy in copies:
        copy.wait()
    kv_out[...] = dot(whole[...], w_kv[...], NT).astype(BF16)


def project(place, blocks, planes, w_q):
    return call(
        project_kernel,
        [((512, 256), BF16), ((512, 256), BF16)],
        [place, *blocks, *planes, w_q],
        PLACED + [ANY] * 4 + [VMEM],
        (*ROWS_SCRATCH, *PLANE_SCRATCH),
        24,
    )


def flip_z(value):
    return jnp.concatenate([value[128:256], value[:128], value[384:], value[256:384]], axis=0)


def flip_c(value):
    return jnp.concatenate([value[256:], value[:256]], axis=0)


def turn_y(value, step):
    if step % 4 == 0:
        return value
    parts = []
    for group in range(4):
        for dy in range(4):
            at = group * 128 + ((dy + step) % 4) * 32
            parts.append(value[at : at + 32])
    return jnp.concatenate(parts, axis=0)


def pick_heads(place, slots, heads):
    own, side, across = slots
    for n in range(2):
        step = (2 * place[2] + n - place[0] + 4) % 4
        for s, slot in enumerate((own, side, across, side)):

            @pl.when(step == s)
            def _():
                value = flip_c(slot[...]) if s == 1 else slot[...]
                heads[n] = turn_y(value, -s)


def spin(value, cosine, sine):
    return value * cosine + pltpu.roll(value, 64, 1) * sine


def spin_back(grad, cosine, sine):
    return grad * cosine - pltpu.roll(grad, 64, 1) * sine


def norm(value):
    value = value.astype(F32)
    scale = lax.rsqrt(jnp.mean(value * value, axis=-1, keepdims=True) + EPS)
    return value * scale, scale


def forward_kernel(
    place, q, s0, s1, s2, cosine, sine, seg, q_gain, k_gain, out, probs, heads
):
    pick_heads(place, (s0, s1, s2), heads)
    co, si = cosine[...], sine[...]
    seg_q, row_q = seg[:, 0:1], seg[:, 1:2]
    turned = seg[...].T
    keep = (seg_q == turned[0:1]) & (row_q >= turned[1:2])
    for n in range(2):
        q_unit, _ = norm(q[:, n * HD : n * HD + HD])
        k_unit, _ = norm(heads[n, :, :HD])
        q_rot = spin(q_unit * q_gain[...], co, si).astype(BF16)
        k_rot = spin(k_unit * k_gain[...], co, si).astype(BF16)
        scores = jnp.where(keep, dot(q_rot, k_rot, NT) * HD**-0.5, -1e30)
        weights = jnp.exp(scores - jnp.max(scores, axis=-1, keepdims=True))
        soft = weights / jnp.sum(weights, axis=-1, keepdims=True)
        probs[n] = soft
        value = dot(soft.astype(BF16), heads[n, :, HD:]).astype(BF16)
        out[:, n * HD : n * HD + HD] = value


SUMS = (
    ((1, 1), (3, 1), (0, 1), (3, 0)),
    ((2, 1), (2, 0), (1, 0)),
)


def rows_of(core, turned):
    slices = []
    for dy, dz in SUMS[core]:
        for dc in range(2):
            slices.append(slice((dc ^ turned) * 256 + dz * 128 + dy * 32, (dc ^ turned) * 256 + dz * 128 + dy * 32 + 32))
    slices += [slice(turned * 256, turned * 256 + 32)] * (9 - len(slices))
    return slices


def backward_kernel(place, *refs):
    blocks = refs[:9]
    w_out, q, s0, s1, s2, cosine, sine, advantage, q_gain, k_gain, probs, attended = refs[9:21]
    dq, keep, send, d0, d1, d2, gains, heads, whole, sems = refs[21:]
    pick_heads(place, (s0, s1, s2), heads)
    load_rows(place, blocks, whole, sems)
    grad_out = (dot(whole[...], w_out[...], NT) * advantage[:, 0:1]).astype(BF16)
    co, si = cosine[...], sine[...]
    q_sum = jnp.zeros((1, HD), F32)
    k_sum = jnp.zeros((1, HD), F32)
    d0[...] = jnp.zeros_like(d0)
    for n in range(2):
        cols = slice(n * HD, n * HD + HD)
        q_unit, q_scale = norm(q[:, cols])
        k_unit, k_scale = norm(heads[n, :, :HD])
        q_rot = spin(q_unit * q_gain[...], co, si).astype(BF16)
        k_rot = spin(k_unit * k_gain[...], co, si).astype(BF16)
        grad = grad_out[:, cols]
        delta = jnp.sum(
            grad.astype(F32) * attended[:, cols].astype(F32), axis=-1, keepdims=True
        )
        soft = probs[n]
        score = (soft * (dot(grad, heads[n, :, HD:], NT) - delta) * HD**-0.5).astype(BF16)
        e_q = spin_back(dot(score, k_rot), co, si)
        e_k = spin_back(dot(q_rot.T, score).T, co, si)
        grad_v = dot(grad.T, soft.astype(BF16)).T.astype(BF16)
        q_sum += jnp.sum(e_q * q_unit, axis=0, keepdims=True)
        k_sum += jnp.sum(e_k * k_unit, axis=0, keepdims=True)
        e_q = e_q * q_gain[...]
        e_k = e_k * k_gain[...]
        grad_q = q_scale * (e_q - q_unit * jnp.mean(e_q * q_unit, axis=-1, keepdims=True))
        grad_k = k_scale * (e_k - k_unit * jnp.mean(e_k * k_unit, axis=-1, keepdims=True))
        dq[:, cols] = grad_q.astype(BF16)
        both = jnp.concatenate([grad_k.astype(BF16), grad_v], axis=1)
        step = (2 * place[2] + n - place[0] + 4) % 4
        for s, slot in enumerate((d0, d1, d2, d1)):

            @pl.when(step == s)
            def _():
                slot[...] = both

    gains[...] = jnp.concatenate([q_sum, k_sum], axis=0)
    for core in range(2):

        @pl.when(place[2] == core)
        def _():
            keep[...] = jnp.concatenate([dq[at] for at in rows_of(core, 0)], axis=0)
            send[...] = jnp.concatenate([dq[at] for at in rows_of(1 - core, 1)], axis=0)


def plane_kernel(place, own, side, across, out):
    total = own[...].astype(F32) + turn_y(across[...], 2).astype(F32)
    home = place[0] // 2 == place[2]

    @pl.when(home)
    def _():
        out[...] = (total + turn_y(side[...], 3).astype(F32)).astype(BF16)

    @pl.when(jnp.logical_not(home))
    def _():
        out[...] = (total + turn_y(flip_c(side[...]), 1).astype(F32)).astype(BF16)


def pair_kernel(a, b, out):
    out[...] = (a[...].astype(F32) + flip_z(b[...]).astype(F32)).astype(BF16)


def columns_kernel(place, a, b, dq, right, rows_here):
    full = (a[...].astype(F32) + flip_c(b[...]).astype(F32)).astype(BF16)
    for core in range(2):

        @pl.when(place[2] == core)
        def _():
            some = [full[at] for at in rows_of(core, 0)]
            some = some[4:9] if core == 0 else some[2:7]
            rows_here[...] = jnp.concatenate(some, axis=0)

    right[:, :256] = dq[...]
    spot = place[1] * 2 + place[2]
    for n in range(4):

        @pl.when(spot == n)
        def _():
            right[:, 256:] = jnp.concatenate(
                [full[:, n * 32 : n * 32 + 32], full[:, HD + n * 32 : HD + n * 32 + 32]], axis=1
            )


def weight_kernel(place, *refs):
    if len(refs) == 17:
        blocks, (right, o0, o1, o2a, o2b, o3, whole, sems) = refs[:9], refs[9:]
    else:
        blocks, (right, w_q, w_kv, gain, o0, o1, o2a, o2b, o3, sums, whole, sems) = refs[:9], refs[9:]
    turned = right[...].T
    one = lax.broadcasted_iota(jnp.int32, (256, 256), 0)
    eye = jnp.where(one == lax.broadcasted_iota(jnp.int32, (256, 256), 1), 1.0, 0.0).astype(BF16)
    load_rows(place, blocks, whole, sems)
    for h in range(4):
        at = slice(h * 1280, h * 1280 + 1280)
        exact = dot(turned, whole[:, at])
        side = exact.astype(BF16)
        part = [dot(eye, side[:, i * 256 : i * 256 + 256], NT).astype(BF16) for i in range(5)]
        part = jnp.concatenate(part, axis=0)
        if len(refs) != 17:
            product = (part[:, :256].astype(F32) * w_q[at].astype(F32)).astype(BF16)
            total = dot(jnp.ones((8, 256), BF16), product, NT)[0:1]
            total += jnp.sum(exact[256:288] * w_kv[0, :, at].astype(F32), axis=0, keepdims=True)
            total += jnp.sum(exact[288:320] * w_kv[1, :, at].astype(F32), axis=0, keepdims=True)
            sums[:, at] = total / gain[:, at]
        k = (h - place[3] + 4) % 4
        for x in range(4):
            s = (x - place[4] + 4) % 4
            tile = part[x * 320 : x * 320 + 320]
            if right.shape[1] == 256:
                tile = jnp.concatenate([tile[:, :HD], tile[:, HD:]], axis=0)
            else:
                tile = jnp.concatenate(
                    [
                        tile[:, :HD],
                        tile[:, HD : 2 * HD],
                        jnp.concatenate([tile[:160, 2 * HD :], tile[160:, 2 * HD :]], axis=1),
                    ],
                    axis=0,
                )
            for at, out in ((0, o0), (1, o1), (3, o3)):

                @pl.when(s == at)
                def _():
                    out[k] = tile

            @pl.when((s == 2) & (k < 2))
            def _():
                o2a[jnp.minimum(k, 1)] = tile

            @pl.when((s == 2) & (k >= 2))
            def _():
                o2b[jnp.maximum(k - 2, 0)] = tile


def weight_grad(blocks, place, right, *more):
    rows = right.shape[1] * 320 // HD
    four, two = ((4, rows, HD), BF16), ((2, rows, HD), BF16)
    return call(
        weight_kernel,
        [four, four, two, two, four] + ([((1, D), F32)] if more else []),
        [place, *blocks, right, *more],
        PLACED + [VMEM] * (1 + len(more)),
        ROWS_SCRATCH,
        32,
    )


def around_kernel(o1, o3, a, b, right, left):
    right[0:2] = (o1[0:2].astype(F32) + a[...].astype(F32)).astype(BF16)
    right[2:4] = o1[2:4]
    left[0:2] = o3[0:2]
    left[2:4] = (o3[2:4].astype(F32) + b[...].astype(F32)).astype(BF16)


def meet_kernel(o0, r, s, gains, p0, p1, p2, p3, own):
    value = gains[...]
    high = value.astype(BF16)
    low = (value - high.astype(F32)).astype(BF16)
    own[...] = high.astype(F32) + low.astype(F32)
    for k, out in enumerate((p0, p1, p2, p3)):
        out[0:800] = (o0[k].astype(F32) + r[k].astype(F32) + s[k].astype(F32)).astype(BF16)
        out[800:848] = high
        out[848:896] = low


def reduce_first(parts):
    o0, o1, o2a, o2b, o3 = parts
    return o0, o1, o3, send_x(o2a, 1), send_x(o2b, -1)


def reduce_around(state):
    o0, o1, o3, a, b = state
    right, left = call(around_kernel, [(o1.shape, BF16)] * 2, [o1, o3, a, b])
    return o0, right, left


def reduce_second(state):
    o0, right, left = state
    return o0, send_x(right, 1), send_x(left, -1)


def halve_kernel(place, o0, r, s, here, near, far):
    def total(k):
        return (o0[k].astype(F32) + r[k].astype(F32) + s[k].astype(F32)).astype(BF16)

    here[...] = total(0)
    far[0:640] = total(2)
    for odd in range(2):

        @pl.when(place[3] % 2 == odd)
        def _():
            near[...] = total(3 if odd else 1)
            far[640:1280] = total(1 if odd else 3)


def reduce_third(state):
    p0, p1, p2, p3 = state
    return p0, send_h(p1, 1), send_h(p2, 2), send_h(p3, -1)


def reduce_last(state):
    zero, one, two, three = [part.astype(F32) for part in state]
    return (zero + two) + (one + three)


def first_kernel(mine, pair, one, two, m, p, s_m, s_p):
    copies = [
        pltpu.make_async_copy(mine.at[pl.ds(0, 128)], m, s_m),
        pltpu.make_async_copy(pair.at[pl.ds(0, 128)], p, s_p),
    ]
    for copy in copies:
        copy.start()
    for copy in copies:
        copy.wait()
    one[...] = (m[0:64].astype(F32) + p[0:64].astype(F32)).astype(BF16)
    two[...] = (m[64:128].astype(F32) + p[64:128].astype(F32)).astype(BF16)


def second_kernel(place, *refs):
    planes, (mine, pair, one, two, here, three, four, own, w_kv, sems, m, p, s_m, s_p) = refs[:4], refs[4:]
    copies = load_plane(place, planes, w_kv, sems)
    at = pl.ds(pl.multiple_of(128 - 64 * place[2], 32), 160)
    sides = [
        pltpu.make_async_copy(mine.at[at], m, s_m),
        pltpu.make_async_copy(pair.at[at], p, s_p),
    ]
    for copy in sides:
        copy.start()
    for copy in copies + sides:
        copy.wait()
    term = dot(here[...], w_kv[...])

    def both(at, size=64):
        return m[at : at + size].astype(F32) + p[at : at + size].astype(F32)

    own[...] = both(128, 32) + term[128:160]
    four[...] = (both(64) + term[64:128]).astype(BF16)

    @pl.when(place[2] == 0)
    def _():
        three[...] = (both(0) + one[...].astype(F32) + two[...].astype(F32)).astype(BF16)

    @pl.when(place[2] == 1)
    def _():
        three[...] = (both(0) + one[...].astype(F32) + term[0:64]).astype(BF16)


def third_kernel(three, four, out):
    out[...] = (three[32:64].astype(F32) + four[32:64].astype(F32)).astype(BF16)


def last_kernel(own, three, four, pair, x, gain, grad, advantage, out):
    total = own[...] + three[0:32].astype(F32) + four[0:32].astype(F32) + pair[...].astype(F32)
    value = x[...].astype(F32)
    scale = lax.rsqrt(jnp.mean(value * value, axis=-1, keepdims=True) + EPS)
    unit = value * scale
    weighted = total * gain[...]
    inner = weighted - unit * jnp.mean(weighted * unit, axis=-1, keepdims=True)
    scaled = (grad[...].astype(F32) * advantage[0:32, 0:1]).astype(BF16)
    out[...] = (scale * inner + scaled.astype(F32)).astype(BF16)


def normed_kernel(x, pair, gain, out):
    for n, ref in enumerate((x, pair)):
        unit, _ = norm(ref[...])
        out[n * 32 : n * 32 + 32] = (unit * gain[...]).astype(BF16)


def stack_kernel(x, pair, out):
    out[0:32] = x[...]
    out[32:64] = pair[...]


def tables_kernel(place, lengths, rewards, groups, inverse, sums, angle, marks):
    lane = lax.broadcasted_iota(jnp.int32, (1, HD), 1)
    count = jnp.zeros((1, HD), F32)
    first, second = count, count
    for n in range(8):
        hit = jnp.where(lane == groups[n], 1.0, 0.0)
        count += hit
        first += hit * rewards[n]
        second += hit * (rewards[n] * rewards[n])
    sums[...] = jnp.zeros_like(sums)
    sums[0:1], sums[1:2], sums[2:3] = count, first, second
    j = lax.broadcasted_iota(jnp.int32, (512, HD), 0)
    spot = (((place[0] + ((j >> 5) & 3)) & 3) << 2) + ((place[1] ^ ((j >> 7) & 1)) << 1)
    rows = ((spot + (place[2] ^ (j >> 8))) << 5) + (j & 31)
    end = lengths[0, 0]
    segment, start = jnp.zeros_like(rows), jnp.zeros_like(rows)
    for n in range(1, 8):
        segment = jnp.where(rows >= end, n, segment)
        start = jnp.where(rows >= end, end, start)
        end = end + lengths[0, n]
    angle[...] = (rows - start).astype(F32) * inverse[...]
    lane = lax.broadcasted_iota(jnp.int32, (512, HD), 1)
    marks[...] = jnp.where(lane == 0, segment, rows).astype(F32)


def advantage_kernel(rewards, groups, gathered, marks, out, held, sems):
    copies = [
        pltpu.make_async_copy(gathered.at[pl.ds(n * SUM_ROWS, 8)], held.at[n], sems.at[n])
        for n in range(16)
    ]
    for copy in copies:
        copy.start()
    for copy in copies:
        copy.wait()
    total = held[0]
    for n in range(1, 16):
        total += held[n]
    safe = jnp.maximum(total[0:1], 1.0)
    mean = total[1:2] / safe
    variance = total[2:3] / safe - mean * mean
    lane = lax.broadcasted_iota(jnp.int32, (1, HD), 1)
    segment = marks[:, 0:1]
    value = jnp.zeros((512, 1), F32)
    for n in range(8):
        hit = lane == groups[n]
        middle = jnp.sum(jnp.where(hit, mean, 0.0), axis=1, keepdims=True)
        spread = jnp.sum(jnp.where(hit, variance, 0.0), axis=1, keepdims=True)
        one = (rewards[n] - middle) / jnp.sqrt(spread + 1.0)
        value = jnp.where(segment == float(n), one, value)
    out[...] = jnp.broadcast_to(value, (512, HD))


def scale_kernel(a, advantage, out):
    out[...] = (a[...].astype(F32) * advantage[:, 0:1]).astype(BF16)


def on_device(
    inputs,
    upstream,
    w_query,
    w_key,
    w_value,
    w_output,
    norm_gain,
    query_gain,
    key_gain,
    lengths,
    rewards,
    groups,
):
    t_at = lax.axis_index("tensor")
    d_at = lax.axis_index("dp")
    y_at, z_at, c_at = t_at // 4, (t_at // 2) % 2, t_at % 2
    place = jnp.stack([y_at, z_at, c_at, d_at // 4, d_at % 4]).astype(jnp.int32)
    gain_row = norm_gain.reshape(1, D)

    inverse = ROPE_BASE ** (-(jnp.arange(HD // 2, dtype=F32) * 2.0 / HD))
    inverse = jnp.concatenate([inverse, inverse]).reshape(1, HD)
    sums, angle, marks = call(
        tables_kernel,
        [((SUM_ROWS, HD), F32), ((512, HD), F32), ((512, HD), F32)],
        [place, lengths, rewards, groups, inverse],
        [SMEM] * 4 + [VMEM],
    )
    gathered = lax.all_gather(sums, "dp", axis=0, tiled=True)
    inputs_pair, upstream_pair, angle, w_key, w_value = tie(
        swap_core(inputs), swap_core(upstream), angle, w_key, w_value
    )
    x_own = call(normed_kernel, ((64, D), BF16), [inputs, inputs_pair, gain_row])

    x_own, w_key, w_value, upstream_pair, angle = tie(x_own, w_key, w_value, upstream_pair, angle)
    x_mid, x_side = gather_one(x_own)
    w_own = jnp.stack([w_key.T, w_value.T])
    w_pair, w_far = swap_core(w_own), swap_z(w_own)
    g_own = call(stack_kernel, ((64, D), BF16), [upstream, upstream_pair])
    cosine, sine = jnp.cos(angle), jnp.sin(angle)
    sine = jnp.where(jnp.arange(HD)[None, :] < HD // 2, -sine, sine)
    x_mid, x_side, w_pair, w_far, g_own, cosine, sine = tie(
        x_mid, x_side, w_pair, w_far, g_own, cosine, sine
    )
    x_far, x_last = gather_two(x_side)
    x_mid_pair, x_side_pair = swap_core(x_mid), swap_core(x_side)
    x_far, x_last, x_mid_pair, x_side_pair, g_own = tie(
        x_far, x_last, x_mid_pair, x_side_pair, g_own
    )
    g_mid, g_side = gather_one(g_own)
    planes = [w_own, w_pair, w_far, swap_core(w_far)]
    x_blocks = [
        x_mid, x_mid_pair, x_side, x_side_pair, x_far, swap_core(x_far), x_last, swap_last(x_last), x_own
    ]
    query_proj, kv = project(place, x_blocks, planes, w_query)
    query_proj, kv, g_mid, g_side = tie(query_proj, kv, g_mid, g_side)

    g_far, g_last = gather_two(g_side)
    slots = [kv, lax.ppermute(kv, "tensor", KV_BESIDE), lax.ppermute(kv, "tensor", KV_ACROSS)]
    *slots, g_mid, g_side, gathered = tie(*slots, g_mid, g_side, gathered)
    advantage = call(
        advantage_kernel,
        ((512, HD), F32),
        [rewards, groups, gathered, marks],
        [SMEM, SMEM, ANY, VMEM],
        (pltpu.VMEM((16, 8, HD), F32), pltpu.SemaphoreType.DMA((16,))),
    )
    g_mid_pair, g_side_pair = swap_core(g_mid), swap_core(g_side)
    q_row, k_row = query_gain.reshape(1, HD), key_gain.reshape(1, HD)
    attended, probs = call(
        forward_kernel,
        [((512, 256), BF16), ((2, 512, 512), F32)],
        [place, query_proj, *slots, cosine, sine, marks, q_row, k_row],
        [SMEM] + [VMEM] * 9,
        (pltpu.VMEM((2, 512, 256), BF16),),
        20,
    )
    scaled = call(scale_kernel, ((512, 256), BF16), [attended, advantage])
    g_far, g_last, g_mid_pair, g_side_pair, attended, scaled, probs, advantage = tie(
        g_far, g_last, g_mid_pair, g_side_pair, attended, scaled, probs, advantage
    )
    g_blocks = [
        g_mid, g_mid_pair, g_side, g_side_pair, g_far, swap_core(g_far), g_last, swap_last(g_last), g_own
    ]
    parts = weight_grad(g_blocks, place, scaled)
    *parts, probs = tie(*parts, probs)
    out_state = reduce_first(parts)
    dq, keep, send, d0, d1, d2, head_gains = call(
        backward_kernel,
        [((512, 256), BF16), ((288, 256), BF16), ((288, 256), BF16)]
        + [((512, 256), BF16)] * 3
        + [((2, HD), F32)],
        [place, *g_blocks, w_output, query_proj, *slots, cosine, sine, advantage, q_row, k_row, probs, attended],
        PLACED + [VMEM] * 12,
        (pltpu.VMEM((2, 512, 256), BF16), *ROWS_SCRATCH),
        32,
    )
    dq, keep, send, d0, d1, d2, *out_state = tie(dq, keep, send, d0, d1, d2, *out_state)
    d1, d2 = lax.ppermute(d1, "tensor", DKV_BESIDE), lax.ppermute(d2, "tensor", DKV_ACROSS)
    out_state = reduce_second(reduce_around(out_state))

    back = lambda rows: dot(rows, w_query, NT).astype(BF16)
    other, mine = back(send), back(keep)
    other, mine, d0, d1, d2 = tie(other, mine, d0, d1, d2)
    pair = swap_core(other)
    dkv = call(plane_kernel, ((512, 256), BF16), [place, d0, d1, d2], [SMEM] + [VMEM] * 3)
    dkv_pair = swap_z(dkv)
    one, two = call(
        first_kernel,
        [((64, D), BF16)] * 2,
        [mine, pair],
        [ANY] * 2,
        (pltpu.VMEM((128, D), BF16),) * 2 + (pltpu.SemaphoreType.DMA(()),) * 2,
    )
    dkv, dkv_pair, one, two = tie(dkv, dkv_pair, one, two)
    dkv = call(pair_kernel, ((512, 256), BF16), [dkv, dkv_pair])
    dkv_pair = swap_core(dkv)
    one = lax.ppermute(one, "tensor", by_core(UP, OTHER))
    two = lax.ppermute(two, "tensor", by_core(DOWN, None))
    dkv, dkv_pair, *out_state = tie(dkv, dkv_pair, *out_state)
    out_here, out_near, out_far = call(
        halve_kernel,
        [((640, HD), BF16), ((640, HD), BF16), ((1280, HD), BF16)],
        [place, *out_state],
        [SMEM] + [VMEM] * 3,
    )
    out_far = swap_h(out_far, 2)
    combined, rows_here = call(
        columns_kernel,
        [((512, 320), BF16), ((160, 256), BF16)],
        [place, dkv, dkv_pair, dq],
        [SMEM] + [VMEM] * 3,
    )
    *parts, norm_sums = weight_grad(x_blocks, place, combined, w_query, w_own, gain_row)
    *parts, one, two, norm_sums, out_near, out_far = tie(
        *parts, one, two, norm_sums, out_near, out_far
    )
    state = reduce_first(parts)
    out_near = (out_near.astype(F32) + out_far[640:].astype(F32)).astype(BF16)
    out_near = swap_h(out_near, 1)
    gains = jnp.concatenate([norm_sums.reshape(40, HD), head_gains, jnp.zeros((6, HD), F32)])
    gains = gains + swap_core(gains)
    gains = gains + swap_z(gains)
    three, four, own = call(
        second_kernel,
        [((64, D), BF16), ((64, D), BF16), ((32, D), F32)],
        [place, *planes, mine, pair, one, two, rows_here],
        [SMEM] + [ANY] * 6 + [VMEM] * 3,
        (
            *PLANE_SCRATCH,
            pltpu.VMEM((160, D), BF16),
            pltpu.VMEM((160, D), BF16),
            pltpu.SemaphoreType.DMA(()),
            pltpu.SemaphoreType.DMA(()),
        ),
        28,
    )
    three = lax.ppermute(three, "tensor", by_core(OTHER, ACROSS))
    four = lax.ppermute(four, "tensor", by_core(DOWN, UP))
    *state, gains = tie(*state, gains)

    state = reduce_second(reduce_around(state))
    pair = swap_core(call(third_kernel, ((32, D), BF16), [three, four]))
    input_grad = call(
        last_kernel,
        ((32, D), BF16),
        [own, three, four, pair, inputs, gain_row, upstream, advantage],
    )
    for swap in (swap_y, swap_x):
        gains = gains + swap(gains, 1)
        gains = gains + swap(gains, 2)
    *state, gains, input_grad = tie(*state, gains, input_grad)
    *state, gains = call(
        meet_kernel,
        [((896, HD), BF16)] * 4 + [((48, HD), F32)],
        [*state, gains],
    )
    state = reduce_third(state)
    gains = [gains] + [part[800:848].astype(F32) + part[848:].astype(F32) for part in state[1:]]
    gains = ((gains[0] + gains[2]) + (gains[1] + gains[3])).reshape(-1)
    state = [part[:800] for part in state]
    out_grads = out_here.astype(F32) + out_far[:640].astype(F32) + out_near.astype(F32)
    grads = reduce_last(state)
    last = grads[640:]
    return (
        input_grad,
        jnp.concatenate([grads[:320], grads[320:640]], axis=1),
        jnp.concatenate([last[:, :32], last[:, 64:96]], axis=0),
        jnp.concatenate([last[:, 32:64], last[:, 96:]], axis=0),
        jnp.concatenate([out_grads[:320], out_grads[320:]], axis=1),
        gains[:D],
        gains[D : D + HD],
        gains[D + HD : D + 2 * HD],
    )


def solution(mesh):
    in_specs = (
        P(("dp", "tensor"), None),
        P(("dp", "tensor"), None),
        P(None, "tensor"),
        P(None, "tensor"),
        P(None, "tensor"),
        P("tensor", None),
        P(),
        P(),
        P(),
        P("dp", None),
        P("dp"),
        P("dp"),
    )
    out_specs = (
        P(("dp", "tensor"), None),
        P("dp", "tensor"),
        P("dp", "tensor"),
        P("dp", "tensor"),
        P("dp", "tensor"),
        P(),
        P(),
        P(),
    )
    return jax.shard_map(
        on_device, mesh=mesh, in_specs=in_specs, out_specs=out_specs, check_vma=False
    )
```

```python
import functools

import jax
import jax.numpy as jnp
from jax import lax
from jax.experimental import pallas as pl
from jax.experimental.pallas import tpu as pltpu
from jax.sharding import PartitionSpec as P

KVH = 4
GROUPS = 16
HD = 128
EPS = 1e-06
ROPE_BASE = 1000000.0


F32 = jnp.float32
BF16 = jnp.bfloat16


def t_pairs(move, keep=None):
    pairs = []
    for y in range(4):
        for z in range(2):
            for c in range(2):
                if keep is None or keep(y, z, c):
                    a, b, d = move(y, z, c)
                    pairs.append((y * 4 + z * 2 + c, (a % 4) * 4 + b * 2 + d))
    return pairs


def send_y(value, step, keep=None):
    return lax.ppermute(value, "tensor", t_pairs(lambda y, z, c: (y + step, z, c), keep))


def swap_y(value, bits):
    return lax.ppermute(value, "tensor", t_pairs(lambda y, z, c: (y ^ bits, z, c)))


def swap_z(value):
    return lax.ppermute(value, "tensor", t_pairs(lambda y, z, c: (y, 1 - z, c)))


def swap_core(value):
    return lax.ppermute(value, "tensor", t_pairs(lambda y, z, c: (y, z, 1 - c)))


def send_x(value, step):
    return lax.ppermute(
        value, "dp", [(h * 4 + x, h * 4 + (x + step) % 4) for h in range(4) for x in range(4)]
    )


def send_h(value, step):
    return lax.ppermute(
        value, "dp", [(h * 4 + x, ((h + step) % 4) * 4 + x) for h in range(4) for x in range(4)]
    )


def swap_x(value, bits):
    return lax.ppermute(
        value, "dp", [(h * 4 + x, h * 4 + (x ^ bits)) for h in range(4) for x in range(4)]
    )


def swap_h(value, bits):
    return lax.ppermute(
        value, "dp", [(h * 4 + x, (h ^ bits) * 4 + x) for h in range(4) for x in range(4)]
    )


def total4(value, swap):
    one, two, three = swap(value, 1), swap(value, 2), swap(value, 3)
    return (value + one) + (two + three)


def tie(*values):
    return lax.optimization_barrier(values)


VMEM = pl.BlockSpec(memory_space=pltpu.VMEM)
SMEM = pl.BlockSpec(memory_space=pltpu.SMEM)
ANY = pl.BlockSpec(memory_space=pl.ANY)
NT = (((1,), (1,)), ((), ()))
TN = (((0,), (0,)), ((), ()))
D = 5120


def dot(a, b, dims=(((1,), (0,)), ((), ()))):
    return lax.dot_general(a, b, dims, preferred_element_type=F32)


def call(kernel, out, args, specs=None, scratch=(), limit=12):
    many = isinstance(out, list)
    shapes = [jax.ShapeDtypeStruct(s, t) for s, t in (out if many else [out])]
    result = pl.pallas_call(
        kernel,
        out_shape=shapes,
        in_specs=list(specs) if specs else [VMEM] * len(args),
        out_specs=[VMEM] * len(shapes),
        scratch_shapes=list(scratch),
        compiler_params=pltpu.CompilerParams(vmem_limit_bytes=limit * 2**20),
        cost_estimate=pl.CostEstimate(flops=1, bytes_accessed=1, transcendentals=0),
    )(*args)
    return result if many else result[0]


def load_rows(place, blocks, whole, sems):
    mid, mid_pair, side, side_pair, far, far_pair, last, last_pair, own = blocks
    core = place[2]

    def pick(zero, one):
        return zero + (one - zero) * core

    plan = [
        (own, 0, 0),
        (mid, pick(96, 32), 0),
        (mid_pair, pick(32, 96), 1),
        (side, pick(128, 64), 0),
        (side_pair, pick(64, 128), 1),
        (far, pick(224, 192), 0),
        (far_pair, pick(192, 224), 1),
    ]
    copies = []
    for n, (block, base, turned) in enumerate(plan):
        for half in range(2):
            at = pl.multiple_of(base + 256 * (half ^ turned), 32)
            copies.append(
                pltpu.make_async_copy(
                    block.at[pl.ds(half * 32, 32)], whole.at[pl.ds(at, 32)], sems.at[2 * n + half]
                )
            )
    for half in range(2):
        for n, (block, turned) in enumerate(((last, 0), (last_pair, 1))):
            copy = pltpu.make_async_copy(
                block.at[pl.ds(half * 32, 32)],
                whole.at[pl.ds(160 + 256 * (half ^ turned), 32)],
                sems.at[14 + half],
            )

            @pl.when(core == n)
            def _():
                copy.start()

    for copy in copies:
        copy.start()
    for copy in copies:
        copy.wait()
    for half in range(2):
        pltpu.make_async_copy(
            last.at[pl.ds(half * 32, 32)], whole.at[pl.ds(160, 32)], sems.at[14 + half]
        ).wait()


def load_plane(place, parts, w_kv, sems):
    copies = []
    for n, part in enumerate(parts):
        z, core = place[1] ^ (n // 2), place[2] ^ (n % 2)
        for kind in range(2):
            at = pl.multiple_of(kind * HD + z * 64 + core * 32, 32)
            copies.append(
                pltpu.make_async_copy(part.at[kind], w_kv.at[pl.ds(at, 32)], sems.at[2 * n + kind])
            )
    for copy in copies:
        copy.start()
    return copies


PLANE_SCRATCH = (pltpu.VMEM((256, D), BF16), pltpu.SemaphoreType.DMA((8,)))
ROWS_SCRATCH = (pltpu.VMEM((512, D), BF16), pltpu.SemaphoreType.DMA((16,)))
PLACED = [SMEM] + [ANY] * 9


def by_core(zero, one):
    pairs = []
    for y in range(4):
        for z in range(2):
            for c, move in enumerate((zero, one)):
                if move is not None:
                    a, b = move(y, z)
                    pairs.append((y * 4 + z * 2 + c, (a % 4) * 4 + b * 2 + c))
    return pairs


UP = lambda y, z: (y + 1, z)
DOWN = lambda y, z: (y - 1, z)
ACROSS = lambda y, z: (y + 2, z)
OTHER = lambda y, z: (y, 1 - z)


def gather_one(own):
    mid = lax.ppermute(own, "tensor", by_core(UP, DOWN))
    side = lax.ppermute(own, "tensor", by_core(OTHER, ACROSS))
    return mid, side


def gather_two(side):
    far = lax.ppermute(side, "tensor", by_core(UP, OTHER))
    last = lax.ppermute(side, "tensor", by_core(DOWN, None))
    return far, last


def kv_pairs(beside, back):
    pairs = []
    for y in range(4):
        for z in range(2):
            e = y // 2
            ways = [(y + 1, e), (y - 1, 1 - e)] if beside else [(y + 2, e)]
            for to, via in ways:
                here, there = y * 4 + z * 2 + via, (to % 4) * 4 + z * 2 + e
                pairs.append((there, here) if back else (here, there))
    return pairs


KV_BESIDE, KV_ACROSS = kv_pairs(True, False), kv_pairs(False, False)
DKV_BESIDE, DKV_ACROSS = kv_pairs(True, True), kv_pairs(False, True)


def swap_last(value):
    return lax.ppermute(value, "tensor", [(t, t + 1) for t in range(0, 16, 2)])


def project_kernel(place, *refs):
    blocks, planes, (w_q, q_out, kv_out, whole, sems, w_kv, w_sems) = refs[:9], refs[9:13], refs[13:]
    copies = load_plane(place, planes, w_kv, w_sems)
    load_rows(place, blocks, whole, sems)
    q_out[...] = dot(whole[...], w_q[...]).astype(BF16)
    for copy in copies:
        copy.wait()
    kv_out[...] = dot(whole[...], w_kv[...], NT).astype(BF16)


def project(place, blocks, planes, w_q):
    return call(
        project_kernel,
        [((512, 256), BF16), ((512, 256), BF16)],
        [place, *blocks, *planes, w_q],
        PLACED + [ANY] * 4 + [VMEM],
        (*ROWS_SCRATCH, *PLANE_SCRATCH),
        24,
    )


def flip_z(value):
    return jnp.concatenate([value[128:256], value[:128], value[384:], value[256:384]], axis=0)


def flip_c(value):
    return jnp.concatenate([value[256:], value[:256]], axis=0)


def turn_y(value, step):
    if step % 4 == 0:
        return value
    parts = []
    for group in range(4):
        for dy in range(4):
            at = group * 128 + ((dy + step) % 4) * 32
            parts.append(value[at : at + 32])
    return jnp.concatenate(parts, axis=0)


def pick_heads(place, slots, heads):
    own, side, across = slots
    for n in range(2):
        step = (2 * place[2] + n - place[0] + 4) % 4
        for s, slot in enumerate((own, side, across, side)):

            @pl.when(step == s)
            def _():
                value = flip_c(slot[...]) if s == 1 else slot[...]
                heads[n] = turn_y(value, -s)


def spin(value, cosine, sine):
    return value * cosine + pltpu.roll(value, 64, 1) * sine


def spin_back(grad, cosine, sine):
    return grad * cosine - pltpu.roll(grad, 64, 1) * sine


def norm(value):
    value = value.astype(F32)
    scale = lax.rsqrt(jnp.mean(value * value, axis=-1, keepdims=True) + EPS)
    return value * scale, scale


def forward_kernel(
    place, q, s0, s1, s2, cosine, sine, seg, q_gain, k_gain, out, probs, heads
):
    pick_heads(place, (s0, s1, s2), heads)
    co, si = cosine[...], sine[...]
    seg_q, row_q = seg[:, 0:1], seg[:, 1:2]
    turned = seg[...].T
    keep = (seg_q == turned[0:1]) & (row_q >= turned[1:2])
    for n in range(2):
        q_unit, _ = norm(q[:, n * HD : n * HD + HD])
        k_unit, _ = norm(heads[n, :, :HD])
        q_rot = spin(q_unit * q_gain[...], co, si).astype(BF16)
        k_rot = spin(k_unit * k_gain[...], co, si).astype(BF16)
        scores = jnp.where(keep, dot(q_rot, k_rot, NT) * HD**-0.5, -1e30)
        weights = jnp.exp(scores - jnp.max(scores, axis=-1, keepdims=True))
        soft = weights / jnp.sum(weights, axis=-1, keepdims=True)
        probs[n] = soft
        value = dot(soft.astype(BF16), heads[n, :, HD:]).astype(BF16)
        out[:, n * HD : n * HD + HD] = value


SUMS = (
    ((1, 1), (3, 1), (0, 1), (3, 0)),
    ((2, 1), (2, 0), (1, 0)),
)


def rows_of(core, turned):
    slices = []
    for dy, dz in SUMS[core]:
        for dc in range(2):
            slices.append(slice((dc ^ turned) * 256 + dz * 128 + dy * 32, (dc ^ turned) * 256 + dz * 128 + dy * 32 + 32))
    slices += [slice(turned * 256, turned * 256 + 32)] * (9 - len(slices))
    return slices


def backward_kernel(place, *refs):
    blocks = refs[:9]
    w_out, q, s0, s1, s2, cosine, sine, advantage, q_gain, k_gain, probs, attended = refs[9:21]
    dq, keep, send, d0, d1, d2, gains, heads, whole, sems = refs[21:]
    pick_heads(place, (s0, s1, s2), heads)
    load_rows(place, blocks, whole, sems)
    grad_out = (dot(whole[...], w_out[...], NT) * advantage[:, 0:1]).astype(BF16)
    co, si = cosine[...], sine[...]
    q_sum = jnp.zeros((1, HD), F32)
    k_sum = jnp.zeros((1, HD), F32)
    d0[...] = jnp.zeros_like(d0)
    for n in range(2):
        cols = slice(n * HD, n * HD + HD)
        q_unit, q_scale = norm(q[:, cols])
        k_unit, k_scale = norm(heads[n, :, :HD])
        q_rot = spin(q_unit * q_gain[...], co, si).astype(BF16)
        k_rot = spin(k_unit * k_gain[...], co, si).astype(BF16)
        grad = grad_out[:, cols]
        delta = jnp.sum(
            grad.astype(F32) * attended[:, cols].astype(F32), axis=-1, keepdims=True
        )
        soft = probs[n]
        score = (soft * (dot(grad, heads[n, :, HD:], NT) - delta) * HD**-0.5).astype(BF16)
        e_q = spin_back(dot(score, k_rot), co, si)
        e_k = spin_back(dot(q_rot.T, score).T, co, si)
        grad_v = dot(grad.T, soft.astype(BF16)).T.astype(BF16)
        q_sum += jnp.sum(e_q * q_unit, axis=0, keepdims=True)
        k_sum += jnp.sum(e_k * k_unit, axis=0, keepdims=True)
        e_q = e_q * q_gain[...]
        e_k = e_k * k_gain[...]
        grad_q = q_scale * (e_q - q_unit * jnp.mean(e_q * q_unit, axis=-1, keepdims=True))
        grad_k = k_scale * (e_k - k_unit * jnp.mean(e_k * k_unit, axis=-1, keepdims=True))
        dq[:, cols] = grad_q.astype(BF16)
        both = jnp.concatenate([grad_k.astype(BF16), grad_v], axis=1)
        step = (2 * place[2] + n - place[0] + 4) % 4
        for s, slot in enumerate((d0, d1, d2, d1)):

            @pl.when(step == s)
            def _():
                slot[...] = both

    gains[...] = jnp.concatenate([q_sum, k_sum], axis=0)
    for core in range(2):

        @pl.when(place[2] == core)
        def _():
            keep[...] = jnp.concatenate([dq[at] for at in rows_of(core, 0)], axis=0)
            send[...] = jnp.concatenate([dq[at] for at in rows_of(1 - core, 1)], axis=0)


def plane_kernel(place, own, side, across, out):
    total = own[...].astype(F32) + turn_y(across[...], 2).astype(F32)
    home = place[0] // 2 == place[2]

    @pl.when(home)
    def _():
        out[...] = (total + turn_y(side[...], 3).astype(F32)).astype(BF16)

    @pl.when(jnp.logical_not(home))
    def _():
        out[...] = (total + turn_y(flip_c(side[...]), 1).astype(F32)).astype(BF16)


def pair_kernel(a, b, out):
    out[...] = (a[...].astype(F32) + flip_z(b[...]).astype(F32)).astype(BF16)


def columns_kernel(place, a, b, dq, right, rows_here):
    full = (a[...].astype(F32) + flip_c(b[...]).astype(F32)).astype(BF16)
    for core in range(2):

        @pl.when(place[2] == core)
        def _():
            some = [full[at] for at in rows_of(core, 0)]
            some = some[4:9] if core == 0 else some[2:7]
            rows_here[...] = jnp.concatenate(some, axis=0)

    right[:, :256] = dq[...]
    spot = place[1] * 2 + place[2]
    for n in range(4):

        @pl.when(spot == n)
        def _():
            right[:, 256:] = jnp.concatenate(
                [full[:, n * 32 : n * 32 + 32], full[:, HD + n * 32 : HD + n * 32 + 32]], axis=1
            )


def weight_kernel(place, *refs):
    if len(refs) == 17:
        blocks, (right, o0, o1, o2a, o2b, o3, whole, sems) = refs[:9], refs[9:]
    else:
        blocks, (right, w_q, w_kv, gain, o0, o1, o2a, o2b, o3, sums, whole, sems) = refs[:9], refs[9:]
    turned = right[...].T
    one = lax.broadcasted_iota(jnp.int32, (256, 256), 0)
    eye = jnp.where(one == lax.broadcasted_iota(jnp.int32, (256, 256), 1), 1.0, 0.0).astype(BF16)
    load_rows(place, blocks, whole, sems)
    for h in range(4):
        at = slice(h * 1280, h * 1280 + 1280)
        exact = dot(turned, whole[:, at])
        side = exact.astype(BF16)
        part = [dot(eye, side[:, i * 256 : i * 256 + 256], NT).astype(BF16) for i in range(5)]
        part = jnp.concatenate(part, axis=0)
        if len(refs) != 17:
            product = (part[:, :256].astype(F32) * w_q[at].astype(F32)).astype(BF16)
            total = dot(jnp.ones((8, 256), BF16), product, NT)[0:1]
            total += jnp.sum(exact[256:288] * w_kv[0, :, at].astype(F32), axis=0, keepdims=True)
            total += jnp.sum(exact[288:320] * w_kv[1, :, at].astype(F32), axis=0, keepdims=True)
            sums[:, at] = total / gain[:, at]
        k = (h - place[3] + 4) % 4
        for x in range(4):
            s = (x - place[4] + 4) % 4
            tile = part[x * 320 : x * 320 + 320]
            if right.shape[1] == 256:
                tile = jnp.concatenate([tile[:, :HD], tile[:, HD:]], axis=0)
            else:
                tile = jnp.concatenate(
                    [
                        tile[:, :HD],
                        tile[:, HD : 2 * HD],
                        jnp.concatenate([tile[:160, 2 * HD :], tile[160:, 2 * HD :]], axis=1),
                    ],
                    axis=0,
                )
            for at, out in ((0, o0), (1, o1), (3, o3)):

                @pl.when(s == at)
                def _():
                    out[k] = tile

            @pl.when((s == 2) & (k < 2))
            def _():
                o2a[jnp.minimum(k, 1)] = tile

            @pl.when((s == 2) & (k >= 2))
            def _():
                o2b[jnp.maximum(k - 2, 0)] = tile


def weight_grad(blocks, place, right, *more):
    rows = right.shape[1] * 320 // HD
    four, two = ((4, rows, HD), BF16), ((2, rows, HD), BF16)
    return call(
        weight_kernel,
        [four, four, two, two, four] + ([((1, D), F32)] if more else []),
        [place, *blocks, right, *more],
        PLACED + [VMEM] * (1 + len(more)),
        ROWS_SCRATCH,
        32,
    )


def around_kernel(o1, o3, a, b, right, left):
    right[0:2] = (o1[0:2].astype(F32) + a[...].astype(F32)).astype(BF16)
    right[2:4] = o1[2:4]
    left[0:2] = o3[0:2]
    left[2:4] = (o3[2:4].astype(F32) + b[...].astype(F32)).astype(BF16)


def meet_kernel(o0, r, s, gains, p0, p1, p2, p3, own):
    value = gains[...]
    high = value.astype(BF16)
    low = (value - high.astype(F32)).astype(BF16)
    own[...] = high.astype(F32) + low.astype(F32)
    for k, out in enumerate((p0, p1, p2, p3)):
        out[0:800] = (o0[k].astype(F32) + r[k].astype(F32) + s[k].astype(F32)).astype(BF16)
        out[800:848] = high
        out[848:896] = low


def reduce_first(parts):
    o0, o1, o2a, o2b, o3 = parts
    return o0, o1, o3, send_x(o2a, 1), send_x(o2b, -1)


def reduce_around(state):
    o0, o1, o3, a, b = state
    right, left = call(around_kernel, [(o1.shape, BF16)] * 2, [o1, o3, a, b])
    return o0, right, left


def reduce_second(state):
    o0, right, left = state
    return o0, send_x(right, 1), send_x(left, -1)


def halve_kernel(place, o0, r, s, here, near, far):
    def total(k):
        return (o0[k].astype(F32) + r[k].astype(F32) + s[k].astype(F32)).astype(BF16)

    here[...] = total(0)
    far[0:640] = total(2)
    for odd in range(2):

        @pl.when(place[3] % 2 == odd)
        def _():
            near[...] = total(3 if odd else 1)
            far[640:1280] = total(1 if odd else 3)


def reduce_third(state):
    p0, p1, p2, p3 = state
    return p0, send_h(p1, 1), send_h(p2, 2), send_h(p3, -1)


def reduce_last(state):
    zero, one, two, three = [part.astype(F32) for part in state]
    return (zero + two) + (one + three)


def first_kernel(mine, pair, one, two, m, p, s_m, s_p):
    copies = [
        pltpu.make_async_copy(mine.at[pl.ds(0, 128)], m, s_m),
        pltpu.make_async_copy(pair.at[pl.ds(0, 128)], p, s_p),
    ]
    for copy in copies:
        copy.start()
    for copy in copies:
        copy.wait()
    one[...] = (m[0:64].astype(F32) + p[0:64].astype(F32)).astype(BF16)
    two[...] = (m[64:128].astype(F32) + p[64:128].astype(F32)).astype(BF16)


def second_kernel(place, *refs):
    planes, (mine, pair, one, two, here, three, four, own, w_kv, sems, m, p, s_m, s_p) = refs[:4], refs[4:]
    copies = load_plane(place, planes, w_kv, sems)
    at = pl.ds(pl.multiple_of(128 - 64 * place[2], 32), 160)
    sides = [
        pltpu.make_async_copy(mine.at[at], m, s_m),
        pltpu.make_async_copy(pair.at[at], p, s_p),
    ]
    for copy in sides:
        copy.start()
    for copy in copies + sides:
        copy.wait()
    term = dot(here[...], w_kv[...])

    def both(at, size=64):
        return m[at : at + size].astype(F32) + p[at : at + size].astype(F32)

    own[...] = both(128, 32) + term[128:160]
    four[...] = (both(64) + term[64:128]).astype(BF16)

    @pl.when(place[2] == 0)
    def _():
        three[...] = (both(0) + one[...].astype(F32) + two[...].astype(F32)).astype(BF16)

    @pl.when(place[2] == 1)
    def _():
        three[...] = (both(0) + one[...].astype(F32) + term[0:64]).astype(BF16)


def third_kernel(three, four, out):
    out[...] = (three[32:64].astype(F32) + four[32:64].astype(F32)).astype(BF16)


def last_kernel(own, three, four, pair, x, gain, grad, advantage, out):
    total = own[...] + three[0:32].astype(F32) + four[0:32].astype(F32) + pair[...].astype(F32)
    value = x[...].astype(F32)
    scale = lax.rsqrt(jnp.mean(value * value, axis=-1, keepdims=True) + EPS)
    unit = value * scale
    weighted = total * gain[...]
    inner = weighted - unit * jnp.mean(weighted * unit, axis=-1, keepdims=True)
    scaled = (grad[...].astype(F32) * advantage[0:32, 0:1]).astype(BF16)
    out[...] = (scale * inner + scaled.astype(F32)).astype(BF16)


def normed_kernel(x, pair, gain, out):
    for n, ref in enumerate((x, pair)):
        unit, _ = norm(ref[...])
        out[n * 32 : n * 32 + 32] = (unit * gain[...]).astype(BF16)


def stack_kernel(x, pair, out):
    out[0:32] = x[...]
    out[32:64] = pair[...]


def tables_kernel(place, lengths, rewards, groups, inverse, sums, angle, marks):
    lane = lax.broadcasted_iota(jnp.int32, (1, HD), 1)
    count = jnp.zeros((1, HD), F32)
    first, second = count, count
    for n in range(8):
        hit = jnp.where(lane == groups[n], 1.0, 0.0)
        count += hit
        first += hit * rewards[n]
        second += hit * (rewards[n] * rewards[n])
    sums[...] = jnp.concatenate([count, first, second, jnp.zeros((5, HD), F32)], axis=0)
    j = lax.broadcasted_iota(jnp.int32, (512, HD), 0)
    spot = (((place[0] + ((j >> 5) & 3)) & 3) << 2) + ((place[1] ^ ((j >> 7) & 1)) << 1)
    rows = ((spot + (place[2] ^ (j >> 8))) << 5) + (j & 31)
    end = lengths[0, 0]
    segment, start = jnp.zeros_like(rows), jnp.zeros_like(rows)
    for n in range(1, 8):
        segment = jnp.where(rows >= end, n, segment)
        start = jnp.where(rows >= end, end, start)
        end = end + lengths[0, n]
    angle[...] = (rows - start).astype(F32) * inverse[...]
    lane = lax.broadcasted_iota(jnp.int32, (512, HD), 1)
    marks[...] = jnp.where(lane == 0, segment, rows).astype(F32)


def advantage_kernel(rewards, groups, total, marks, out):
    safe = jnp.maximum(total[0:1], 1.0)
    mean = total[1:2] / safe
    variance = total[2:3] / safe - mean * mean
    lane = lax.broadcasted_iota(jnp.int32, (1, HD), 1)
    segment = marks[:, 0:1]
    value = jnp.zeros((512, 1), F32)
    for n in range(8):
        hit = lane == groups[n]
        middle = jnp.sum(jnp.where(hit, mean, 0.0), axis=1, keepdims=True)
        spread = jnp.sum(jnp.where(hit, variance, 0.0), axis=1, keepdims=True)
        one = (rewards[n] - middle) / jnp.sqrt(spread + 1.0)
        value = jnp.where(segment == float(n), one, value)
    out[...] = jnp.broadcast_to(value, (512, HD))


def scale_kernel(a, advantage, out):
    out[...] = (a[...].astype(F32) * advantage[:, 0:1]).astype(BF16)


def on_device(
    inputs,
    upstream,
    w_query,
    w_key,
    w_value,
    w_output,
    norm_gain,
    query_gain,
    key_gain,
    lengths,
    rewards,
    groups,
):
    t_at = lax.axis_index("tensor")
    d_at = lax.axis_index("dp")
    y_at, z_at, c_at = t_at // 4, (t_at // 2) % 2, t_at % 2
    place = jnp.stack([y_at, z_at, c_at, d_at // 4, d_at % 4]).astype(jnp.int32)
    gain_row = norm_gain.reshape(1, D)

    inverse = ROPE_BASE ** (-(jnp.arange(HD // 2, dtype=F32) * 2.0 / HD))
    inverse = jnp.concatenate([inverse, inverse]).reshape(1, HD)
    sums, angle, marks = call(
        tables_kernel,
        [((8, HD), F32), ((512, HD), F32), ((512, HD), F32)],
        [place, lengths, rewards, groups, inverse],
        [SMEM] * 4 + [VMEM],
    )
    inputs_pair, upstream_pair, angle, sums, w_key, w_value = tie(
        swap_core(inputs), swap_core(upstream), angle, sums, w_key, w_value
    )
    x_own = call(normed_kernel, ((64, D), BF16), [inputs, inputs_pair, gain_row])

    x_own, w_key, w_value, upstream_pair, angle, sums = tie(
        x_own, w_key, w_value, upstream_pair, angle, sums
    )
    x_mid, x_side = gather_one(x_own)
    w_own = jnp.stack([w_key.T, w_value.T])
    w_pair, w_far = swap_core(w_own), swap_z(w_own)
    g_own = call(stack_kernel, ((64, D), BF16), [upstream, upstream_pair])
    cosine, sine = jnp.cos(angle), jnp.sin(angle)
    sine = jnp.where(jnp.arange(HD)[None, :] < HD // 2, -sine, sine)
    sums = sums + swap_x(sums, 1)
    sums = sums + swap_x(sums, 2)
    x_mid, x_side, w_pair, w_far, g_own, cosine, sine, sums = tie(
        x_mid, x_side, w_pair, w_far, g_own, cosine, sine, sums
    )
    x_far, x_last = gather_two(x_side)
    x_mid_pair, x_side_pair = swap_core(x_mid), swap_core(x_side)
    sums = sums + swap_h(sums, 1)
    x_far, x_last, x_mid_pair, x_side_pair, g_own, sums = tie(
        x_far, x_last, x_mid_pair, x_side_pair, g_own, sums
    )
    g_mid, g_side = gather_one(g_own)
    planes = [w_own, w_pair, w_far, swap_core(w_far)]
    x_blocks = [
        x_mid, x_mid_pair, x_side, x_side_pair, x_far, swap_core(x_far), x_last, swap_last(x_last), x_own
    ]
    query_proj, kv = project(place, x_blocks, planes, w_query)
    sums = sums + swap_h(sums, 2)
    query_proj, kv, g_mid, g_side, sums = tie(query_proj, kv, g_mid, g_side, sums)

    g_far, g_last = gather_two(g_side)
    slots = [kv, lax.ppermute(kv, "tensor", KV_BESIDE), lax.ppermute(kv, "tensor", KV_ACROSS)]
    *slots, g_mid, g_side = tie(*slots, g_mid, g_side)
    advantage = call(
        advantage_kernel,
        ((512, HD), F32),
        [rewards, groups, sums, marks],
        [SMEM, SMEM, VMEM, VMEM],
    )
    g_mid_pair, g_side_pair = swap_core(g_mid), swap_core(g_side)
    q_row, k_row = query_gain.reshape(1, HD), key_gain.reshape(1, HD)
    attended, probs = call(
        forward_kernel,
        [((512, 256), BF16), ((2, 512, 512), F32)],
        [place, query_proj, *slots, cosine, sine, marks, q_row, k_row],
        [SMEM] + [VMEM] * 9,
        (pltpu.VMEM((2, 512, 256), BF16),),
        20,
    )
    scaled = call(scale_kernel, ((512, 256), BF16), [attended, advantage])
    g_far, g_last, g_mid_pair, g_side_pair, attended, scaled, probs, advantage = tie(
        g_far, g_last, g_mid_pair, g_side_pair, attended, scaled, probs, advantage
    )
    g_blocks = [
        g_mid, g_mid_pair, g_side, g_side_pair, g_far, swap_core(g_far), g_last, swap_last(g_last), g_own
    ]
    parts = weight_grad(g_blocks, place, scaled)
    *parts, probs = tie(*parts, probs)
    out_state = reduce_first(parts)
    dq, keep, send, d0, d1, d2, head_gains = call(
        backward_kernel,
        [((512, 256), BF16), ((288, 256), BF16), ((288, 256), BF16)]
        + [((512, 256), BF16)] * 3
        + [((2, HD), F32)],
        [place, *g_blocks, w_output, query_proj, *slots, cosine, sine, advantage, q_row, k_row, probs, attended],
        PLACED + [VMEM] * 12,
        (pltpu.VMEM((2, 512, 256), BF16), *ROWS_SCRATCH),
        32,
    )
    dq, keep, send, d0, d1, d2, *out_state = tie(dq, keep, send, d0, d1, d2, *out_state)
    d1, d2 = lax.ppermute(d1, "tensor", DKV_BESIDE), lax.ppermute(d2, "tensor", DKV_ACROSS)
    out_state = reduce_second(reduce_around(out_state))

    back = lambda rows: dot(rows, w_query, NT).astype(BF16)
    other, mine = back(send), back(keep)
    other, mine, d0, d1, d2 = tie(other, mine, d0, d1, d2)
    pair = swap_core(other)
    dkv = call(plane_kernel, ((512, 256), BF16), [place, d0, d1, d2], [SMEM] + [VMEM] * 3)
    dkv_pair = swap_z(dkv)
    one, two = call(
        first_kernel,
        [((64, D), BF16)] * 2,
        [mine, pair],
        [ANY] * 2,
        (pltpu.VMEM((128, D), BF16),) * 2 + (pltpu.SemaphoreType.DMA(()),) * 2,
    )
    dkv, dkv_pair, one, two = tie(dkv, dkv_pair, one, two)
    dkv = call(pair_kernel, ((512, 256), BF16), [dkv, dkv_pair])
    dkv_pair = swap_core(dkv)
    dkv, dkv_pair, *out_state = tie(dkv, dkv_pair, *out_state)
    out_here, out_near, out_far = call(
        halve_kernel,
        [((640, HD), BF16), ((640, HD), BF16), ((1280, HD), BF16)],
        [place, *out_state],
        [SMEM] + [VMEM] * 3,
    )
    out_far = swap_h(out_far, 2)
    combined, rows_here = call(
        columns_kernel,
        [((512, 320), BF16), ((160, 256), BF16)],
        [place, dkv, dkv_pair, dq],
        [SMEM] + [VMEM] * 3,
    )
    *parts, norm_sums = weight_grad(x_blocks, place, combined, w_query, w_own, gain_row)
    *parts, norm_sums, one, two, out_near, out_far = tie(
        *parts, norm_sums, one, two, out_near, out_far
    )
    state = reduce_first(parts)
    one = lax.ppermute(one, "tensor", by_core(UP, OTHER))
    two = lax.ppermute(two, "tensor", by_core(DOWN, None))
    gains = jnp.concatenate([norm_sums.reshape(40, HD), head_gains, jnp.zeros((6, HD), F32)])
    gains = gains + swap_core(gains)
    gains = gains + swap_z(gains)
    *state, one, two, gains = tie(*state, one, two, gains)

    state = reduce_second(reduce_around(state))
    three, four, own = call(
        second_kernel,
        [((64, D), BF16), ((64, D), BF16), ((32, D), F32)],
        [place, *planes, mine, pair, one, two, rows_here],
        [SMEM] + [ANY] * 6 + [VMEM] * 3,
        (
            *PLANE_SCRATCH,
            pltpu.VMEM((160, D), BF16),
            pltpu.VMEM((160, D), BF16),
            pltpu.SemaphoreType.DMA(()),
            pltpu.SemaphoreType.DMA(()),
        ),
        28,
    )
    three = lax.ppermute(three, "tensor", by_core(OTHER, ACROSS))
    four = lax.ppermute(four, "tensor", by_core(DOWN, UP))
    out_near = (out_near.astype(F32) + out_far[640:].astype(F32)).astype(BF16)
    out_near = swap_h(out_near, 1)
    pair = swap_core(call(third_kernel, ((32, D), BF16), [three, four]))
    input_grad = call(
        last_kernel,
        ((32, D), BF16),
        [own, three, four, pair, inputs, gain_row, upstream, advantage],
    )
    for swap in (swap_y, swap_x):
        gains = gains + swap(gains, 1)
        gains = gains + swap(gains, 2)
    *state, gains, input_grad = tie(*state, gains, input_grad)
    *state, gains = call(
        meet_kernel,
        [((896, HD), BF16)] * 4 + [((48, HD), F32)],
        [*state, gains],
    )
    state = reduce_third(state)
    gains = [gains] + [part[800:848].astype(F32) + part[848:].astype(F32) for part in state[1:]]
    gains = ((gains[0] + gains[2]) + (gains[1] + gains[3])).reshape(-1)
    state = [part[:800] for part in state]
    out_grads = out_here.astype(F32) + out_far[:640].astype(F32) + out_near.astype(F32)
    grads = reduce_last(state)
    last = grads[640:]
    return (
        input_grad,
        jnp.concatenate([grads[:320], grads[320:640]], axis=1),
        jnp.concatenate([last[:, :32], last[:, 64:96]], axis=0),
        jnp.concatenate([last[:, 32:64], last[:, 96:]], axis=0),
        jnp.concatenate([out_grads[:320], out_grads[320:]], axis=1),
        gains[:D],
        gains[D : D + HD],
        gains[D + HD : D + 2 * HD],
    )


def solution(mesh):
    in_specs = (
        P(("dp", "tensor"), None),
        P(("dp", "tensor"), None),
        P(None, "tensor"),
        P(None, "tensor"),
        P(None, "tensor"),
        P("tensor", None),
        P(),
        P(),
        P(),
        P("dp", None),
        P("dp"),
        P("dp"),
    )
    out_specs = (
        P(("dp", "tensor"), None),
        P("dp", "tensor"),
        P("dp", "tensor"),
        P("dp", "tensor"),
        P("dp", "tensor"),
        P(),
        P(),
        P(),
    )
    return jax.shard_map(
        on_device, mesh=mesh, in_specs=in_specs, out_specs=out_specs, check_vma=False
    )
```

```python
import functools

import jax
import jax.numpy as jnp
from jax import lax
from jax.experimental import pallas as pl
from jax.experimental.pallas import tpu as pltpu
from jax.sharding import PartitionSpec as P

KVH = 4
GROUPS = 16
HD = 128
EPS = 1e-06
ROPE_BASE = 1000000.0


F32 = jnp.float32
BF16 = jnp.bfloat16


def t_pairs(move, keep=None):
    pairs = []
    for y in range(4):
        for z in range(2):
            for c in range(2):
                if keep is None or keep(y, z, c):
                    a, b, d = move(y, z, c)
                    pairs.append((y * 4 + z * 2 + c, (a % 4) * 4 + b * 2 + d))
    return pairs


def send_y(value, step, keep=None):
    return lax.ppermute(value, "tensor", t_pairs(lambda y, z, c: (y + step, z, c), keep))


def swap_y(value, bits):
    return lax.ppermute(value, "tensor", t_pairs(lambda y, z, c: (y ^ bits, z, c)))


def swap_z(value):
    return lax.ppermute(value, "tensor", t_pairs(lambda y, z, c: (y, 1 - z, c)))


def swap_core(value):
    return lax.ppermute(value, "tensor", t_pairs(lambda y, z, c: (y, z, 1 - c)))


def send_x(value, step):
    return lax.ppermute(
        value, "dp", [(h * 4 + x, h * 4 + (x + step) % 4) for h in range(4) for x in range(4)]
    )


def send_h(value, step):
    return lax.ppermute(
        value, "dp", [(h * 4 + x, ((h + step) % 4) * 4 + x) for h in range(4) for x in range(4)]
    )


def swap_x(value, bits):
    return lax.ppermute(
        value, "dp", [(h * 4 + x, h * 4 + (x ^ bits)) for h in range(4) for x in range(4)]
    )


def swap_h(value, bits):
    return lax.ppermute(
        value, "dp", [(h * 4 + x, (h ^ bits) * 4 + x) for h in range(4) for x in range(4)]
    )


def total4(value, swap):
    one, two, three = swap(value, 1), swap(value, 2), swap(value, 3)
    return (value + one) + (two + three)


def tie(*values):
    return lax.optimization_barrier(values)


VMEM = pl.BlockSpec(memory_space=pltpu.VMEM)
SMEM = pl.BlockSpec(memory_space=pltpu.SMEM)
ANY = pl.BlockSpec(memory_space=pl.ANY)
NT = (((1,), (1,)), ((), ()))
TN = (((0,), (0,)), ((), ()))
D = 5120


def dot(a, b, dims=(((1,), (0,)), ((), ()))):
    return lax.dot_general(a, b, dims, preferred_element_type=F32)


def call(kernel, out, args, specs=None, scratch=(), limit=12):
    many = isinstance(out, list)
    shapes = [jax.ShapeDtypeStruct(s, t) for s, t in (out if many else [out])]
    result = pl.pallas_call(
        kernel,
        out_shape=shapes,
        in_specs=list(specs) if specs else [VMEM] * len(args),
        out_specs=[VMEM] * len(shapes),
        scratch_shapes=list(scratch),
        compiler_params=pltpu.CompilerParams(vmem_limit_bytes=limit * 2**20),
        cost_estimate=pl.CostEstimate(flops=1, bytes_accessed=1, transcendentals=0),
    )(*args)
    return result if many else result[0]


def load_rows(place, blocks, whole, sems):
    mid, mid_pair, side, side_pair, far, far_pair, last, last_pair, own = blocks
    core = place[2]

    def pick(zero, one):
        return zero + (one - zero) * core

    plan = [
        (own, 0, 0),
        (mid, pick(96, 32), 0),
        (mid_pair, pick(32, 96), 1),
        (side, pick(128, 64), 0),
        (side_pair, pick(64, 128), 1),
        (far, pick(224, 192), 0),
        (far_pair, pick(192, 224), 1),
    ]
    copies = []
    for n, (block, base, turned) in enumerate(plan):
        for half in range(2):
            at = pl.multiple_of(base + 256 * (half ^ turned), 32)
            copies.append(
                pltpu.make_async_copy(
                    block.at[pl.ds(half * 32, 32)], whole.at[pl.ds(at, 32)], sems.at[2 * n + half]
                )
            )
    for half in range(2):
        for n, (block, turned) in enumerate(((last, 0), (last_pair, 1))):
            copy = pltpu.make_async_copy(
                block.at[pl.ds(half * 32, 32)],
                whole.at[pl.ds(160 + 256 * (half ^ turned), 32)],
                sems.at[14 + half],
            )

            @pl.when(core == n)
            def _():
                copy.start()

    for copy in copies:
        copy.start()
    for copy in copies:
        copy.wait()
    for half in range(2):
        pltpu.make_async_copy(
            last.at[pl.ds(half * 32, 32)], whole.at[pl.ds(160, 32)], sems.at[14 + half]
        ).wait()


def load_plane(place, parts, w_kv, sems):
    copies = []
    for n, part in enumerate(parts):
        z, core = place[1] ^ (n // 2), place[2] ^ (n % 2)
        for kind in range(2):
            at = pl.multiple_of(kind * HD + z * 64 + core * 32, 32)
            copies.append(
                pltpu.make_async_copy(part.at[kind], w_kv.at[pl.ds(at, 32)], sems.at[2 * n + kind])
            )
    for copy in copies:
        copy.start()
    return copies


PLANE_SCRATCH = (pltpu.VMEM((256, D), BF16), pltpu.SemaphoreType.DMA((8,)))
ROWS_SCRATCH = (pltpu.VMEM((512, D), BF16), pltpu.SemaphoreType.DMA((16,)))
PLACED = [SMEM] + [ANY] * 9


def by_core(zero, one):
    pairs = []
    for y in range(4):
        for z in range(2):
            for c, move in enumerate((zero, one)):
                if move is not None:
                    a, b = move(y, z)
                    pairs.append((y * 4 + z * 2 + c, (a % 4) * 4 + b * 2 + c))
    return pairs


UP = lambda y, z: (y + 1, z)
DOWN = lambda y, z: (y - 1, z)
ACROSS = lambda y, z: (y + 2, z)
OTHER = lambda y, z: (y, 1 - z)


def gather_one(own):
    mid = lax.ppermute(own, "tensor", by_core(UP, DOWN))
    side = lax.ppermute(own, "tensor", by_core(OTHER, ACROSS))
    return mid, side


def gather_two(side):
    far = lax.ppermute(side, "tensor", by_core(UP, OTHER))
    last = lax.ppermute(side, "tensor", by_core(DOWN, None))
    return far, last


def kv_pairs(beside, back):
    pairs = []
    for y in range(4):
        for z in range(2):
            e = y // 2
            ways = [(y + 1, e), (y - 1, 1 - e)] if beside else [(y + 2, e)]
            for to, via in ways:
                here, there = y * 4 + z * 2 + via, (to % 4) * 4 + z * 2 + e
                pairs.append((there, here) if back else (here, there))
    return pairs


KV_BESIDE, KV_ACROSS = kv_pairs(True, False), kv_pairs(False, False)
DKV_BESIDE, DKV_ACROSS = kv_pairs(True, True), kv_pairs(False, True)


def swap_last(value):
    return lax.ppermute(value, "tensor", [(t, t + 1) for t in range(0, 16, 2)])


def project_kernel(place, *refs):
    blocks, planes, (w_q, q_out, kv_out, whole, sems, w_kv, w_sems) = refs[:9], refs[9:13], refs[13:]
    copies = load_plane(place, planes, w_kv, w_sems)
    load_rows(place, blocks, whole, sems)
    q_out[...] = dot(whole[...], w_q[...]).astype(BF16)
    for copy in copies:
        copy.wait()
    kv_out[...] = dot(whole[...], w_kv[...], NT).astype(BF16)


def project(place, blocks, planes, w_q):
    return call(
        project_kernel,
        [((512, 256), BF16), ((512, 256), BF16)],
        [place, *blocks, *planes, w_q],
        PLACED + [ANY] * 4 + [VMEM],
        (*ROWS_SCRATCH, *PLANE_SCRATCH),
        24,
    )


def flip_z(value):
    return jnp.concatenate([value[128:256], value[:128], value[384:], value[256:384]], axis=0)


def flip_c(value):
    return jnp.concatenate([value[256:], value[:256]], axis=0)


def turn_y(value, step):
    if step % 4 == 0:
        return value
    parts = []
    for group in range(4):
        for dy in range(4):
            at = group * 128 + ((dy + step) % 4) * 32
            parts.append(value[at : at + 32])
    return jnp.concatenate(parts, axis=0)


def pick_heads(place, slots, heads):
    own, side, across = slots
    for n in range(2):
        step = (2 * place[2] + n - place[0] + 4) % 4
        for s, slot in enumerate((own, side, across, side)):

            @pl.when(step == s)
            def _():
                value = flip_c(slot[...]) if s == 1 else slot[...]
                heads[n] = turn_y(value, -s)


def spin(value, cosine, sine):
    return value * cosine + pltpu.roll(value, 64, 1) * sine


def spin_back(grad, cosine, sine):
    return grad * cosine - pltpu.roll(grad, 64, 1) * sine


def norm(value):
    value = value.astype(F32)
    scale = lax.rsqrt(jnp.mean(value * value, axis=-1, keepdims=True) + EPS)
    return value * scale, scale


def forward_kernel(
    place, q, s0, s1, s2, cosine, sine, seg, q_gain, k_gain, out, probs, heads
):
    pick_heads(place, (s0, s1, s2), heads)
    co, si = cosine[...], sine[...]
    seg_q, row_q = seg[:, 0:1], seg[:, 1:2]
    turned = seg[...].T
    keep = (seg_q == turned[0:1]) & (row_q >= turned[1:2])
    for n in range(2):
        q_unit, _ = norm(q[:, n * HD : n * HD + HD])
        k_unit, _ = norm(heads[n, :, :HD])
        q_rot = spin(q_unit * q_gain[...], co, si).astype(BF16)
        k_rot = spin(k_unit * k_gain[...], co, si).astype(BF16)
        scores = jnp.where(keep, dot(q_rot, k_rot, NT) * HD**-0.5, -1e30)
        weights = jnp.exp(scores - jnp.max(scores, axis=-1, keepdims=True))
        soft = weights / jnp.sum(weights, axis=-1, keepdims=True)
        probs[n] = soft
        value = dot(soft.astype(BF16), heads[n, :, HD:]).astype(BF16)
        out[:, n * HD : n * HD + HD] = value


SUMS = (
    ((1, 1), (3, 1), (0, 1), (3, 0)),
    ((2, 1), (2, 0), (1, 0)),
)


def rows_of(core, turned):
    slices = []
    for dy, dz in SUMS[core]:
        for dc in range(2):
            slices.append(slice((dc ^ turned) * 256 + dz * 128 + dy * 32, (dc ^ turned) * 256 + dz * 128 + dy * 32 + 32))
    slices += [slice(turned * 256, turned * 256 + 32)] * (9 - len(slices))
    return slices


def backward_kernel(place, *refs):
    blocks = refs[:9]
    w_out, q, s0, s1, s2, cosine, sine, advantage, q_gain, k_gain, probs, attended = refs[9:21]
    dq, keep, send, d0, d1, d2, gains, heads, whole, sems = refs[21:]
    pick_heads(place, (s0, s1, s2), heads)
    load_rows(place, blocks, whole, sems)
    grad_out = (dot(whole[...], w_out[...], NT) * advantage[:, 0:1]).astype(BF16)
    co, si = cosine[...], sine[...]
    q_sum = jnp.zeros((1, HD), F32)
    k_sum = jnp.zeros((1, HD), F32)
    d0[...] = jnp.zeros_like(d0)
    for n in range(2):
        cols = slice(n * HD, n * HD + HD)
        q_unit, q_scale = norm(q[:, cols])
        k_unit, k_scale = norm(heads[n, :, :HD])
        q_rot = spin(q_unit * q_gain[...], co, si).astype(BF16)
        k_rot = spin(k_unit * k_gain[...], co, si).astype(BF16)
        grad = grad_out[:, cols]
        delta = jnp.sum(
            grad.astype(F32) * attended[:, cols].astype(F32), axis=-1, keepdims=True
        )
        soft = probs[n]
        score = (soft * (dot(grad, heads[n, :, HD:], NT) - delta) * HD**-0.5).astype(BF16)
        e_q = spin_back(dot(score, k_rot), co, si)
        e_k = spin_back(dot(q_rot.T, score).T, co, si)
        grad_v = dot(grad.T, soft.astype(BF16)).T.astype(BF16)
        q_sum += jnp.sum(e_q * q_unit, axis=0, keepdims=True)
        k_sum += jnp.sum(e_k * k_unit, axis=0, keepdims=True)
        e_q = e_q * q_gain[...]
        e_k = e_k * k_gain[...]
        grad_q = q_scale * (e_q - q_unit * jnp.mean(e_q * q_unit, axis=-1, keepdims=True))
        grad_k = k_scale * (e_k - k_unit * jnp.mean(e_k * k_unit, axis=-1, keepdims=True))
        dq[:, cols] = grad_q.astype(BF16)
        both = jnp.concatenate([grad_k.astype(BF16), grad_v], axis=1)
        step = (2 * place[2] + n - place[0] + 4) % 4
        for s, slot in enumerate((d0, d1, d2, d1)):

            @pl.when(step == s)
            def _():
                slot[...] = both

    gains[...] = jnp.concatenate([q_sum, k_sum], axis=0)
    for core in range(2):

        @pl.when(place[2] == core)
        def _():
            keep[...] = jnp.concatenate([dq[at] for at in rows_of(core, 0)], axis=0)
            send[...] = jnp.concatenate([dq[at] for at in rows_of(1 - core, 1)], axis=0)


def plane_kernel(place, own, side, across, out):
    total = own[...].astype(F32) + turn_y(across[...], 2).astype(F32)
    home = place[0] // 2 == place[2]

    @pl.when(home)
    def _():
        out[...] = (total + turn_y(side[...], 3).astype(F32)).astype(BF16)

    @pl.when(jnp.logical_not(home))
    def _():
        out[...] = (total + turn_y(flip_c(side[...]), 1).astype(F32)).astype(BF16)


def pair_kernel(a, b, out):
    out[...] = (a[...].astype(F32) + flip_z(b[...]).astype(F32)).astype(BF16)


def columns_kernel(place, a, b, dq, right, rows_here):
    full = (a[...].astype(F32) + flip_c(b[...]).astype(F32)).astype(BF16)
    for core in range(2):

        @pl.when(place[2] == core)
        def _():
            some = [full[at] for at in rows_of(core, 0)]
            some = some[4:9] if core == 0 else some[2:7]
            rows_here[...] = jnp.concatenate(some, axis=0)

    right[:, :256] = dq[...]
    spot = place[1] * 2 + place[2]
    for n in range(4):

        @pl.when(spot == n)
        def _():
            right[:, 256:] = jnp.concatenate(
                [full[:, n * 32 : n * 32 + 32], full[:, HD + n * 32 : HD + n * 32 + 32]], axis=1
            )


def weight_kernel(place, *refs):
    if len(refs) == 17:
        blocks, (right, o0, o1, o2a, o2b, o3, whole, sems) = refs[:9], refs[9:]
    else:
        blocks, (right, w_q, w_kv, gain, o0, o1, o2a, o2b, o3, sums, whole, sems) = refs[:9], refs[9:]
    turned = right[...].T
    one = lax.broadcasted_iota(jnp.int32, (256, 256), 0)
    eye = jnp.where(one == lax.broadcasted_iota(jnp.int32, (256, 256), 1), 1.0, 0.0).astype(BF16)
    load_rows(place, blocks, whole, sems)
    for h in range(4):
        at = slice(h * 1280, h * 1280 + 1280)
        exact = dot(turned, whole[:, at])
        side = exact.astype(BF16)
        part = [dot(eye, side[:, i * 256 : i * 256 + 256], NT).astype(BF16) for i in range(5)]
        part = jnp.concatenate(part, axis=0)
        if len(refs) != 17:
            product = (part[:, :256].astype(F32) * w_q[at].astype(F32)).astype(BF16)
            total = dot(jnp.ones((8, 256), BF16), product, NT)[0:1]
            total += jnp.sum(exact[256:288] * w_kv[0, :, at].astype(F32), axis=0, keepdims=True)
            total += jnp.sum(exact[288:320] * w_kv[1, :, at].astype(F32), axis=0, keepdims=True)
            sums[:, at] = total / gain[:, at]
        k = (h - place[3] + 4) % 4
        for x in range(4):
            s = (x - place[4] + 4) % 4
            tile = part[x * 320 : x * 320 + 320]
            if right.shape[1] == 256:
                tile = jnp.concatenate([tile[:, :HD], tile[:, HD:]], axis=0)
            else:
                tile = jnp.concatenate(
                    [
                        tile[:, :HD],
                        tile[:, HD : 2 * HD],
                        jnp.concatenate([tile[:160, 2 * HD :], tile[160:, 2 * HD :]], axis=1),
                    ],
                    axis=0,
                )
            for at, out in ((0, o0), (1, o1), (3, o3)):

                @pl.when(s == at)
                def _():
                    out[k] = tile

            @pl.when((s == 2) & (k < 2))
            def _():
                o2a[jnp.minimum(k, 1)] = tile

            @pl.when((s == 2) & (k >= 2))
            def _():
                o2b[jnp.maximum(k - 2, 0)] = tile


def weight_grad(blocks, place, right, *more):
    rows = right.shape[1] * 320 // HD
    four, two = ((4, rows, HD), BF16), ((2, rows, HD), BF16)
    return call(
        weight_kernel,
        [four, four, two, two, four] + ([((1, D), F32)] if more else []),
        [place, *blocks, right, *more],
        PLACED + [VMEM] * (1 + len(more)),
        ROWS_SCRATCH,
        32,
    )


def around_kernel(o1, o3, a, b, right, left):
    right[0:2] = (o1[0:2].astype(F32) + a[...].astype(F32)).astype(BF16)
    right[2:4] = o1[2:4]
    left[0:2] = o3[0:2]
    left[2:4] = (o3[2:4].astype(F32) + b[...].astype(F32)).astype(BF16)


def meet_kernel(o0, r, s, gains, p0, p1, p2, p3, own):
    value = gains[...]
    high = value.astype(BF16)
    low = (value - high.astype(F32)).astype(BF16)
    own[...] = high.astype(F32) + low.astype(F32)
    for k, out in enumerate((p0, p1, p2, p3)):
        out[0:800] = (o0[k].astype(F32) + r[k].astype(F32) + s[k].astype(F32)).astype(BF16)
        out[800:848] = high
        out[848:896] = low


def reduce_first(parts):
    o0, o1, o2a, o2b, o3 = parts
    return o0, o1, o3, send_x(o2a, 1), send_x(o2b, -1)


def reduce_around(state):
    o0, o1, o3, a, b = state
    right, left = call(around_kernel, [(o1.shape, BF16)] * 2, [o1, o3, a, b])
    return o0, right, left


def reduce_second(state):
    o0, right, left = state
    return o0, send_x(right, 1), send_x(left, -1)


def halve_kernel(place, o0, r, s, here, near, far):
    def total(k):
        return (o0[k].astype(F32) + r[k].astype(F32) + s[k].astype(F32)).astype(BF16)

    here[...] = total(0)
    far[0:640] = total(2)
    for odd in range(2):

        @pl.when(place[3] % 2 == odd)
        def _():
            near[...] = total(3 if odd else 1)
            far[640:1280] = total(1 if odd else 3)


def reduce_third(state):
    p0, p1, p2, p3 = state
    return p0, send_h(p1, 1), send_h(p2, 2), send_h(p3, -1)


def reduce_last(state):
    zero, one, two, three = [part.astype(F32) for part in state]
    return (zero + two) + (one + three)


def first_kernel(mine, pair, one, two, m, p, s_m, s_p):
    copies = [
        pltpu.make_async_copy(mine.at[pl.ds(0, 128)], m, s_m),
        pltpu.make_async_copy(pair.at[pl.ds(0, 128)], p, s_p),
    ]
    for copy in copies:
        copy.start()
    for copy in copies:
        copy.wait()
    one[...] = (m[0:64].astype(F32) + p[0:64].astype(F32)).astype(BF16)
    two[...] = (m[64:128].astype(F32) + p[64:128].astype(F32)).astype(BF16)


def second_kernel(place, *refs):
    planes, (mine, pair, one, two, here, three, four, own, w_kv, sems, m, p, s_m, s_p) = refs[:4], refs[4:]
    copies = load_plane(place, planes, w_kv, sems)
    at = pl.ds(pl.multiple_of(128 - 64 * place[2], 32), 160)
    sides = [
        pltpu.make_async_copy(mine.at[at], m, s_m),
        pltpu.make_async_copy(pair.at[at], p, s_p),
    ]
    for copy in sides:
        copy.start()
    for copy in copies + sides:
        copy.wait()
    term = dot(here[...], w_kv[...])

    def both(at, size=64):
        return m[at : at + size].astype(F32) + p[at : at + size].astype(F32)

    own[...] = both(128, 32) + term[128:160]
    four[...] = (both(64) + term[64:128]).astype(BF16)

    @pl.when(place[2] == 0)
    def _():
        three[...] = (both(0) + one[...].astype(F32) + two[...].astype(F32)).astype(BF16)

    @pl.when(place[2] == 1)
    def _():
        three[...] = (both(0) + one[...].astype(F32) + term[0:64]).astype(BF16)


def third_kernel(three, four, out):
    out[...] = (three[32:64].astype(F32) + four[32:64].astype(F32)).astype(BF16)


def last_kernel(own, three, four, pair, x, gain, grad, advantage, out):
    total = own[...] + three[0:32].astype(F32) + four[0:32].astype(F32) + pair[...].astype(F32)
    value = x[...].astype(F32)
    scale = lax.rsqrt(jnp.mean(value * value, axis=-1, keepdims=True) + EPS)
    unit = value * scale
    weighted = total * gain[...]
    inner = weighted - unit * jnp.mean(weighted * unit, axis=-1, keepdims=True)
    scaled = (grad[...].astype(F32) * advantage[0:32, 0:1]).astype(BF16)
    out[...] = (scale * inner + scaled.astype(F32)).astype(BF16)


def normed_kernel(x, pair, gain, out):
    for n, ref in enumerate((x, pair)):
        unit, _ = norm(ref[...])
        out[n * 32 : n * 32 + 32] = (unit * gain[...]).astype(BF16)


def stack_kernel(x, pair, out):
    out[0:32] = x[...]
    out[32:64] = pair[...]


def tables_kernel(place, lengths, rewards, groups, inverse, sums, angle, marks):
    lane = lax.broadcasted_iota(jnp.int32, (1, HD), 1)
    count = jnp.zeros((1, HD), F32)
    first, second = count, count
    for n in range(8):
        hit = jnp.where(lane == groups[n], 1.0, 0.0)
        count += hit
        first += hit * rewards[n]
        second += hit * (rewards[n] * rewards[n])
    sums[...] = jnp.concatenate([count, first, second, jnp.zeros((5, HD), F32)], axis=0)
    j = lax.broadcasted_iota(jnp.int32, (512, HD), 0)
    spot = (((place[0] + ((j >> 5) & 3)) & 3) << 2) + ((place[1] ^ ((j >> 7) & 1)) << 1)
    rows = ((spot + (place[2] ^ (j >> 8))) << 5) + (j & 31)
    end = lengths[0, 0]
    segment, start = jnp.zeros_like(rows), jnp.zeros_like(rows)
    for n in range(1, 8):
        segment = jnp.where(rows >= end, n, segment)
        start = jnp.where(rows >= end, end, start)
        end = end + lengths[0, n]
    angle[...] = (rows - start).astype(F32) * inverse[...]
    lane = lax.broadcasted_iota(jnp.int32, (512, HD), 1)
    marks[...] = jnp.where(lane == 0, segment, rows).astype(F32)


def advantage_kernel(rewards, groups, total, marks, out):
    safe = jnp.maximum(total[0:1], 1.0)
    mean = total[1:2] / safe
    variance = total[2:3] / safe - mean * mean
    lane = lax.broadcasted_iota(jnp.int32, (1, HD), 1)
    segment = marks[:, 0:1]
    value = jnp.zeros((512, 1), F32)
    for n in range(8):
        hit = lane == groups[n]
        middle = jnp.sum(jnp.where(hit, mean, 0.0), axis=1, keepdims=True)
        spread = jnp.sum(jnp.where(hit, variance, 0.0), axis=1, keepdims=True)
        one = (rewards[n] - middle) / jnp.sqrt(spread + 1.0)
        value = jnp.where(segment == float(n), one, value)
    out[...] = jnp.broadcast_to(value, (512, HD))


def scale_kernel(a, advantage, out):
    out[...] = (a[...].astype(F32) * advantage[:, 0:1]).astype(BF16)


def on_device(
    inputs,
    upstream,
    w_query,
    w_key,
    w_value,
    w_output,
    norm_gain,
    query_gain,
    key_gain,
    lengths,
    rewards,
    groups,
):
    t_at = lax.axis_index("tensor")
    d_at = lax.axis_index("dp")
    y_at, z_at, c_at = t_at // 4, (t_at // 2) % 2, t_at % 2
    place = jnp.stack([y_at, z_at, c_at, d_at // 4, d_at % 4]).astype(jnp.int32)
    gain_row = norm_gain.reshape(1, D)

    inverse = ROPE_BASE ** (-(jnp.arange(HD // 2, dtype=F32) * 2.0 / HD))
    inverse = jnp.concatenate([inverse, inverse]).reshape(1, HD)
    sums, angle, marks = call(
        tables_kernel,
        [((8, HD), F32), ((512, HD), F32), ((512, HD), F32)],
        [place, lengths, rewards, groups, inverse],
        [SMEM] * 4 + [VMEM],
    )
    inputs_pair, upstream_pair, angle, sums, w_key, w_value = tie(
        swap_core(inputs), swap_core(upstream), angle, sums, w_key, w_value
    )
    x_own = call(normed_kernel, ((64, D), BF16), [inputs, inputs_pair, gain_row])

    x_own, w_key, w_value, upstream_pair, angle, sums = tie(
        x_own, w_key, w_value, upstream_pair, angle, sums
    )
    x_mid, x_side = gather_one(x_own)
    w_own = jnp.stack([w_key.T, w_value.T])
    w_pair, w_far = swap_core(w_own), swap_z(w_own)
    g_own = call(stack_kernel, ((64, D), BF16), [upstream, upstream_pair])
    cosine, sine = jnp.cos(angle), jnp.sin(angle)
    sine = jnp.where(jnp.arange(HD)[None, :] < HD // 2, -sine, sine)
    sums = sums + swap_x(sums, 1)
    sums = sums + swap_x(sums, 2)
    x_mid, x_side, w_pair, w_far, g_own, cosine, sine, sums = tie(
        x_mid, x_side, w_pair, w_far, g_own, cosine, sine, sums
    )
    x_far, x_last = gather_two(x_side)
    x_mid_pair, x_side_pair = swap_core(x_mid), swap_core(x_side)
    sums = sums + swap_h(sums, 1)
    x_far, x_last, x_mid_pair, x_side_pair, g_own, sums = tie(
        x_far, x_last, x_mid_pair, x_side_pair, g_own, sums
    )
    g_mid, g_side = gather_one(g_own)
    planes = [w_own, w_pair, w_far, swap_core(w_far)]
    x_blocks = [
        x_mid, x_mid_pair, x_side, x_side_pair, x_far, swap_core(x_far), x_last, swap_last(x_last), x_own
    ]
    query_proj, kv = project(place, x_blocks, planes, w_query)
    query_proj, kv, g_mid, g_side, sums = tie(query_proj, kv, g_mid, g_side, sums)

    g_far, g_last = gather_two(g_side)
    slots = [kv, lax.ppermute(kv, "tensor", KV_BESIDE), lax.ppermute(kv, "tensor", KV_ACROSS)]
    sums = sums + swap_h(sums, 2)
    *slots, g_mid, g_side, sums = tie(*slots, g_mid, g_side, sums)
    advantage = call(
        advantage_kernel,
        ((512, HD), F32),
        [rewards, groups, sums, marks],
        [SMEM, SMEM, VMEM, VMEM],
    )
    g_mid_pair, g_side_pair = swap_core(g_mid), swap_core(g_side)
    q_row, k_row = query_gain.reshape(1, HD), key_gain.reshape(1, HD)
    attended, probs = call(
        forward_kernel,
        [((512, 256), BF16), ((2, 512, 512), F32)],
        [place, query_proj, *slots, cosine, sine, marks, q_row, k_row],
        [SMEM] + [VMEM] * 9,
        (pltpu.VMEM((2, 512, 256), BF16),),
        20,
    )
    scaled = call(scale_kernel, ((512, 256), BF16), [attended, advantage])
    g_far, g_last, g_mid_pair, g_side_pair, attended, scaled, probs, advantage = tie(
        g_far, g_last, g_mid_pair, g_side_pair, attended, scaled, probs, advantage
    )
    g_blocks = [
        g_mid, g_mid_pair, g_side, g_side_pair, g_far, swap_core(g_far), g_last, swap_last(g_last), g_own
    ]
    parts = weight_grad(g_blocks, place, scaled)
    *parts, probs = tie(*parts, probs)
    out_state = reduce_first(parts)
    dq, keep, send, d0, d1, d2, head_gains = call(
        backward_kernel,
        [((512, 256), BF16), ((288, 256), BF16), ((288, 256), BF16)]
        + [((512, 256), BF16)] * 3
        + [((2, HD), F32)],
        [place, *g_blocks, w_output, query_proj, *slots, cosine, sine, advantage, q_row, k_row, probs, attended],
        PLACED + [VMEM] * 12,
        (pltpu.VMEM((2, 512, 256), BF16), *ROWS_SCRATCH),
        32,
    )
    dq, keep, send, d0, d1, d2, *out_state = tie(dq, keep, send, d0, d1, d2, *out_state)
    d1, d2 = lax.ppermute(d1, "tensor", DKV_BESIDE), lax.ppermute(d2, "tensor", DKV_ACROSS)
    out_state = reduce_second(reduce_around(out_state))

    back = lambda rows: dot(rows, w_query, NT).astype(BF16)
    other, mine = back(send), back(keep)
    other, mine, d0, d1, d2 = tie(other, mine, d0, d1, d2)
    pair = swap_core(other)
    dkv = call(plane_kernel, ((512, 256), BF16), [place, d0, d1, d2], [SMEM] + [VMEM] * 3)
    dkv_pair = swap_z(dkv)
    one, two = call(
        first_kernel,
        [((64, D), BF16)] * 2,
        [mine, pair],
        [ANY] * 2,
        (pltpu.VMEM((128, D), BF16),) * 2 + (pltpu.SemaphoreType.DMA(()),) * 2,
    )
    dkv, dkv_pair, one, two = tie(dkv, dkv_pair, one, two)
    dkv = call(pair_kernel, ((512, 256), BF16), [dkv, dkv_pair])
    dkv_pair = swap_core(dkv)
    dkv, dkv_pair, *out_state = tie(dkv, dkv_pair, *out_state)
    out_here, out_near, out_far = call(
        halve_kernel,
        [((640, HD), BF16), ((640, HD), BF16), ((1280, HD), BF16)],
        [place, *out_state],
        [SMEM] + [VMEM] * 3,
    )
    out_far = swap_h(out_far, 2)
    combined, rows_here = call(
        columns_kernel,
        [((512, 320), BF16), ((160, 256), BF16)],
        [place, dkv, dkv_pair, dq],
        [SMEM] + [VMEM] * 3,
    )
    *parts, norm_sums = weight_grad(x_blocks, place, combined, w_query, w_own, gain_row)
    *parts, norm_sums, one, two, out_near, out_far = tie(
        *parts, norm_sums, one, two, out_near, out_far
    )
    state = reduce_first(parts)
    gains = jnp.concatenate([norm_sums.reshape(40, HD), head_gains, jnp.zeros((6, HD), F32)])
    gains = gains + swap_core(gains)
    one, two, gains = tie(one, two, gains)
    one = lax.ppermute(one, "tensor", by_core(UP, OTHER))
    two = lax.ppermute(two, "tensor", by_core(DOWN, None))
    gains = gains + swap_z(gains)
    *state, one, two, gains = tie(*state, one, two, gains)

    state = reduce_second(reduce_around(state))
    three, four, own = call(
        second_kernel,
        [((64, D), BF16), ((64, D), BF16), ((32, D), F32)],
        [place, *planes, mine, pair, one, two, rows_here],
        [SMEM] + [ANY] * 6 + [VMEM] * 3,
        (
            *PLANE_SCRATCH,
            pltpu.VMEM((160, D), BF16),
            pltpu.VMEM((160, D), BF16),
            pltpu.SemaphoreType.DMA(()),
            pltpu.SemaphoreType.DMA(()),
        ),
        28,
    )
    three = lax.ppermute(three, "tensor", by_core(OTHER, ACROSS))
    four = lax.ppermute(four, "tensor", by_core(DOWN, UP))
    out_near = (out_near.astype(F32) + out_far[640:].astype(F32)).astype(BF16)
    out_near = swap_h(out_near, 1)
    three, four, out_near, gains = tie(three, four, out_near, gains)
    pair = swap_core(call(third_kernel, ((32, D), BF16), [three, four]))
    input_grad = call(
        last_kernel,
        ((32, D), BF16),
        [own, three, four, pair, inputs, gain_row, upstream, advantage],
    )
    gains = total4(total4(gains, swap_y), swap_x)
    *state, gains, input_grad = tie(*state, gains, input_grad)
    *state, gains = call(
        meet_kernel,
        [((896, HD), BF16)] * 4 + [((48, HD), F32)],
        [*state, gains],
    )
    state = reduce_third(state)
    gains = [gains] + [part[800:848].astype(F32) + part[848:].astype(F32) for part in state[1:]]
    gains = ((gains[0] + gains[2]) + (gains[1] + gains[3])).reshape(-1)
    state = [part[:800] for part in state]
    out_grads = out_here.astype(F32) + out_far[:640].astype(F32) + out_near.astype(F32)
    grads = reduce_last(state)
    last = grads[640:]
    return (
        input_grad,
        jnp.concatenate([grads[:320], grads[320:640]], axis=1),
        jnp.concatenate([last[:, :32], last[:, 64:96]], axis=0),
        jnp.concatenate([last[:, 32:64], last[:, 96:]], axis=0),
        jnp.concatenate([out_grads[:320], out_grads[320:]], axis=1),
        gains[:D],
        gains[D : D + HD],
        gains[D + HD : D + 2 * HD],
    )


def solution(mesh):
    in_specs = (
        P(("dp", "tensor"), None),
        P(("dp", "tensor"), None),
        P(None, "tensor"),
        P(None, "tensor"),
        P(None, "tensor"),
        P("tensor", None),
        P(),
        P(),
        P(),
        P("dp", None),
        P("dp"),
        P("dp"),
    )
    out_specs = (
        P(("dp", "tensor"), None),
        P("dp", "tensor"),
        P("dp", "tensor"),
        P("dp", "tensor"),
        P("dp", "tensor"),
        P(),
        P(),
        P(),
    )
    return jax.shard_map(
        on_device, mesh=mesh, in_specs=in_specs, out_specs=out_specs, check_vma=False
    )
```

```python
import functools

import jax
import jax.numpy as jnp
from jax import lax
from jax.experimental import pallas as pl
from jax.experimental.pallas import tpu as pltpu
from jax.sharding import PartitionSpec as P

KVH = 4
GROUPS = 16
HD = 128
EPS = 1e-06
ROPE_BASE = 1000000.0


F32 = jnp.float32
BF16 = jnp.bfloat16


def t_pairs(move, keep=None):
    pairs = []
    for y in range(4):
        for z in range(2):
            for c in range(2):
                if keep is None or keep(y, z, c):
                    a, b, d = move(y, z, c)
                    pairs.append((y * 4 + z * 2 + c, (a % 4) * 4 + b * 2 + d))
    return pairs


def send_y(value, step, keep=None):
    return lax.ppermute(value, "tensor", t_pairs(lambda y, z, c: (y + step, z, c), keep))


def swap_y(value, bits):
    return lax.ppermute(value, "tensor", t_pairs(lambda y, z, c: (y ^ bits, z, c)))


def swap_z(value):
    return lax.ppermute(value, "tensor", t_pairs(lambda y, z, c: (y, 1 - z, c)))


def swap_core(value):
    return lax.ppermute(value, "tensor", t_pairs(lambda y, z, c: (y, z, 1 - c)))


def send_x(value, step):
    return lax.ppermute(
        value, "dp", [(h * 4 + x, h * 4 + (x + step) % 4) for h in range(4) for x in range(4)]
    )


def send_h(value, step):
    return lax.ppermute(
        value, "dp", [(h * 4 + x, ((h + step) % 4) * 4 + x) for h in range(4) for x in range(4)]
    )


def swap_x(value, bits):
    return lax.ppermute(
        value, "dp", [(h * 4 + x, h * 4 + (x ^ bits)) for h in range(4) for x in range(4)]
    )


def swap_h(value, bits):
    return lax.ppermute(
        value, "dp", [(h * 4 + x, (h ^ bits) * 4 + x) for h in range(4) for x in range(4)]
    )


def total4(value, swap):
    one, two, three = swap(value, 1), swap(value, 2), swap(value, 3)
    return (value + one) + (two + three)


def tie(*values):
    return lax.optimization_barrier(values)


VMEM = pl.BlockSpec(memory_space=pltpu.VMEM)
SMEM = pl.BlockSpec(memory_space=pltpu.SMEM)
ANY = pl.BlockSpec(memory_space=pl.ANY)
NT = (((1,), (1,)), ((), ()))
TN = (((0,), (0,)), ((), ()))
D = 5120


def dot(a, b, dims=(((1,), (0,)), ((), ()))):
    return lax.dot_general(a, b, dims, preferred_element_type=F32)


def call(kernel, out, args, specs=None, scratch=(), limit=12):
    many = isinstance(out, list)
    shapes = [jax.ShapeDtypeStruct(s, t) for s, t in (out if many else [out])]
    result = pl.pallas_call(
        kernel,
        out_shape=shapes,
        in_specs=list(specs) if specs else [VMEM] * len(args),
        out_specs=[VMEM] * len(shapes),
        scratch_shapes=list(scratch),
        compiler_params=pltpu.CompilerParams(vmem_limit_bytes=limit * 2**20),
        cost_estimate=pl.CostEstimate(flops=1, bytes_accessed=1, transcendentals=0),
    )(*args)
    return result if many else result[0]


def load_rows(place, blocks, whole, sems):
    mid, mid_pair, side, side_pair, far, far_pair, last, last_pair, own = blocks
    core = place[2]

    def pick(zero, one):
        return zero + (one - zero) * core

    plan = [
        (own, 0, 0),
        (mid, pick(96, 32), 0),
        (mid_pair, pick(32, 96), 1),
        (side, pick(128, 64), 0),
        (side_pair, pick(64, 128), 1),
        (far, pick(224, 192), 0),
        (far_pair, pick(192, 224), 1),
    ]
    copies = []
    for n, (block, base, turned) in enumerate(plan):
        for half in range(2):
            at = pl.multiple_of(base + 256 * (half ^ turned), 32)
            copies.append(
                pltpu.make_async_copy(
                    block.at[pl.ds(half * 32, 32)], whole.at[pl.ds(at, 32)], sems.at[2 * n + half]
                )
            )
    for half in range(2):
        for n, (block, turned) in enumerate(((last, 0), (last_pair, 1))):
            copy = pltpu.make_async_copy(
                block.at[pl.ds(half * 32, 32)],
                whole.at[pl.ds(160 + 256 * (half ^ turned), 32)],
                sems.at[14 + half],
            )

            @pl.when(core == n)
            def _():
                copy.start()

    for copy in copies:
        copy.start()
    for copy in copies:
        copy.wait()
    for half in range(2):
        pltpu.make_async_copy(
            last.at[pl.ds(half * 32, 32)], whole.at[pl.ds(160, 32)], sems.at[14 + half]
        ).wait()


def load_plane(place, parts, w_kv, sems):
    copies = []
    for n, part in enumerate(parts):
        z, core = place[1] ^ (n // 2), place[2] ^ (n % 2)
        for kind in range(2):
            at = pl.multiple_of(kind * HD + z * 64 + core * 32, 32)
            copies.append(
                pltpu.make_async_copy(part.at[kind], w_kv.at[pl.ds(at, 32)], sems.at[2 * n + kind])
            )
    for copy in copies:
        copy.start()
    return copies


PLANE_SCRATCH = (pltpu.VMEM((256, D), BF16), pltpu.SemaphoreType.DMA((8,)))
ROWS_SCRATCH = (pltpu.VMEM((512, D), BF16), pltpu.SemaphoreType.DMA((16,)))
PLACED = [SMEM] + [ANY] * 9


def by_core(zero, one):
    pairs = []
    for y in range(4):
        for z in range(2):
            for c, move in enumerate((zero, one)):
                if move is not None:
                    a, b = move(y, z)
                    pairs.append((y * 4 + z * 2 + c, (a % 4) * 4 + b * 2 + c))
    return pairs


UP = lambda y, z: (y + 1, z)
DOWN = lambda y, z: (y - 1, z)
ACROSS = lambda y, z: (y + 2, z)
OTHER = lambda y, z: (y, 1 - z)


def gather_one(own):
    mid = lax.ppermute(own, "tensor", by_core(UP, DOWN))
    side = lax.ppermute(own, "tensor", by_core(OTHER, ACROSS))
    return mid, side


def gather_two(side):
    far = lax.ppermute(side, "tensor", by_core(UP, OTHER))
    last = lax.ppermute(side, "tensor", by_core(DOWN, None))
    return far, last


def kv_pairs(beside, back):
    pairs = []
    for y in range(4):
        for z in range(2):
            e = y // 2
            ways = [(y + 1, e), (y - 1, 1 - e)] if beside else [(y + 2, e)]
            for to, via in ways:
                here, there = y * 4 + z * 2 + via, (to % 4) * 4 + z * 2 + e
                pairs.append((there, here) if back else (here, there))
    return pairs


KV_BESIDE, KV_ACROSS = kv_pairs(True, False), kv_pairs(False, False)
DKV_BESIDE, DKV_ACROSS = kv_pairs(True, True), kv_pairs(False, True)


def swap_last(value):
    return lax.ppermute(value, "tensor", [(t, t + 1) for t in range(0, 16, 2)])


def project_kernel(place, *refs):
    blocks, planes, (w_q, q_out, kv_out, whole, sems, w_kv, w_sems) = refs[:9], refs[9:13], refs[13:]
    copies = load_plane(place, planes, w_kv, w_sems)
    load_rows(place, blocks, whole, sems)
    q_out[...] = dot(whole[...], w_q[...]).astype(BF16)
    for copy in copies:
        copy.wait()
    kv_out[...] = dot(whole[...], w_kv[...], NT).astype(BF16)


def project(place, blocks, planes, w_q):
    return call(
        project_kernel,
        [((512, 256), BF16), ((512, 256), BF16)],
        [place, *blocks, *planes, w_q],
        PLACED + [ANY] * 4 + [VMEM],
        (*ROWS_SCRATCH, *PLANE_SCRATCH),
        24,
    )


def flip_z(value):
    return jnp.concatenate([value[128:256], value[:128], value[384:], value[256:384]], axis=0)


def flip_c(value):
    return jnp.concatenate([value[256:], value[:256]], axis=0)


def turn_y(value, step):
    if step % 4 == 0:
        return value
    parts = []
    for group in range(4):
        for dy in range(4):
            at = group * 128 + ((dy + step) % 4) * 32
            parts.append(value[at : at + 32])
    return jnp.concatenate(parts, axis=0)


def pick_heads(place, slots, heads):
    own, side, across = slots
    for n in range(2):
        step = (2 * place[2] + n - place[0] + 4) % 4
        for s, slot in enumerate((own, side, across, side)):

            @pl.when(step == s)
            def _():
                value = flip_c(slot[...]) if s == 1 else slot[...]
                heads[n] = turn_y(value, -s)


def spin(value, cosine, sine):
    return value * cosine + pltpu.roll(value, 64, 1) * sine


def spin_back(grad, cosine, sine):
    return grad * cosine - pltpu.roll(grad, 64, 1) * sine


def norm(value):
    value = value.astype(F32)
    scale = lax.rsqrt(jnp.mean(value * value, axis=-1, keepdims=True) + EPS)
    return value * scale, scale


def forward_kernel(
    place, q, s0, s1, s2, cosine, sine, seg, q_gain, k_gain, out, probs, heads
):
    pick_heads(place, (s0, s1, s2), heads)
    co, si = cosine[...], sine[...]
    seg_q, row_q = seg[:, 0:1], seg[:, 1:2]
    turned = seg[...].T
    keep = (seg_q == turned[0:1]) & (row_q >= turned[1:2])
    for n in range(2):
        q_unit, _ = norm(q[:, n * HD : n * HD + HD])
        k_unit, _ = norm(heads[n, :, :HD])
        q_rot = spin(q_unit * q_gain[...], co, si).astype(BF16)
        k_rot = spin(k_unit * k_gain[...], co, si).astype(BF16)
        scores = jnp.where(keep, dot(q_rot, k_rot, NT) * HD**-0.5, -1e30)
        weights = jnp.exp(scores - jnp.max(scores, axis=-1, keepdims=True))
        soft = weights / jnp.sum(weights, axis=-1, keepdims=True)
        probs[n] = soft
        value = dot(soft.astype(BF16), heads[n, :, HD:]).astype(BF16)
        out[:, n * HD : n * HD + HD] = value


SUMS = (
    ((1, 1), (3, 1), (0, 1), (3, 0)),
    ((2, 1), (2, 0), (1, 0)),
)


def rows_of(core, turned):
    slices = []
    for dy, dz in SUMS[core]:
        for dc in range(2):
            slices.append(slice((dc ^ turned) * 256 + dz * 128 + dy * 32, (dc ^ turned) * 256 + dz * 128 + dy * 32 + 32))
    slices += [slice(turned * 256, turned * 256 + 32)] * (9 - len(slices))
    return slices


def backward_kernel(place, *refs):
    blocks = refs[:9]
    w_out, q, s0, s1, s2, cosine, sine, advantage, q_gain, k_gain, probs, attended = refs[9:21]
    dq, keep, send, d0, d1, d2, gains, heads, whole, sems = refs[21:]
    pick_heads(place, (s0, s1, s2), heads)
    load_rows(place, blocks, whole, sems)
    grad_out = (dot(whole[...], w_out[...], NT) * advantage[:, 0:1]).astype(BF16)
    co, si = cosine[...], sine[...]
    q_sum = jnp.zeros((1, HD), F32)
    k_sum = jnp.zeros((1, HD), F32)
    d0[...] = jnp.zeros_like(d0)
    for n in range(2):
        cols = slice(n * HD, n * HD + HD)
        q_unit, q_scale = norm(q[:, cols])
        k_unit, k_scale = norm(heads[n, :, :HD])
        q_rot = spin(q_unit * q_gain[...], co, si).astype(BF16)
        k_rot = spin(k_unit * k_gain[...], co, si).astype(BF16)
        grad = grad_out[:, cols]
        delta = jnp.sum(
            grad.astype(F32) * attended[:, cols].astype(F32), axis=-1, keepdims=True
        )
        soft = probs[n]
        score = (soft * (dot(grad, heads[n, :, HD:], NT) - delta) * HD**-0.5).astype(BF16)
        e_q = spin_back(dot(score, k_rot), co, si)
        e_k = spin_back(dot(q_rot.T, score).T, co, si)
        grad_v = dot(grad.T, soft.astype(BF16)).T.astype(BF16)
        q_sum += jnp.sum(e_q * q_unit, axis=0, keepdims=True)
        k_sum += jnp.sum(e_k * k_unit, axis=0, keepdims=True)
        e_q = e_q * q_gain[...]
        e_k = e_k * k_gain[...]
        grad_q = q_scale * (e_q - q_unit * jnp.mean(e_q * q_unit, axis=-1, keepdims=True))
        grad_k = k_scale * (e_k - k_unit * jnp.mean(e_k * k_unit, axis=-1, keepdims=True))
        dq[:, cols] = grad_q.astype(BF16)
        both = jnp.concatenate([grad_k.astype(BF16), grad_v], axis=1)
        step = (2 * place[2] + n - place[0] + 4) % 4
        for s, slot in enumerate((d0, d1, d2, d1)):

            @pl.when(step == s)
            def _():
                slot[...] = both

    gains[...] = jnp.concatenate([q_sum, k_sum], axis=0)
    for core in range(2):

        @pl.when(place[2] == core)
        def _():
            keep[...] = jnp.concatenate([dq[at] for at in rows_of(core, 0)], axis=0)
            send[...] = jnp.concatenate([dq[at] for at in rows_of(1 - core, 1)], axis=0)


def plane_kernel(place, own, side, across, out):
    total = own[...].astype(F32) + turn_y(across[...], 2).astype(F32)
    home = place[0] // 2 == place[2]

    @pl.when(home)
    def _():
        out[...] = (total + turn_y(side[...], 3).astype(F32)).astype(BF16)

    @pl.when(jnp.logical_not(home))
    def _():
        out[...] = (total + turn_y(flip_c(side[...]), 1).astype(F32)).astype(BF16)


def pair_kernel(a, b, out):
    out[...] = (a[...].astype(F32) + flip_z(b[...]).astype(F32)).astype(BF16)


def columns_kernel(place, a, b, dq, right, rows_here):
    full = (a[...].astype(F32) + flip_c(b[...]).astype(F32)).astype(BF16)
    for core in range(2):

        @pl.when(place[2] == core)
        def _():
            some = [full[at] for at in rows_of(core, 0)]
            some = some[4:9] if core == 0 else some[2:7]
            rows_here[...] = jnp.concatenate(some, axis=0)

    right[:, :256] = dq[...]
    spot = place[1] * 2 + place[2]
    for n in range(4):

        @pl.when(spot == n)
        def _():
            right[:, 256:] = jnp.concatenate(
                [full[:, n * 32 : n * 32 + 32], full[:, HD + n * 32 : HD + n * 32 + 32]], axis=1
            )


def weight_kernel(place, *refs):
    if len(refs) == 17:
        blocks, (right, o0, o1, o2a, o2b, o3, whole, sems) = refs[:9], refs[9:]
    else:
        blocks, (right, w_q, w_kv, gain, o0, o1, o2a, o2b, o3, sums, whole, sems) = refs[:9], refs[9:]
    turned = right[...].T
    one = lax.broadcasted_iota(jnp.int32, (256, 256), 0)
    eye = jnp.where(one == lax.broadcasted_iota(jnp.int32, (256, 256), 1), 1.0, 0.0).astype(BF16)
    load_rows(place, blocks, whole, sems)
    for h in range(4):
        at = slice(h * 1280, h * 1280 + 1280)
        exact = dot(turned, whole[:, at])
        side = exact.astype(BF16)
        part = [dot(eye, side[:, i * 256 : i * 256 + 256], NT).astype(BF16) for i in range(5)]
        part = jnp.concatenate(part, axis=0)
        if len(refs) != 17:
            product = (part[:, :256].astype(F32) * w_q[at].astype(F32)).astype(BF16)
            total = dot(jnp.ones((8, 256), BF16), product, NT)[0:1]
            total += jnp.sum(exact[256:288] * w_kv[0, :, at].astype(F32), axis=0, keepdims=True)
            total += jnp.sum(exact[288:320] * w_kv[1, :, at].astype(F32), axis=0, keepdims=True)
            sums[:, at] = total / gain[:, at]
        k = (h - place[3] + 4) % 4
        for x in range(4):
            s = (x - place[4] + 4) % 4
            tile = part[x * 320 : x * 320 + 320]
            if right.shape[1] == 256:
                tile = jnp.concatenate([tile[:, :HD], tile[:, HD:]], axis=0)
            else:
                tile = jnp.concatenate(
                    [
                        tile[:, :HD],
                        tile[:, HD : 2 * HD],
                        jnp.concatenate([tile[:160, 2 * HD :], tile[160:, 2 * HD :]], axis=1),
                    ],
                    axis=0,
                )
            for at, out in ((0, o0), (1, o1), (3, o3)):

                @pl.when(s == at)
                def _():
                    out[k] = tile

            @pl.when((s == 2) & (k < 2))
            def _():
                o2a[jnp.minimum(k, 1)] = tile

            @pl.when((s == 2) & (k >= 2))
            def _():
                o2b[jnp.maximum(k - 2, 0)] = tile


def weight_grad(blocks, place, right, *more):
    rows = right.shape[1] * 320 // HD
    four, two = ((4, rows, HD), BF16), ((2, rows, HD), BF16)
    return call(
        weight_kernel,
        [four, four, two, two, four] + ([((1, D), F32)] if more else []),
        [place, *blocks, right, *more],
        PLACED + [VMEM] * (1 + len(more)),
        ROWS_SCRATCH,
        32,
    )


def around_kernel(o1, o3, a, b, right, left):
    right[0:2] = (o1[0:2].astype(F32) + a[...].astype(F32)).astype(BF16)
    right[2:4] = o1[2:4]
    left[0:2] = o3[0:2]
    left[2:4] = (o3[2:4].astype(F32) + b[...].astype(F32)).astype(BF16)


def meet_kernel(o0, r, s, gains, p0, p1, p2, p3, own):
    value = gains[...]
    high = value.astype(BF16)
    low = (value - high.astype(F32)).astype(BF16)
    own[...] = high.astype(F32) + low.astype(F32)
    for k, out in enumerate((p0, p1, p2, p3)):
        out[0:800] = (o0[k].astype(F32) + r[k].astype(F32) + s[k].astype(F32)).astype(BF16)
        out[800:848] = high
        out[848:896] = low


def reduce_first(parts):
    o0, o1, o2a, o2b, o3 = parts
    return o0, o1, o3, send_x(o2a, 1), send_x(o2b, -1)


def reduce_around(state):
    o0, o1, o3, a, b = state
    right, left = call(around_kernel, [(o1.shape, BF16)] * 2, [o1, o3, a, b])
    return o0, right, left


def reduce_second(state):
    o0, right, left = state
    return o0, send_x(right, 1), send_x(left, -1)


def halve_kernel(place, o0, r, s, here, near, far):
    def total(k):
        return (o0[k].astype(F32) + r[k].astype(F32) + s[k].astype(F32)).astype(BF16)

    here[...] = total(0)
    far[0:640] = total(2)
    for odd in range(2):

        @pl.when(place[3] % 2 == odd)
        def _():
            near[...] = total(3 if odd else 1)
            far[640:1280] = total(1 if odd else 3)


def reduce_third(state):
    p0, p1, p2, p3 = state
    return p0, send_h(p1, 1), send_h(p2, 2), send_h(p3, -1)


def reduce_last(state):
    zero, one, two, three = [part.astype(F32) for part in state]
    return (zero + two) + (one + three)


def first_kernel(mine, pair, one, two, m, p, s_m, s_p):
    copies = [
        pltpu.make_async_copy(mine.at[pl.ds(0, 128)], m, s_m),
        pltpu.make_async_copy(pair.at[pl.ds(0, 128)], p, s_p),
    ]
    for copy in copies:
        copy.start()
    for copy in copies:
        copy.wait()
    one[...] = (m[0:64].astype(F32) + p[0:64].astype(F32)).astype(BF16)
    two[...] = (m[64:128].astype(F32) + p[64:128].astype(F32)).astype(BF16)


def second_kernel(place, *refs):
    planes, (mine, pair, one, two, here, three, four, own, w_kv, sems, m, p, s_m, s_p) = refs[:4], refs[4:]
    copies = load_plane(place, planes, w_kv, sems)
    at = pl.ds(pl.multiple_of(128 - 64 * place[2], 32), 160)
    sides = [
        pltpu.make_async_copy(mine.at[at], m, s_m),
        pltpu.make_async_copy(pair.at[at], p, s_p),
    ]
    for copy in sides:
        copy.start()
    for copy in copies + sides:
        copy.wait()
    term = dot(here[...], w_kv[...])

    def both(at, size=64):
        return m[at : at + size].astype(F32) + p[at : at + size].astype(F32)

    own[...] = both(128, 32) + term[128:160]
    four[...] = (both(64) + term[64:128]).astype(BF16)

    @pl.when(place[2] == 0)
    def _():
        three[...] = (both(0) + one[...].astype(F32) + two[...].astype(F32)).astype(BF16)

    @pl.when(place[2] == 1)
    def _():
        three[...] = (both(0) + one[...].astype(F32) + term[0:64]).astype(BF16)


def third_kernel(three, four, out):
    out[...] = (three[32:64].astype(F32) + four[32:64].astype(F32)).astype(BF16)


def last_kernel(own, three, four, pair, x, gain, grad, advantage, out):
    total = own[...] + three[0:32].astype(F32) + four[0:32].astype(F32) + pair[...].astype(F32)
    value = x[...].astype(F32)
    scale = lax.rsqrt(jnp.mean(value * value, axis=-1, keepdims=True) + EPS)
    unit = value * scale
    weighted = total * gain[...]
    inner = weighted - unit * jnp.mean(weighted * unit, axis=-1, keepdims=True)
    scaled = (grad[...].astype(F32) * advantage[0:32, 0:1]).astype(BF16)
    out[...] = (scale * inner + scaled.astype(F32)).astype(BF16)


def normed_kernel(x, pair, gain, out):
    for n, ref in enumerate((x, pair)):
        unit, _ = norm(ref[...])
        out[n * 32 : n * 32 + 32] = (unit * gain[...]).astype(BF16)


def stack_kernel(x, pair, out):
    out[0:32] = x[...]
    out[32:64] = pair[...]


def tables_kernel(place, lengths, rewards, groups, inverse, sums, angle, marks):
    lane = lax.broadcasted_iota(jnp.int32, (1, HD), 1)
    count = jnp.zeros((1, HD), F32)
    first, second = count, count
    for n in range(8):
        hit = jnp.where(lane == groups[n], 1.0, 0.0)
        count += hit
        first += hit * rewards[n]
        second += hit * (rewards[n] * rewards[n])
    sums[...] = jnp.concatenate([count, first, second, jnp.zeros((5, HD), F32)], axis=0)
    j = lax.broadcasted_iota(jnp.int32, (512, HD), 0)
    spot = (((place[0] + ((j >> 5) & 3)) & 3) << 2) + ((place[1] ^ ((j >> 7) & 1)) << 1)
    rows = ((spot + (place[2] ^ (j >> 8))) << 5) + (j & 31)
    end = lengths[0, 0]
    segment, start = jnp.zeros_like(rows), jnp.zeros_like(rows)
    for n in range(1, 8):
        segment = jnp.where(rows >= end, n, segment)
        start = jnp.where(rows >= end, end, start)
        end = end + lengths[0, n]
    angle[...] = (rows - start).astype(F32) * inverse[...]
    lane = lax.broadcasted_iota(jnp.int32, (512, HD), 1)
    marks[...] = jnp.where(lane == 0, segment, rows).astype(F32)


def advantage_kernel(rewards, groups, total, marks, out):
    safe = jnp.maximum(total[0:1], 1.0)
    mean = total[1:2] / safe
    variance = total[2:3] / safe - mean * mean
    lane = lax.broadcasted_iota(jnp.int32, (1, HD), 1)
    segment = marks[:, 0:1]
    value = jnp.zeros((512, 1), F32)
    for n in range(8):
        hit = lane == groups[n]
        middle = jnp.sum(jnp.where(hit, mean, 0.0), axis=1, keepdims=True)
        spread = jnp.sum(jnp.where(hit, variance, 0.0), axis=1, keepdims=True)
        one = (rewards[n] - middle) / jnp.sqrt(spread + 1.0)
        value = jnp.where(segment == float(n), one, value)
    out[...] = jnp.broadcast_to(value, (512, HD))


def scale_kernel(a, advantage, out):
    out[...] = (a[...].astype(F32) * advantage[:, 0:1]).astype(BF16)


def on_device(
    inputs,
    upstream,
    w_query,
    w_key,
    w_value,
    w_output,
    norm_gain,
    query_gain,
    key_gain,
    lengths,
    rewards,
    groups,
):
    t_at = lax.axis_index("tensor")
    d_at = lax.axis_index("dp")
    y_at, z_at, c_at = t_at // 4, (t_at // 2) % 2, t_at % 2
    place = jnp.stack([y_at, z_at, c_at, d_at // 4, d_at % 4]).astype(jnp.int32)
    gain_row = norm_gain.reshape(1, D)

    inverse = ROPE_BASE ** (-(jnp.arange(HD // 2, dtype=F32) * 2.0 / HD))
    inverse = jnp.concatenate([inverse, inverse]).reshape(1, HD)
    sums, angle, marks = call(
        tables_kernel,
        [((8, HD), F32), ((512, HD), F32), ((512, HD), F32)],
        [place, lengths, rewards, groups, inverse],
        [SMEM] * 4 + [VMEM],
    )
    inputs_pair, upstream_pair, angle, sums, w_key, w_value = tie(
        swap_core(inputs), swap_core(upstream), angle, sums, w_key, w_value
    )
    x_own = call(normed_kernel, ((64, D), BF16), [inputs, inputs_pair, gain_row])

    x_own, w_key, w_value, upstream_pair, angle, sums = tie(
        x_own, w_key, w_value, upstream_pair, angle, sums
    )
    x_mid, x_side = gather_one(x_own)
    w_own = jnp.stack([w_key.T, w_value.T])
    w_pair, w_far = swap_core(w_own), swap_z(w_own)
    g_own = call(stack_kernel, ((64, D), BF16), [upstream, upstream_pair])
    cosine, sine = jnp.cos(angle), jnp.sin(angle)
    sine = jnp.where(jnp.arange(HD)[None, :] < HD // 2, -sine, sine)
    sums = sums + swap_x(sums, 1)
    sums = sums + swap_x(sums, 2)
    x_mid, x_side, w_pair, w_far, g_own, cosine, sine, sums = tie(
        x_mid, x_side, w_pair, w_far, g_own, cosine, sine, sums
    )
    x_far, x_last = gather_two(x_side)
    x_mid_pair, x_side_pair = swap_core(x_mid), swap_core(x_side)
    sums = sums + swap_h(sums, 1)
    x_far, x_last, x_mid_pair, x_side_pair, g_own, sums = tie(
        x_far, x_last, x_mid_pair, x_side_pair, g_own, sums
    )
    g_mid, g_side = gather_one(g_own)
    planes = [w_own, w_pair, w_far, swap_core(w_far)]
    x_blocks = [
        x_mid, x_mid_pair, x_side, x_side_pair, x_far, swap_core(x_far), x_last, swap_last(x_last), x_own
    ]
    query_proj, kv = project(place, x_blocks, planes, w_query)
    query_proj, kv, g_mid, g_side, sums = tie(query_proj, kv, g_mid, g_side, sums)

    g_far, g_last = gather_two(g_side)
    slots = [kv, lax.ppermute(kv, "tensor", KV_BESIDE), lax.ppermute(kv, "tensor", KV_ACROSS)]
    sums = sums + swap_h(sums, 2)
    *slots, g_mid, g_side, sums = tie(*slots, g_mid, g_side, sums)
    advantage = call(
        advantage_kernel,
        ((512, HD), F32),
        [rewards, groups, sums, marks],
        [SMEM, SMEM, VMEM, VMEM],
    )
    g_mid_pair, g_side_pair = swap_core(g_mid), swap_core(g_side)
    q_row, k_row = query_gain.reshape(1, HD), key_gain.reshape(1, HD)
    attended, probs = call(
        forward_kernel,
        [((512, 256), BF16), ((2, 512, 512), F32)],
        [place, query_proj, *slots, cosine, sine, marks, q_row, k_row],
        [SMEM] + [VMEM] * 9,
        (pltpu.VMEM((2, 512, 256), BF16),),
        20,
    )
    scaled = call(scale_kernel, ((512, 256), BF16), [attended, advantage])
    g_far, g_last, g_mid_pair, g_side_pair, attended, scaled, probs, advantage = tie(
        g_far, g_last, g_mid_pair, g_side_pair, attended, scaled, probs, advantage
    )
    g_blocks = [
        g_mid, g_mid_pair, g_side, g_side_pair, g_far, swap_core(g_far), g_last, swap_last(g_last), g_own
    ]
    parts = weight_grad(g_blocks, place, scaled)
    *parts, probs = tie(*parts, probs)
    out_state = reduce_first(parts)
    dq, keep, send, d0, d1, d2, head_gains = call(
        backward_kernel,
        [((512, 256), BF16), ((288, 256), BF16), ((288, 256), BF16)]
        + [((512, 256), BF16)] * 3
        + [((2, HD), F32)],
        [place, *g_blocks, w_output, query_proj, *slots, cosine, sine, advantage, q_row, k_row, probs, attended],
        PLACED + [VMEM] * 12,
        (pltpu.VMEM((2, 512, 256), BF16), *ROWS_SCRATCH),
        32,
    )
    dq, keep, send, d0, d1, d2, *out_state = tie(dq, keep, send, d0, d1, d2, *out_state)
    d1, d2 = lax.ppermute(d1, "tensor", DKV_BESIDE), lax.ppermute(d2, "tensor", DKV_ACROSS)
    out_state = reduce_second(reduce_around(out_state))

    back = lambda rows: dot(rows, w_query, NT).astype(BF16)
    other, mine = back(send), back(keep)
    other, mine, d0, d1, d2 = tie(other, mine, d0, d1, d2)
    pair = swap_core(other)
    dkv = call(plane_kernel, ((512, 256), BF16), [place, d0, d1, d2], [SMEM] + [VMEM] * 3)
    dkv_pair = swap_z(dkv)
    one, two = call(
        first_kernel,
        [((64, D), BF16)] * 2,
        [mine, pair],
        [ANY] * 2,
        (pltpu.VMEM((128, D), BF16),) * 2 + (pltpu.SemaphoreType.DMA(()),) * 2,
    )
    dkv, dkv_pair, one, two = tie(dkv, dkv_pair, one, two)
    dkv = call(pair_kernel, ((512, 256), BF16), [dkv, dkv_pair])
    dkv_pair = swap_core(dkv)
    dkv, dkv_pair = tie(dkv, dkv_pair)
    combined, rows_here = call(
        columns_kernel,
        [((512, 320), BF16), ((160, 256), BF16)],
        [place, dkv, dkv_pair, dq],
        [SMEM] + [VMEM] * 3,
    )
    *parts, norm_sums = weight_grad(x_blocks, place, combined, w_query, w_own, gain_row)
    *parts, norm_sums, one, two, o0, o1, o2 = tie(*parts, norm_sums, one, two, *out_state)
    out_state = o0, o1, o2
    out_here, out_near, out_far = call(
        halve_kernel,
        [((640, HD), BF16), ((640, HD), BF16), ((1280, HD), BF16)],
        [place, *out_state],
        [SMEM] + [VMEM] * 3,
    )
    out_far = swap_h(out_far, 2)
    state = reduce_first(parts)
    gains = jnp.concatenate([norm_sums.reshape(40, HD), head_gains, jnp.zeros((6, HD), F32)])
    gains = gains + swap_core(gains)
    one, two, gains = tie(one, two, gains)
    one = lax.ppermute(one, "tensor", by_core(UP, OTHER))
    two = lax.ppermute(two, "tensor", by_core(DOWN, None))
    gains = gains + swap_z(gains)
    *state, one, two, gains = tie(*state, one, two, gains)

    state = reduce_second(reduce_around(state))
    three, four, own = call(
        second_kernel,
        [((64, D), BF16), ((64, D), BF16), ((32, D), F32)],
        [place, *planes, mine, pair, one, two, rows_here],
        [SMEM] + [ANY] * 6 + [VMEM] * 3,
        (
            *PLANE_SCRATCH,
            pltpu.VMEM((160, D), BF16),
            pltpu.VMEM((160, D), BF16),
            pltpu.SemaphoreType.DMA(()),
            pltpu.SemaphoreType.DMA(()),
        ),
        28,
    )
    three = lax.ppermute(three, "tensor", by_core(OTHER, ACROSS))
    four = lax.ppermute(four, "tensor", by_core(DOWN, UP))
    out_near = (out_near.astype(F32) + out_far[640:].astype(F32)).astype(BF16)
    out_near = swap_h(out_near, 1)
    three, four, gains = tie(three, four, gains)
    pair = swap_core(call(third_kernel, ((32, D), BF16), [three, four]))
    input_grad = call(
        last_kernel,
        ((32, D), BF16),
        [own, three, four, pair, inputs, gain_row, upstream, advantage],
    )
    gains = total4(total4(gains, swap_y), swap_x)
    *state, gains, input_grad, out_near = tie(*state, gains, input_grad, out_near)
    *state, gains = call(
        meet_kernel,
        [((896, HD), BF16)] * 4 + [((48, HD), F32)],
        [*state, gains],
    )
    state = reduce_third(state)
    gains = [gains] + [part[800:848].astype(F32) + part[848:].astype(F32) for part in state[1:]]
    gains = ((gains[0] + gains[2]) + (gains[1] + gains[3])).reshape(-1)
    state = [part[:800] for part in state]
    out_grads = out_here.astype(F32) + out_far[:640].astype(F32) + out_near.astype(F32)
    grads = reduce_last(state)
    last = grads[640:]
    return (
        input_grad,
        jnp.concatenate([grads[:320], grads[320:640]], axis=1),
        jnp.concatenate([last[:, :32], last[:, 64:96]], axis=0),
        jnp.concatenate([last[:, 32:64], last[:, 96:]], axis=0),
        jnp.concatenate([out_grads[:320], out_grads[320:]], axis=1),
        gains[:D],
        gains[D : D + HD],
        gains[D + HD : D + 2 * HD],
    )


def solution(mesh):
    in_specs = (
        P(("dp", "tensor"), None),
        P(("dp", "tensor"), None),
        P(None, "tensor"),
        P(None, "tensor"),
        P(None, "tensor"),
        P("tensor", None),
        P(),
        P(),
        P(),
        P("dp", None),
        P("dp"),
        P("dp"),
    )
    out_specs = (
        P(("dp", "tensor"), None),
        P("dp", "tensor"),
        P("dp", "tensor"),
        P("dp", "tensor"),
        P("dp", "tensor"),
        P(),
        P(),
        P(),
    )
    return jax.shard_map(
        on_device, mesh=mesh, in_specs=in_specs, out_specs=out_specs, check_vma=False
    )
```
